32 devices in a mesh: dp: 32 (over z, y, x, core).
Axes of the slice: x: 2, y: 2, z: 4, core: 2. Of those that a mesh axis runs over, the one named last changes fastest.
Arguments:
- images: bfloat16 [256, 197, 512], P('dp'), may hold values from -6 to 6
- image_count: int32 [32], P('dp'), may hold values from 1 to 8, as said below
- expert_index: int32 [256, 197, 2], P('dp'), may hold values from 0 to 7, as said below
- expert_slot: int32 [256, 197, 2], P('dp'), may hold values from 0 to 127, as said below
- keep: int32 [256, 197, 2], P('dp'), may hold values from 0 to 1, as said below
- cotangent: bfloat16 [256, 197, 512], P('dp'), may hold values from -6 to 6
- ln1_gain: bfloat16 [512], P('dp'), may hold values from 0.5 to 1.5
- ln1_bias: bfloat16 [512], P('dp'), may hold values from -1.1953125 to 1.1953125
- qkv_weight: bfloat16 [512, 1536], P('dp'), may hold values from -0.375 to 0.375
- qv_bias: bfloat16 [2, 512], P(None, 'dp'), may hold values from -1.796875 to 1.796875
- out_weight: bfloat16 [512, 512], P('dp'), may hold values from -0.75 to 0.75
- out_bias: bfloat16 [512], P('dp'), may hold values from -0.59765625 to 0.59765625
- ln2_gain: bfloat16 [512], P('dp'), may hold values from 0.5 to 1.5
- ln2_bias: bfloat16 [512], P('dp'), may hold values from -0.59765625 to 0.59765625
- router_weight: bfloat16 [512, 8], P('dp'), may hold values from -0.1875 to 0.1875
- expert_in: bfloat16 [8, 512, 2048], P(None, 'dp'), may hold values from -0.25 to 0.25
- expert_in_bias: bfloat16 [8, 2048], P(None, 'dp'), may hold values from -1.1953125 to 1.1953125
- expert_out: bfloat16 [8, 2048, 512], P(None, 'dp'), may hold values from -0.75 to 0.75
- expert_out_bias: bfloat16 [8, 512], P(None, 'dp'), may hold values from -2.3 to 2.3
Outputs:
- block_out: bfloat16 [256, 197, 512], P('dp')
- image_grad: bfloat16 [256, 197, 512], P('dp')
- balance: float32 [], replicated
- ln1_gain_grad: float32 [512], P('dp')
- ln1_bias_grad: float32 [512], P('dp')
- qkv_weight_grad: float32 [512, 1536], P('dp')
- qv_bias_grad: float32 [2, 512], P(None, 'dp')
- out_weight_grad: float32 [512, 512], P('dp')
- out_bias_grad: float32 [512], P('dp')
- ln2_gain_grad: float32 [512], P('dp')
- ln2_bias_grad: float32 [512], P('dp')
- router_weight_grad: float32 [512, 8], P('dp')
- expert_in_grad: float32 [8, 512, 2048], P(None, 'dp')
- expert_in_bias_grad: float32 [8, 2048], P(None, 'dp')
- expert_out_grad: float32 [8, 2048, 512], P(None, 'dp')
- expert_out_bias_grad: float32 [8, 512], P(None, 'dp')
The draws below stay inside these ranges and needn't reach their ends.
Inputs may be any that keep to these rules, and one draw needn't show every extreme that they name: Device d's live images fill its first image_count[d] slots; some device has all 8 slots live. `expert_index`: the two experts of a token differ. `expert_slot`: within one micro-batch of one device, the dispatched choices of one expert have distinct positions; choices that are not dispatched hold 0. In some micro-batch some expert uses all 128 positions. `keep`: choices of tokens in padding slots are never dispatched.
All inputs are finite; a program needn't handle non-finite values.
Results may differ from the reference program's by a relative error of at most 0.014.
Values may be sent and summed in bfloat16 or wider, within the bound.
No kernel may reach another device: no remote copies, remote signals or barrier semaphores. Data moves between devices by JAX's collectives and lax.ppermute only.
A program may use at most 384 MiB of HBM per device.

```python
import jax
import jax.numpy as jnp
from jax import lax

D = 512
HEADS = 8
HEAD_DIM = 64
FF = 2048
EXPERTS = 8
TOP = 2
LEN = 197
SLOTS = 8
MICRO = 4
MB_IMG = 2
CAP = 128
IMAGES = 256
N_DP = 32


def routing_tables(key):
    base_key = jax.random.fold_in(key, 7)
    key_count = jax.random.fold_in(base_key, 1)
    key_full = jax.random.fold_in(base_key, 2)
    key_popular = jax.random.fold_in(base_key, 3)
    key_first = jax.random.fold_in(base_key, 4)
    key_second = jax.random.fold_in(base_key, 5)
    device_ids = jnp.arange(N_DP)
    rising = (SLOTS * (device_ids + 1) + N_DP - 1) // N_DP // 2
    extra = jax.random.randint(key_count, (N_DP,), 0, SLOTS // 2 + 1)
    counts = jnp.clip(rising + extra, 1, SLOTS)
    full_device = jax.random.randint(key_full, (), 0, N_DP)
    counts = jnp.where(device_ids == full_device, SLOTS, counts).astype(jnp.int32)
    popular_base = jax.random.randint(key_popular, (), 0, EXPERTS)
    popular_dev = (popular_base + device_ids) % EXPERTS
    popular_tok = jnp.repeat(popular_dev, SLOTS)[:, None]
    first = jax.random.randint(key_first, (IMAGES, LEN), 0, EXPERTS + 8)
    first = jnp.where(first >= EXPERTS, popular_tok, first)
    offset = jax.random.randint(key_second, (IMAGES, LEN), 1, EXPERTS)
    second = (first + offset) % EXPERTS
    chosen = jnp.stack([first, second], -1).astype(jnp.int32)
    tok_block = SLOTS // MICRO * LEN
    live_slots = jnp.arange(SLOTS)[None, :] < counts[:, None]
    live_tok = jnp.repeat(live_slots, LEN, axis=1).reshape(N_DP, MICRO, tok_block)
    grouped = chosen.reshape(N_DP, MICRO, tok_block, 2)
    order = jnp.concatenate([grouped[..., 0], grouped[..., 1]], axis=2)
    live_pairs = jnp.concatenate([live_tok, live_tok], axis=2)
    hot_table = ((order[..., None] == jnp.arange(EXPERTS)) & live_pairs[..., None]).astype(jnp.int32)
    before = jnp.cumsum(hot_table, axis=2) - hot_table
    ranks = jnp.sum(before * hot_table, axis=-1)
    kept_pairs = live_pairs & (ranks < CAP)
    positions = jnp.where(kept_pairs, ranks, 0).astype(jnp.int32)
    positions = positions.reshape(N_DP, MICRO, 2, tok_block).transpose(0, 1, 3, 2).reshape(IMAGES, LEN, 2)
    kept_out = kept_pairs.astype(jnp.int32).reshape(N_DP, MICRO, 2, tok_block).transpose(0, 1, 3, 2).reshape(IMAGES, LEN, 2)
    return (counts, chosen, positions, kept_out)


def draw_image_count(key, part):
    return routing_tables(key)[0]


def draw_expert_index(key, part):
    return routing_tables(key)[1]


def draw_expert_slot(key, part):
    return routing_tables(key)[2]


def draw_keep(key, part):
    return routing_tables(key)[3]


def draw_expert_out_bias(key, part):
    key_cols = jax.random.fold_in(key, 12)
    values = 0.5 * jax.random.normal(key_cols, (EXPERTS, D), jnp.float32)
    values = jnp.clip(values, -2.3, 2.3)
    return values.astype(jnp.bfloat16)


def level_of(own_key, extent, cuts, least, largest):
    factor_of = 1.0
    for dim, shards_of in cuts:
        draws = jax.random.uniform(jax.random.fold_in(jax.random.fold_in(own_key, 6), dim), (shards_of,), jnp.float32, least / len(cuts), largest / len(cuts))
        factor_of = factor_of * jnp.repeat(jnp.exp(draws), extent[dim] // shards_of).reshape((-1,) + (1,) * (len(extent) - 1 - dim))
    return factor_of


def scatter_about(own_key, extent, scale, most, pieces=(), held_as=jnp.bfloat16):
    values = scale * jax.random.normal(own_key, extent, jnp.float32)
    if pieces:
        values = values * level_of(own_key, extent, pieces, -0.22, 0.18)
    return jnp.clip(values, -most, most).astype(held_as)


def setup_inputs(seed: int = 0) -> dict:
    splits = jax.random.split(jax.random.key(seed), 20)
    return {
        "images": scatter_about(splits[0], (IMAGES, LEN, D), 1.0, 6.0, ((0, 32),)),
        "image_count": draw_image_count(jax.random.fold_in(splits[19], 71), 0),
        "expert_index": draw_expert_index(jax.random.fold_in(splits[19], 71), 0),
        "expert_slot": draw_expert_slot(jax.random.fold_in(splits[19], 71), 0),
        "keep": draw_keep(jax.random.fold_in(splits[19], 71), 0),
        "cotangent": scatter_about(splits[5], (IMAGES, LEN, D), 1.0, 6.0, ((0, 32),)),
        "ln1_gain": jnp.clip(1.0 + 0.1 * jax.random.normal(splits[6], (D,), jnp.float32), 0.5, 1.5).astype(jnp.bfloat16),
        "ln1_bias": scatter_about(splits[7], (D,), 0.2, 1.1953125, ((0, 32),)),
        "qkv_weight": scatter_about(splits[8], (D, 3 * D), (D // 2) ** -0.5, 0.375, ((0, 32),)),
        "qv_bias": scatter_about(splits[9], (2, D), 0.3, 1.796875, ((1, 32),)),
        "out_weight": scatter_about(splits[10], (D, D), (D // 8) ** -0.5, 0.75, ((0, 32),)),
        "out_bias": scatter_about(splits[11], (D,), 0.1, 0.59765625, ((0, 32),)),
        "ln2_gain": jnp.clip(1.0 + 0.1 * jax.random.normal(splits[12], (D,), jnp.float32), 0.5, 1.5).astype(jnp.bfloat16),
        "ln2_bias": scatter_about(splits[13], (D,), 0.1, 0.59765625, ((0, 32),)),
        "router_weight": scatter_about(splits[14], (D, EXPERTS), (2 * D) ** -0.5, 0.1875, ((0, 32),)),
        "expert_in": scatter_about(splits[15], (EXPERTS, D, FF), D ** -0.5, 0.25, ((1, 32),)),
        "expert_in_bias": scatter_about(splits[16], (EXPERTS, FF), 0.2, 1.1953125, ((1, 32),)),
        "expert_out": scatter_about(splits[17], (EXPERTS, FF, D), (FF // 32) ** -0.5, 0.75, ((1, 32),)),
        "expert_out_bias": draw_expert_out_bias(jax.random.fold_in(splits[19], 71), 0),
    }


@jax.custom_vjp
def low(v):
    return lax.optimization_barrier(v.astype(jnp.bfloat16)).astype(jnp.float32)

@jax.custom_vjp
def low_back(v):
    return v

def low_keep(v):
    return (low(v), None)

def low_pass(kept, grad):
    return (grad,)

def back_keep(v):
    return (v, None)

def back_low(kept, grad):
    return (low(grad),)
low.defvjp(low_keep, low_pass)
low_back.defvjp(back_keep, back_low)
HIGH = lax.Precision.HIGHEST
EPSILON = 1e-06
BALANCE_WEIGHT = 8.0

def both_round(value):
    return low_back(low(value))

def layer_norm(values, gain_vec, shift_vec):
    average = lax.optimization_barrier(jnp.mean(values, -1, keepdims=True))
    centered = values - average
    spread = lax.optimization_barrier(jnp.mean(centered * centered, -1, keepdims=True))
    return centered * lax.rsqrt(spread + EPSILON) * gain_vec + shift_vec

def block_forward(params, tokens_in, routes, slot_pos, kept_flag, live_img):
    gain_one, shift_one, qkv_mat, qv_vec, out_mat, out_vec, gain_two, shift_two, router_mat, inner_mat, inner_vec, outer_mat, outer_vec = params
    row_count = MB_IMG * LEN
    scale_val = HEAD_DIM ** (-0.5)
    flat_tok = tokens_in.reshape(row_count, D)
    normed = low(layer_norm(flat_tok, gain_one, shift_one))
    bias_full = jnp.concatenate([qv_vec[0], jnp.zeros((D,), jnp.float32), qv_vec[1]])
    projected = both_round(jnp.dot(normed, qkv_mat, precision=HIGH) + bias_full)
    head_shape = (MB_IMG, LEN, HEADS, HEAD_DIM)
    query_part = projected[:, :D].reshape(head_shape)
    key_part = projected[:, D:2 * D].reshape(head_shape)
    value_part = projected[:, 2 * D:].reshape(head_shape)
    scores = low_back(jnp.einsum('bqhd,bkhd->bhqk', query_part, key_part, precision=HIGH) * scale_val)
    prob_low = low(jax.nn.softmax(scores, axis=-1))
    attended = both_round(jnp.einsum('bhqk,bkhd->bqhd', prob_low, value_part, precision=HIGH).reshape(row_count, D))
    branch = low_back(jnp.dot(attended, out_mat, precision=HIGH))
    middle = flat_tok + branch + out_vec
    mixed_in = low(layer_norm(middle, gain_two, shift_two))
    logits = low_back(jnp.dot(mixed_in, router_mat, precision=HIGH))
    router_prob = jax.nn.softmax(logits, axis=-1)
    target = jnp.where(kept_flag == 1, routes * CAP + slot_pos, EXPERTS * CAP).astype(jnp.int32)
    sources = jnp.repeat(mixed_in, TOP, axis=0)
    buffer = jnp.zeros((EXPERTS * CAP + 1, D), jnp.float32).at[target.reshape(-1)].add(sources)
    expert_rows = buffer[:EXPERTS * CAP].reshape(EXPERTS, CAP, D)
    hidden_pre = low_back(jnp.einsum('ecd,edf->ecf', expert_rows, inner_mat, precision=HIGH) + inner_vec[:, None, :])
    activated = low(jax.nn.gelu(hidden_pre, approximate=False))
    expert_res = low_back(jnp.einsum('ecf,efd->ecd', activated, outer_mat, precision=HIGH) + outer_vec[:, None, :])
    padded_res = jnp.concatenate([expert_res.reshape(EXPERTS * CAP, D), jnp.zeros((1, D), jnp.float32)], 0)
    picked = padded_res[target]
    gate_vals = jnp.take_along_axis(router_prob, routes, axis=1) * kept_flag.astype(jnp.float32)
    final_sum = middle + lax.optimization_barrier(jnp.sum(gate_vals[:, :, None] * picked, axis=1))
    live_tok = jnp.repeat(live_img, LEN)
    result = final_sum * live_tok[:, None]
    prob_sum = lax.optimization_barrier(jnp.sum(router_prob * live_tok[:, None], axis=0))
    return (result.reshape(MB_IMG, LEN, D), prob_sum)

def reference(images, image_count, expert_index, expert_slot, keep, cotangent, ln1_gain, ln1_bias, qkv_weight, qv_bias, out_weight, out_bias, ln2_gain, ln2_bias, router_weight, expert_in, expert_in_bias, expert_out, expert_out_bias):
    blocks = N_DP * MICRO
    params = (ln1_gain.astype(jnp.float32), ln1_bias.astype(jnp.float32), qkv_weight.astype(jnp.float32), qv_bias.astype(jnp.float32), out_weight.astype(jnp.float32), out_bias.astype(jnp.float32), ln2_gain.astype(jnp.float32), ln2_bias.astype(jnp.float32), router_weight.astype(jnp.float32), expert_in.astype(jnp.float32), expert_in_bias.astype(jnp.float32), expert_out.astype(jnp.float32), expert_out_bias.astype(jnp.float32))
    inputs = images.astype(jnp.float32).reshape(blocks, MB_IMG, LEN, D)
    live_slots = (jnp.arange(SLOTS)[None, :] < image_count[:, None]).astype(jnp.float32)
    live_img = live_slots.reshape(blocks, MB_IMG)
    routes = expert_index.reshape(blocks, MB_IMG * LEN, TOP)
    slot_pos = expert_slot.reshape(blocks, MB_IMG * LEN, TOP)
    kept_flag = keep.reshape(blocks, MB_IMG * LEN, TOP)
    live_tok = jnp.repeat(live_slots.reshape(-1), LEN)
    hits = (expert_index.reshape(-1, TOP)[:, :, None] == jnp.arange(EXPERTS)[None, None, :]).astype(jnp.float32)
    counts = lax.optimization_barrier(jnp.sum(hits * live_tok[:, None, None], axis=(0, 1)))
    live_total = jnp.sum(live_tok)

    def forward(inputs_in, params_in):

        def one_block(packed):
            return block_forward(params_in, packed[0], packed[1], packed[2], packed[3], packed[4])
        results, prob_sums = lax.map(jax.checkpoint(one_block), (inputs_in, routes, slot_pos, kept_flag, live_img))
        balance_val = EXPERTS * jnp.sum(counts / live_total * lax.optimization_barrier(jnp.sum(prob_sums, 0)) / live_total)
        return (results, balance_val)
    (results, balance_val), pullback = jax.vjp(forward, inputs, params)
    grad_in, grad_params = pullback((cotangent.astype(jnp.float32).reshape(blocks, MB_IMG, LEN, D), BALANCE_WEIGHT * live_total))
    return (results.reshape(IMAGES, LEN, D).astype(jnp.bfloat16), grad_in.reshape(IMAGES, LEN, D).astype(jnp.bfloat16), balance_val, grad_params[0], grad_params[1], grad_params[2], grad_params[3], grad_params[4], grad_params[5], grad_params[6], grad_params[7], grad_params[8], grad_params[9], grad_params[10], grad_params[11], grad_params[12])
```

```python
import functools
import math

import jax
import jax.numpy as jnp
from jax import lax
from jax.experimental import pallas as pl
from jax.experimental.pallas import tpu as pltpu
from jax.sharding import PartitionSpec as P

HEADS = 8
HEAD_DIM = 64
EXPERTS = 8
MICRO = 4
CAP = 128
PAIR = 2 * HEAD_DIM

EPSILON = 1e-06
BALANCE_WEIGHT = 8.0

BF = jnp.bfloat16
F32 = jnp.float32

ROW_GAIN1, ROW_BIAS1, ROW_QBIAS, ROW_VBIAS, ROW_OBIAS, ROW_GAIN2, ROW_BIAS2 = range(8, 15)
SMALL = 128
GRAD_ROWS = 16
COL_T0, COL_T1, COL_R0, COL_R1, COL_K0, COL_K1, COL_LIVE = range(7)
VMEM_LIMIT = 60 * 1024 * 1024


def mm(a, b):
    return lax.dot_general(a, b, (((1,), (0,)), ((), ())), preferred_element_type=F32)


def mm_nt(a, b):
    return lax.dot_general(a, b, (((1,), (1,)), ((), ())), preferred_element_type=F32)


def mm_tn(a, b):
    return lax.dot_general(a, b, (((0,), (0,)), ((), ())), preferred_element_type=F32)


def load_padded(dst, src, seq_len, pad_len):
    for i in range(2):
        tail = (seq_len // 16) * 16
        dst[i * pad_len + tail : (i + 1) * pad_len, :] = jnp.zeros(
            (pad_len - tail, dst.shape[1]), dst.dtype
        )
        dst[i * pad_len : i * pad_len + seq_len, :] = src[i].astype(dst.dtype)


def norm_parts(x):
    mean = jnp.mean(x, -1, keepdims=True)
    centered = x - mean
    spread = jnp.mean(centered * centered, -1, keepdims=True)
    inv = lax.rsqrt(spread + EPSILON)
    return centered * inv, inv


def norm_back(d_out, xhat, inv, gain):
    d_hat = d_out * gain
    first = jnp.mean(d_hat, -1, keepdims=True)
    second = jnp.mean(d_hat * xhat, -1, keepdims=True)
    return inv * (d_hat - first - xhat * second)


def half_masks():
    lane = lax.broadcasted_iota(jnp.int32, (1, PAIR), 1)
    low = jnp.where(lane < HEAD_DIM, 1.0, 0.0)
    return low.astype(BF), (1.0 - low).astype(BF), lane < HEAD_DIM


def stack_heads(block, low, high):
    return jnp.concatenate([block * low, block * high], 0)


def forward_kernel(
    m0,
    seq_len,
    pad_len,
    cnt_ref,
    img_ref,
    cot_ref,
    lane_ref,
    meta_ref,
    w_ref,
    small_ref,
    xd_ref,
    qkv_ref,
    p_ref,
    att_ref,
    mid_ref,
    rp_ref,
    psum_ref,
    xs,
    cs,
):
    step = pl.program_id(0)
    width = xs.shape[1]
    alive = cnt_ref[0] > 2 * (m0 + step)

    @pl.when(step == 0)
    def _():
        psum_ref[...] = jnp.zeros_like(psum_ref)

    @pl.when(jnp.logical_not(alive))
    def _():
        xd_ref[...] = jnp.zeros_like(xd_ref)

    @pl.when(alive)
    def _():
        load_padded(xs, img_ref, seq_len, pad_len)
        load_padded(cs, cot_ref, seq_len, pad_len)
        xhat, inv = norm_parts(xs[...])
        normed = (
            xhat * small_ref[ROW_GAIN1 : ROW_GAIN1 + 1, :] + small_ref[ROW_BIAS1 : ROW_BIAS1 + 1, :]
        ).astype(BF)
        for part, row in ((0, ROW_QBIAS), (1, None), (2, ROW_VBIAS)):
            cols = slice(part * width, (part + 1) * width)
            value = mm(normed, w_ref[:, cols])
            if row is not None:
                value = value + small_ref[row : row + 1, :]
            qkv_ref[0, :, cols] = value.astype(BF)
        low, high, low_mask = half_masks()
        key_ok = lax.broadcasted_iota(jnp.int32, (1, pad_len), 1) < seq_len
        for i in range(2):
            rows = slice(i * pad_len, (i + 1) * pad_len)
            for hp in range(HEADS // 2):
                at = hp * PAIR
                q = qkv_ref[0, rows, at : at + PAIR]
                k = qkv_ref[0, rows, width + at : width + at + PAIR]
                v = qkv_ref[0, rows, 2 * width + at : 2 * width + at + PAIR]
                s = mm_nt(stack_heads(q, low, high), k) * (HEAD_DIM**-0.5)
                s = jnp.where(key_ok, s, -1e30)
                e = jnp.exp(s - jnp.max(s, -1, keepdims=True))
                p = (e * (1.0 / jnp.sum(e, -1, keepdims=True))).astype(BF)
                p_ref[0, i, hp] = p
                o = mm(p, v)
                att_ref[0, rows, at : at + PAIR] = jnp.where(
                    low_mask, o[:pad_len], o[pad_len:]
                ).astype(BF)
        middle = (
            xs[...]
            + mm(att_ref[0], w_ref[:, 3 * width : 4 * width])
            + small_ref[ROW_OBIAS : ROW_OBIAS + 1, :]
        )
        mid_ref[0] = middle
        xhat2, inv2 = norm_parts(middle)
        mixed = (
            xhat2 * small_ref[ROW_GAIN2 : ROW_GAIN2 + 1, :]
            + small_ref[ROW_BIAS2 : ROW_BIAS2 + 1, :]
        ).astype(BF)
        logits = mm(mixed, w_ref[:, 4 * width : 4 * width + SMALL])
        lane = lax.broadcasted_iota(jnp.int32, (1, SMALL), 1)
        logits = jnp.where(lane < EXPERTS, logits, -1e30)
        e = jnp.exp(logits - jnp.max(logits, -1, keepdims=True))
        rp = e * (1.0 / jnp.sum(e, -1, keepdims=True))
        rp_ref[0] = rp
        live = meta_ref[0, :, COL_LIVE : COL_LIVE + 1]
        psum_ref[0:1, :] += jnp.sum(rp * live, 0, keepdims=True)
        d_final = cs[...] * live
        lane_f = lane.astype(F32)
        weighted = []
        for route, kept in ((COL_R0, COL_K0), (COL_R1, COL_K1)):
            hot = lane_f == meta_ref[0, :, route : route + 1]
            gate = jnp.sum(jnp.where(hot, rp, 0.0), -1, keepdims=True)
            gate = gate * meta_ref[0, :, kept : kept + 1]
            weighted.append((gate * d_final).astype(BF))
        slot = lax.broadcasted_iota(jnp.int32, (CAP, 1), 0).astype(F32)
        for e_id in range(EXPERTS):
            here = slot + float(e_id * CAP)
            sel0 = jnp.where(here == lane_ref[0, 0:1, :], 1.0, 0.0)
            sel1 = jnp.where(here == lane_ref[0, 1:2, :], 1.0, 0.0)
            xd_ref[e_id, 0, 0] = mm((sel0 + sel1).astype(BF), mixed).astype(BF)
            xd_ref[e_id, 1, 0] = (
                mm(sel0.astype(BF), weighted[0]) + mm(sel1.astype(BF), weighted[1])
            ).astype(BF)


def full_block(shape):
    return pl.BlockSpec(shape, lambda i: (0,) * len(shape))


def forward_call(m0, mbc, images, cotangent, count, lane_t, meta, weights, small):
    seq_len, width = images.shape[1], images.shape[2]
    rows = meta.shape[1]
    pad_len = rows // 2
    at = lambda i: i + m0
    mb = images.shape[0] // MICRO
    return pl.pallas_call(
        functools.partial(forward_kernel, m0, seq_len, pad_len),
        grid=(mbc,),
        in_specs=[
            pl.BlockSpec(memory_space=pltpu.SMEM),
            pl.BlockSpec((mb, seq_len, width), lambda i: (at(i), 0, 0)),
            pl.BlockSpec((mb, seq_len, width), lambda i: (at(i), 0, 0)),
            pl.BlockSpec((1, 8, rows), lambda i: (at(i), 0, 0)),
            pl.BlockSpec((1, rows, 8), lambda i: (at(i), 0, 0)),
            full_block(weights.shape),
            full_block(small.shape),
        ],
        out_specs=[
            pl.BlockSpec((EXPERTS, 2, 1, CAP, width), lambda i: (0, 0, i, 0, 0)),
            pl.BlockSpec((1, rows, 3 * width), lambda i: (i, 0, 0)),
            pl.BlockSpec((1, 2, HEADS // 2, rows, pad_len), lambda i: (i, 0, 0, 0, 0)),
            pl.BlockSpec((1, rows, width), lambda i: (i, 0, 0)),
            pl.BlockSpec((1, rows, width), lambda i: (i, 0, 0)),
            pl.BlockSpec((1, rows, SMALL), lambda i: (i, 0, 0)),
            full_block((8, SMALL)),
        ],
        out_shape=[
            jax.ShapeDtypeStruct((EXPERTS, 2, mbc, CAP, width), BF),
            jax.ShapeDtypeStruct((mbc, rows, 3 * width), BF),
            jax.ShapeDtypeStruct((mbc, 2, HEADS // 2, rows, pad_len), BF),
            jax.ShapeDtypeStruct((mbc, rows, width), BF),
            jax.ShapeDtypeStruct((mbc, rows, width), F32),
            jax.ShapeDtypeStruct((mbc, rows, SMALL), F32),
            jax.ShapeDtypeStruct((8, SMALL), F32),
        ],
        scratch_shapes=[pltpu.VMEM((rows, width), F32), pltpu.VMEM((rows, width), F32)],
        compiler_params=pltpu.CompilerParams(vmem_limit_bytes=VMEM_LIMIT),
        cost_estimate=pl.CostEstimate(
            flops=mbc * 12 * 10**9, bytes_accessed=mbc * 10 * 10**6, transcendentals=0
        ),
        name="dense_forward",
    )(count, images, cotangent, lane_t, meta, weights, small)


GROUP = 4
FF_TILE = 512


def expert_kernel(
    m0,
    mbc,
    has_acc,
    last,
    cnt_ref,
    x_ref,
    w1_ref,
    w2_ref,
    b1_ref,
    b2_ref,
    *rest,
):
    if has_acc:
        a1_ref, a2_ref, ab1_ref, ab2_ref = rest[:4]
        rest = rest[4:]
    y_ref, g1_ref, g2_ref, gb1_ref, gb2_ref = rest[:5]
    rest = rest[5:]
    if last:
        s1, s2, order, xin, din, xout, dout = rest
    else:
        order, xin, din, xout, dout = rest
        s1, s2 = g1_ref, g2_ref
    width = x_ref.shape[-1]
    ff = w1_ref.shape[1]
    if has_acc:
        s1[...] = a1_ref[...]
        s2[...] = a2_ref[...]
        gb1_ref[...] = ab1_ref[...]
        gb2_ref[...] = ab2_ref[...]
    else:
        s1[...] = jnp.zeros_like(s1)
        s2[...] = jnp.zeros_like(s2)
        gb1_ref[...] = jnp.zeros_like(gb1_ref)
        gb2_ref[...] = jnp.zeros_like(gb2_ref)
    blocks = EXPERTS * mbc

    def is_live(b):
        return (cnt_ref[b // mbc] > 2 * (m0 + b % mbc)).astype(jnp.int32)

    live_total = jnp.int32(0)
    for b in range(blocks):
        live_total = live_total + is_live(b)
    head, tail = jnp.int32(0), live_total
    for b in range(blocks):
        flag = is_live(b)
        order[jnp.where(flag == 1, head, tail)] = b
        head = head + flag
        tail = tail + (1 - flag)

    def one_group(g, carry):
        for j in range(GROUP):
            b = order[g * GROUP + j]
            xin[j * CAP : (j + 1) * CAP, :] = x_ref[b // mbc, 0, b % mbc]
            din[j * CAP : (j + 1) * CAP, :] = x_ref[b // mbc, 1, b % mbc]
        rows_in, d_res = xin[...], din[...]
        gb2_ref[0:1, :] += jnp.sum(d_res.astype(F32), 0, keepdims=True)
        for f in range(ff // FF_TILE):
            cols = slice(f * FF_TILE, (f + 1) * FF_TILE)
            w1 = w1_ref[:, cols]
            w2 = w2_ref[cols, :]
            h = mm(rows_in, w1) + b1_ref[0:1, cols]
            bell = jnp.exp(-0.5 * h * h)
            t = 1.0 / (1.0 + (0.3275911 / math.sqrt(2.0)) * jnp.abs(h))
            poly = t * (
                0.5 * 0.254829592
                + t
                * (
                    0.5 * -0.284496736
                    + t * (0.5 * 1.421413741 + t * (0.5 * -1.453152027 + t * (0.5 * 1.061405429)))
                )
            )
            upper = poly * bell
            cdf = jnp.where(h < 0.0, upper, 1.0 - upper)
            act = (h * cdf).astype(BF)
            slope = cdf + h * bell * (1.0 / math.sqrt(2.0 * math.pi))
            d_act = mm_nt(d_res, w2)
            d_hid_f = (d_act * slope).astype(BF)
            gb1_ref[0:1, cols] += jnp.sum(d_hid_f.astype(F32), 0, keepdims=True)
            res = mm(act, w2)
            d_rows = mm_nt(d_hid_f, w1)
            if f == 0:
                xout[...] = res
                dout[...] = d_rows
            else:
                xout[...] += res
                dout[...] += d_rows
            s1[:, cols] += mm_tn(rows_in, d_hid_f)
            s2[cols, :] += mm_tn(act, d_res)
        for j in range(GROUP):
            b = order[g * GROUP + j]
            y_ref[b // mbc, 0, b % mbc] = (
                xout[j * CAP : (j + 1) * CAP, :] + b2_ref[0:1, :]
            ).astype(BF)
            y_ref[b // mbc, 1, b % mbc] = dout[j * CAP : (j + 1) * CAP, :].astype(BF)
        return carry

    lax.fori_loop(0, (live_total + GROUP - 1) // GROUP, one_group, 0)
    if last:
        g1_ref[...] = s1[...].astype(BF)
        g2_ref[...] = s2[...].astype(BF)


def expert_call(m0, mbc, last, counts, x, w1, w2, b1, b2, acc):
    width, ff = w1.shape
    grad_type = BF if last else F32
    vm = pl.BlockSpec(memory_space=pltpu.VMEM)
    scratch = []
    if last:
        scratch += [pltpu.VMEM((width, ff), F32), pltpu.VMEM((ff, width), F32)]
    scratch += [
        pltpu.SMEM((EXPERTS * mbc,), jnp.int32),
        pltpu.VMEM((GROUP * CAP, width), BF),
        pltpu.VMEM((GROUP * CAP, width), BF),
        pltpu.VMEM((GROUP * CAP, width), F32),
        pltpu.VMEM((GROUP * CAP, width), F32),
    ]
    return pl.pallas_call(
        functools.partial(expert_kernel, m0, mbc, acc is not None, last),
        in_specs=[pl.BlockSpec(memory_space=pltpu.SMEM)] + [vm] * (5 + (0 if acc is None else 4)),
        out_specs=[vm] * 5,
        out_shape=[
            jax.ShapeDtypeStruct(x.shape, BF),
            jax.ShapeDtypeStruct((width, ff), grad_type),
            jax.ShapeDtypeStruct((ff, width), grad_type),
            jax.ShapeDtypeStruct((8, ff), F32),
            jax.ShapeDtypeStruct((8, width), F32),
        ],
        scratch_shapes=scratch,
        compiler_params=pltpu.CompilerParams(vmem_limit_bytes=VMEM_LIMIT),
        cost_estimate=pl.CostEstimate(
            flops=mbc * 20 * 10**9, bytes_accessed=mbc * 10 * 10**6, transcendentals=0
        ),
        name="expert_both",
    )(counts, x, w1, w2, b1, b2, *(() if acc is None else acc))


def backward_kernel(
    m0,
    seq_len,
    pad_len,
    has_acc,
    cnt_ref,
    img_ref,
    cot_ref,
    meta_ref,
    y_ref,
    qkv_ref,
    p_ref,
    att_ref,
    mid_ref,
    rp_ref,
    coef_ref,
    w_ref,
    small_ref,
    *rest,
):
    if has_acc:
        accw_ref, accs_ref = rest[:2]
        rest = rest[4:]
    out_ref, grad_ref, gw_ref, gs_ref, xs, cs, dq = rest
    step = pl.program_id(0)
    width = xs.shape[1]
    alive = cnt_ref[0] > 2 * (m0 + step)

    @pl.when(step == 0)
    def _():
        if has_acc:
            gw_ref[...] = accw_ref[...]
            gs_ref[...] = accs_ref[...]
        else:
            gw_ref[...] = jnp.zeros_like(gw_ref)
            gs_ref[...] = jnp.zeros_like(gs_ref)

    @pl.when(jnp.logical_not(alive))
    def _():
        out_ref[...] = jnp.zeros_like(out_ref)
        grad_ref[...] = jnp.zeros_like(grad_ref)

    def add_row(row, value):
        gs_ref[row : row + 1, :] += jnp.sum(value, 0, keepdims=True)

    @pl.when(alive)
    def _():
        load_padded(xs, img_ref, seq_len, pad_len)
        load_padded(cs, cot_ref, seq_len, pad_len)
        rows = xs.shape[0]
        live = meta_ref[0, :, COL_LIVE : COL_LIVE + 1]
        d_final = cs[...] * live
        middle = mid_ref[0]
        rp = rp_ref[0]
        lane = lax.broadcasted_iota(jnp.int32, (1, SMALL), 1)
        lane_f = lane.astype(F32)
        slot = lax.broadcasted_iota(jnp.int32, (1, EXPERTS * CAP), 1).astype(F32)
        res = y_ref[:, 0, 0].reshape(EXPERTS * CAP, width)
        d_rows = y_ref[:, 1, 0].reshape(EXPERTS * CAP, width)
        final = middle
        d_prob = coef_ref[0:1, :] * live
        sel_all = None
        for target, route, kept in ((COL_T0, COL_R0, COL_K0), (COL_T1, COL_R1, COL_K1)):
            sel = jnp.where(slot == meta_ref[0, :, target : target + 1], 1.0, 0.0).astype(BF)
            sel_all = sel if sel_all is None else sel_all + sel
            picked = mm(sel, res)
            keep = meta_ref[0, :, kept : kept + 1]
            hot = lane_f == meta_ref[0, :, route : route + 1]
            gate = jnp.sum(jnp.where(hot, rp, 0.0), -1, keepdims=True) * keep
            final = final + gate * picked
            d_gate = jnp.sum(picked * d_final, -1, keepdims=True) * keep
            d_prob = d_prob + jnp.where(hot, d_gate, 0.0)
        final = final * live
        for i in range(2):
            out_ref[i] = final[i * pad_len : i * pad_len + seq_len, :].astype(BF)
        d_mixed = mm(sel_all, d_rows)
        d_logits = (rp * (d_prob - jnp.sum(rp * d_prob, -1, keepdims=True))).astype(BF)
        d_mixed = d_mixed + mm_nt(d_logits, w_ref[:, 4 * width : 4 * width + SMALL])
        gain2 = small_ref[ROW_GAIN2 : ROW_GAIN2 + 1, :]
        xhat2, inv2 = norm_parts(middle)
        mixed = (xhat2 * gain2 + small_ref[ROW_BIAS2 : ROW_BIAS2 + 1, :]).astype(BF)
        gs_ref[0:EXPERTS, :] += mm_tn(d_logits, mixed)[0:EXPERTS, :]
        add_row(ROW_GAIN2, d_mixed * xhat2)
        add_row(ROW_BIAS2, d_mixed)
        d_middle = d_final + norm_back(d_mixed, xhat2, inv2, gain2)
        add_row(ROW_OBIAS, d_middle)
        cs[...] = d_middle
        d_branch = d_middle.astype(BF)
        gw_ref[:, 3 * width : 4 * width] += mm_tn(att_ref[0], d_branch)
        d_att_all = mm_nt(d_branch, w_ref[:, 3 * width : 4 * width]).astype(BF)
        low, high, low_mask = half_masks()
        scale = HEAD_DIM**-0.5
        for i in range(2):
            span = slice(i * pad_len, (i + 1) * pad_len)
            for hp in range(HEADS // 2):
                at = hp * PAIR
                q = qkv_ref[0, span, at : at + PAIR]
                k = qkv_ref[0, span, width + at : width + at + PAIR]
                v = qkv_ref[0, span, 2 * width + at : 2 * width + at + PAIR]
                d_att = stack_heads(d_att_all[span, at : at + PAIR], low, high)
                p = p_ref[0, i, hp]
                pf = p.astype(F32)
                d_attn = mm_nt(d_att, v)
                d_s = (pf * (d_attn - jnp.sum(pf * d_attn, -1, keepdims=True))).astype(BF)
                d_v = mm_tn(p, d_att)
                d_k = mm_tn(d_s, stack_heads(q, low, high)) * scale
                d_q = mm(d_s, k) * scale
                dq[span, at : at + PAIR] = jnp.where(
                    low_mask, d_q[:pad_len], d_q[pad_len:]
                ).astype(BF)
                dq[span, width + at : width + at + PAIR] = d_k.astype(BF)
                dq[span, 2 * width + at : 2 * width + at + PAIR] = d_v.astype(BF)
        gain1 = small_ref[ROW_GAIN1 : ROW_GAIN1 + 1, :]
        xhat, inv = norm_parts(xs[...])
        normed = (xhat * gain1 + small_ref[ROW_BIAS1 : ROW_BIAS1 + 1, :]).astype(BF)
        add_row(ROW_QBIAS, dq[:, 0:width].astype(F32))
        add_row(ROW_VBIAS, dq[:, 2 * width : 3 * width].astype(F32))
        gw_ref[:, 0 : 3 * width] += mm_tn(normed, dq[...])
        d_normed = mm_nt(dq[...], w_ref[:, 0 : 3 * width])
        add_row(ROW_GAIN1, d_normed * xhat)
        add_row(ROW_BIAS1, d_normed)
        d_tok = cs[...] + norm_back(d_normed, xhat, inv, gain1)
        for i in range(2):
            grad_ref[i] = d_tok[i * pad_len : i * pad_len + seq_len, :].astype(BF)


def backward_call(m0, mbc, images, cotangent, count, meta, back, saved, coef, weights, small, acc):
    seq_len, width = images.shape[1], images.shape[2]
    rows = meta.shape[1]
    pad_len = rows // 2
    mb = images.shape[0] // MICRO
    qkv, probs, att, mid, rp = saved
    at = lambda i: i + m0
    image_block = pl.BlockSpec((mb, seq_len, width), lambda i: (at(i), 0, 0))
    in_specs = [
        pl.BlockSpec(memory_space=pltpu.SMEM),
        image_block,
        image_block,
        pl.BlockSpec((1, rows, 8), lambda i: (at(i), 0, 0)),
        pl.BlockSpec((EXPERTS, 2, 1, CAP, width), lambda i: (0, 0, i, 0, 0)),
        pl.BlockSpec((1, rows, 3 * width), lambda i: (i, 0, 0)),
        pl.BlockSpec((1, 2, HEADS // 2, rows, pad_len), lambda i: (i, 0, 0, 0, 0)),
        pl.BlockSpec((1, rows, width), lambda i: (i, 0, 0)),
        pl.BlockSpec((1, rows, width), lambda i: (i, 0, 0)),
        pl.BlockSpec((1, rows, SMALL), lambda i: (i, 0, 0)),
        full_block(coef.shape),
        full_block(weights.shape),
        full_block(small.shape),
    ]
    args = [count, images, cotangent, meta, back, qkv, probs, att, mid, rp, coef, weights, small]
    aliases = {}
    if acc is not None:
        base = len(args)
        in_specs += [full_block(acc[0].shape), full_block(acc[1].shape)]
        in_specs += [pl.BlockSpec(memory_space=pl.ANY)] * 2
        args += list(acc)
        aliases = {base + 2: 0, base + 3: 1}
    return pl.pallas_call(
        functools.partial(backward_kernel, m0, seq_len, pad_len, acc is not None),
        grid=(mbc,),
        in_specs=in_specs,
        out_specs=[
            image_block,
            image_block,
            full_block((width, 4 * width)),
            full_block((GRAD_ROWS, width)),
        ],
        out_shape=[
            jax.ShapeDtypeStruct(images.shape, BF),
            jax.ShapeDtypeStruct(images.shape, BF),
            jax.ShapeDtypeStruct((width, 4 * width), F32),
            jax.ShapeDtypeStruct((GRAD_ROWS, width), F32),
        ],
        scratch_shapes=[
            pltpu.VMEM((rows, width), F32),
            pltpu.VMEM((rows, width), F32),
            pltpu.VMEM((rows, 3 * width), BF),
        ],
        input_output_aliases=aliases,
        compiler_params=pltpu.CompilerParams(vmem_limit_bytes=VMEM_LIMIT),
        cost_estimate=pl.CostEstimate(
            flops=mbc * 20 * 10**9, bytes_accessed=mbc * 10 * 10**6, transcendentals=0
        ),
        name="dense_backward",
    )(*args)


def shards(
    total,
    images,
    image_count,
    expert_index,
    expert_slot,
    keep,
    cotangent,
    ln1_gain,
    ln1_bias,
    qkv_weight,
    qv_bias,
    out_weight,
    out_bias,
    ln2_gain,
    ln2_bias,
    router_weight,
    expert_in,
    expert_in_bias,
    expert_out,
    expert_out_bias,
):
    slots, seq_len, width = images.shape
    planes = total // EXPERTS
    rows = width // total
    ff = expert_in.shape[2]
    ff_rows = ff // total
    mb = slots // MICRO
    pad_len = -(-seq_len // 16) * 16
    plane_groups = [[z * EXPERTS + p for p in range(EXPERTS)] for z in range(planes)]
    z_groups = [[z * EXPERTS + p for z in range(planes)] for p in range(EXPERTS)]

    def plane_swap(v):
        return lax.all_to_all(v, "dp", 0, 0, tiled=True, axis_index_groups=plane_groups)

    def z_swap(v):
        return lax.all_to_all(v, "dp", 0, 0, tiled=True, axis_index_groups=z_groups)

    def z_gather(v):
        return lax.all_gather(v, "dp", axis=0, tiled=True, axis_index_groups=z_groups)

    small_cols = jnp.concatenate(
        [
            router_weight,
            ln1_gain[:, None],
            ln1_bias[:, None],
            qv_bias.T,
            out_bias[:, None],
            ln2_gain[:, None],
            ln2_bias[:, None],
            jnp.zeros((rows, SMALL - 15), BF),
        ],
        1,
    )
    packed = jnp.concatenate([qkv_weight, out_weight, small_cols], 1)
    wide = packed.shape[1]
    packed = z_gather(packed)
    packed = plane_swap(jnp.broadcast_to(packed[None], (EXPERTS,) + packed.shape))
    weights = (
        packed.reshape(EXPERTS, planes, rows, wide).transpose(1, 0, 2, 3).reshape(width, wide)
    )
    small = weights[:, 4 * width :].astype(F32).T

    live_img = jnp.arange(slots) < image_count[0]
    live_tok = jnp.broadcast_to(live_img[:, None, None], (slots, seq_len, 1)).astype(F32)
    target = jnp.where(keep == 1, expert_index * CAP + expert_slot, -1).astype(F32)
    hits = (expert_index[..., None] == jnp.arange(EXPERTS)).astype(F32) * live_tok[..., None]
    local_counts = jnp.sum(hits, axis=(0, 1, 2))
    meta = jnp.concatenate(
        [
            target,
            expert_index.astype(F32),
            keep.astype(F32),
            live_tok,
            jnp.zeros((slots, seq_len, 1), F32),
        ],
        -1,
    )
    fill = jnp.array([-1.0, -1.0, 0.0, 0.0, 0.0, 0.0, 0.0, 0.0], F32)
    meta = jnp.concatenate(
        [meta, jnp.broadcast_to(fill, (slots, pad_len - seq_len, 8))], 1
    ).reshape(MICRO, mb * pad_len, 8)
    lane_t = meta.transpose(0, 2, 1)

    high = jnp.floor(local_counts * (1.0 / 128.0))
    told = jnp.concatenate(
        [
            expert_in_bias,
            expert_out_bias,
            jnp.broadcast_to(
                jnp.concatenate(
                    [high, local_counts - 128.0 * high, image_count.astype(F32)]
                ).astype(BF)[None],
                (EXPERTS, 2 * EXPERTS + 1),
            ),
        ],
        1,
    )
    told = jnp.pad(told, ((0, 0), (0, 128 - told.shape[1])))
    told = jnp.broadcast_to(told[None], (planes,) + told.shape).reshape(total, 128)
    heard = lax.all_to_all(told, "dp", 0, 0, tiled=True).astype(F32)
    in_bias = heard[:, :ff_rows].reshape(1, ff)
    out_bias_e = heard[:, ff_rows : ff_rows + rows].reshape(1, width)
    base = ff_rows + rows
    tail = heard[:, base : base + 2 * EXPERTS + 1]
    counts_all = jnp.sum(tail[:, :EXPERTS] * 128.0 + tail[:, EXPERTS : 2 * EXPERTS], 0)
    all_images = tail[:, 2 * EXPERTS]
    live_total = jnp.sum(all_images) * float(seq_len)
    plane_id = lax.axis_index("dp") // EXPERTS
    plane_counts = lax.dynamic_slice(all_images, (plane_id * EXPERTS,), (EXPERTS,)).astype(
        jnp.int32
    )
    coef = jnp.pad(BALANCE_WEIGHT * EXPERTS * counts_all / live_total, (0, SMALL - EXPERTS))
    coef = jnp.broadcast_to(coef[None], (8, SMALL))
    in_bias = jnp.broadcast_to(in_bias, (8, ff))
    out_bias_e = jnp.broadcast_to(out_bias_e, (8, width))

    w1 = z_gather(plane_swap(expert_in).reshape(EXPERTS * rows, ff))
    w2 = z_gather(plane_swap(expert_out).reshape(EXPERTS * ff_rows, width))

    chunks = 2
    mbc = MICRO // chunks
    saved, sent, prob_sums = [], [], []
    for c in range(chunks):
        xd, qkv, probs, att, mid, rp, prob = forward_call(
            c * mbc, mbc, images, cotangent, image_count, lane_t, meta, weights, small
        )
        saved.append((qkv, probs, att, mid, rp))
        prob_sums.append(prob[0, :EXPERTS])
        sent.append(plane_swap(xd))
    acc = None
    back = []
    for c in range(chunks):
        y, *acc = expert_call(
            c * mbc, mbc, c == chunks - 1, plane_counts, sent[c], w1, w2, in_bias, out_bias_e, acc
        )
        back.append(plane_swap(y))
    g1, g2, gb1, gb2 = acc

    def z_reduce(v):
        return lax.psum_scatter(
            v, "dp", scatter_dimension=0, tiled=True, axis_index_groups=z_groups
        )

    expert_in_grad = plane_swap(z_reduce(g1).reshape(EXPERTS, rows, ff)).astype(F32)
    expert_out_grad = plane_swap(z_reduce(g2).reshape(EXPERTS, ff_rows, width)).astype(F32)
    bias_told = jnp.concatenate([gb1[0].reshape(total, ff_rows), gb2[0].reshape(total, rows)], 1)
    bias_told = jnp.pad(bias_told, ((0, 0), (0, 128 - bias_told.shape[1])))
    bias_heard = lax.all_to_all(bias_told, "dp", 0, 0, tiled=True)
    bias_heard = jnp.sum(bias_heard.reshape(planes, EXPERTS, 128), 0)
    expert_in_bias_grad = bias_heard[:, :ff_rows]
    expert_out_bias_grad = bias_heard[:, ff_rows : ff_rows + rows]

    acc = None
    for c in range(chunks):
        block_out, image_grad, gw, gs = backward_call(
            c * mbc,
            mbc,
            images,
            cotangent,
            image_count,
            meta,
            back[c],
            saved[c],
            coef,
            weights,
            small,
            acc,
        )
        acc = (gw, gs, block_out, image_grad)

    prob_sum = prob_sums[0]
    for piece in prob_sums[1:]:
        prob_sum = prob_sum + piece
    p_hi = prob_sum.astype(BF)
    p_mid = (prob_sum - p_hi.astype(F32)).astype(BF)
    extra = jnp.broadcast_to(jnp.concatenate([p_hi, p_mid])[None], (width, 2 * EXPERTS))
    grads = jnp.concatenate(
        [
            gw.astype(BF),
            gs.T.astype(BF),
            extra,
            jnp.zeros((width, SMALL - GRAD_ROWS - 2 * EXPERTS), BF),
        ],
        1,
    )
    grads = grads.reshape(planes, EXPERTS, rows, wide).transpose(1, 0, 2, 3)
    grads = plane_swap(grads.reshape(EXPERTS, planes * rows, wide))
    grads = jnp.sum(grads.astype(F32), 0).reshape(planes, rows, wide)
    grads = jnp.sum(z_swap(grads), 0)
    small_grads = grads[:, 4 * width :]
    prob_all = (
        small_grads[0, GRAD_ROWS : GRAD_ROWS + EXPERTS]
        + small_grads[0, GRAD_ROWS + EXPERTS : GRAD_ROWS + 2 * EXPERTS]
    )
    balance = EXPERTS * jnp.sum(counts_all / live_total * prob_all / live_total)
    return (
        block_out,
        image_grad,
        balance,
        small_grads[:, ROW_GAIN1],
        small_grads[:, ROW_BIAS1],
        grads[:, : 3 * width],
        small_grads[:, ROW_QBIAS : ROW_VBIAS + 1].T,
        grads[:, 3 * width : 4 * width],
        small_grads[:, ROW_OBIAS],
        small_grads[:, ROW_GAIN2],
        small_grads[:, ROW_BIAS2],
        small_grads[:, :EXPERTS],
        expert_in_grad,
        expert_in_bias_grad,
        expert_out_grad,
        expert_out_bias_grad,
    )


def solution(mesh):
    placed = (
        P("dp", None, None),
        P("dp"),
        P("dp", None, None),
        P("dp", None, None),
        P("dp", None, None),
        P("dp", None, None),
        P("dp"),
        P("dp"),
        P("dp", None),
        P(None, "dp"),
        P("dp", None),
        P("dp"),
        P("dp"),
        P("dp"),
        P("dp", None),
        P(None, "dp", None),
        P(None, "dp"),
        P(None, "dp", None),
        P(None, "dp"),
    )
    return jax.shard_map(
        functools.partial(shards, mesh.shape["dp"]),
        mesh=mesh,
        in_specs=placed,
        out_specs=(
            P("dp", None, None),
            P("dp", None, None),
            P(),
            P("dp"),
            P("dp"),
            P("dp", None),
            P(None, "dp"),
            P("dp", None),
            P("dp"),
            P("dp"),
            P("dp"),
            P("dp", None),
            P(None, "dp", None),
            P(None, "dp"),
            P(None, "dp", None),
            P(None, "dp"),
        ),
        check_vma=False,
    )
```

```python
import functools
import math

import jax
import jax.numpy as jnp
from jax import lax
from jax.experimental import pallas as pl
from jax.experimental.pallas import tpu as pltpu
from jax.sharding import PartitionSpec as P

HEADS = 8
HEAD_DIM = 64
EXPERTS = 8
MICRO = 4
CAP = 128
CHUNKS = (2, 2)
PAIR = 2 * HEAD_DIM

EPSILON = 1e-06
BALANCE_WEIGHT = 8.0

BF = jnp.bfloat16
F32 = jnp.float32

ROW_GAIN1, ROW_BIAS1, ROW_QBIAS, ROW_VBIAS, ROW_OBIAS, ROW_GAIN2, ROW_BIAS2 = range(8, 15)
SMALL = 128
ROW_PROB, ROW_EOUT, ROW_EIN = 16, 32, 40
BLOCK = 16
COL_T0, COL_T1, COL_R0, COL_R1, COL_K0, COL_K1, COL_LIVE = range(7)
VMEM_LIMIT = 60 * 1024 * 1024


def mm(a, b):
    return lax.dot_general(a, b, (((1,), (0,)), ((), ())), preferred_element_type=F32)


def mm_nt(a, b):
    return lax.dot_general(a, b, (((1,), (1,)), ((), ())), preferred_element_type=F32)


def mm_tn(a, b):
    return lax.dot_general(a, b, (((0,), (0,)), ((), ())), preferred_element_type=F32)


def load_padded(dst, src, seq_len, pad_len):
    for i in range(2):
        tail = (seq_len // 16) * 16
        dst[i * pad_len + tail : (i + 1) * pad_len, :] = jnp.zeros(
            (pad_len - tail, dst.shape[1]), dst.dtype
        )
        dst[i * pad_len : i * pad_len + seq_len, :] = src[i].astype(dst.dtype)


def norm_parts(x):
    mean = jnp.mean(x, -1, keepdims=True)
    centered = x - mean
    spread = jnp.mean(centered * centered, -1, keepdims=True)
    inv = lax.rsqrt(spread + EPSILON)
    return centered * inv, inv


def norm_back(d_out, xhat, inv, gain):
    d_hat = d_out * gain
    first = jnp.mean(d_hat, -1, keepdims=True)
    second = jnp.mean(d_hat * xhat, -1, keepdims=True)
    return inv * (d_hat - first - xhat * second)


def half_masks():
    lane = lax.broadcasted_iota(jnp.int32, (1, PAIR), 1)
    low = jnp.where(lane < HEAD_DIM, 1.0, 0.0)
    return low.astype(BF), (1.0 - low).astype(BF), lane < HEAD_DIM


def stack_heads(block, low, high):
    return jnp.concatenate([block * low, block * high], 0)


def forward_kernel(
    m0,
    seq_len,
    pad_len,
    cnt_ref,
    img_ref,
    cot_ref,
    lane_ref,
    meta_ref,
    w_ref,
    small_ref,
    xd_ref,
    qkv_ref,
    p_ref,
    att_ref,
    mid_ref,
    rp_ref,
    psum_ref,
    xs,
    cs,
):
    step = pl.program_id(0)
    width = xs.shape[1]
    alive = cnt_ref[0] > 2 * (m0 + step)

    @pl.when(step == 0)
    def _():
        psum_ref[...] = jnp.zeros_like(psum_ref)

    @pl.when(jnp.logical_not(alive))
    def _():
        xd_ref[...] = jnp.zeros_like(xd_ref)

    @pl.when(alive)
    def _():
        load_padded(xs, img_ref, seq_len, pad_len)
        load_padded(cs, cot_ref, seq_len, pad_len)
        xhat, inv = norm_parts(xs[...])
        normed = (
            xhat * small_ref[ROW_GAIN1 : ROW_GAIN1 + 1, :] + small_ref[ROW_BIAS1 : ROW_BIAS1 + 1, :]
        ).astype(BF)
        for part, row in ((0, ROW_QBIAS), (1, None), (2, ROW_VBIAS)):
            cols = slice(part * width, (part + 1) * width)
            value = mm(normed, w_ref[:, cols])
            if row is not None:
                value = value + small_ref[row : row + 1, :]
            qkv_ref[0, :, cols] = value.astype(BF)
        low, high, low_mask = half_masks()
        key_ok = lax.broadcasted_iota(jnp.int32, (1, pad_len), 1) < seq_len
        for i in range(2):
            rows = slice(i * pad_len, (i + 1) * pad_len)
            for hp in range(HEADS // 2):
                at = hp * PAIR
                q = qkv_ref[0, rows, at : at + PAIR]
                k = qkv_ref[0, rows, width + at : width + at + PAIR]
                v = qkv_ref[0, rows, 2 * width + at : 2 * width + at + PAIR]
                s = mm_nt(stack_heads(q, low, high), k) * (HEAD_DIM**-0.5)
                s = jnp.where(key_ok, s, -1e30)
                e = jnp.exp(s - jnp.max(s, -1, keepdims=True))
                p = (e * (1.0 / jnp.sum(e, -1, keepdims=True))).astype(BF)
                p_ref[0, i, hp] = p
                o = mm(p, v)
                att_ref[0, rows, at : at + PAIR] = jnp.where(
                    low_mask, o[:pad_len], o[pad_len:]
                ).astype(BF)
        middle = (
            xs[...]
            + mm(att_ref[0], w_ref[:, 3 * width : 4 * width])
            + small_ref[ROW_OBIAS : ROW_OBIAS + 1, :]
        )
        mid_ref[0] = middle
        xhat2, inv2 = norm_parts(middle)
        mixed = (
            xhat2 * small_ref[ROW_GAIN2 : ROW_GAIN2 + 1, :]
            + small_ref[ROW_BIAS2 : ROW_BIAS2 + 1, :]
        ).astype(BF)
        logits = mm(mixed, w_ref[:, 4 * width : 4 * width + SMALL])
        lane = lax.broadcasted_iota(jnp.int32, (1, SMALL), 1)
        logits = jnp.where(lane < EXPERTS, logits, -1e30)
        e = jnp.exp(logits - jnp.max(logits, -1, keepdims=True))
        rp = e * (1.0 / jnp.sum(e, -1, keepdims=True))
        rp_ref[0] = rp
        live = meta_ref[0, :, COL_LIVE : COL_LIVE + 1]
        psum_ref[0:1, :] += jnp.sum(rp * live, 0, keepdims=True)
        d_final = cs[...] * live
        lane_f = lane.astype(F32)
        weighted = []
        for route, kept in ((COL_R0, COL_K0), (COL_R1, COL_K1)):
            hot = lane_f == meta_ref[0, :, route : route + 1]
            gate = jnp.sum(jnp.where(hot, rp, 0.0), -1, keepdims=True)
            gate = gate * meta_ref[0, :, kept : kept + 1]
            weighted.append((gate * d_final).astype(BF))
        slot = lax.broadcasted_iota(jnp.int32, (CAP, 1), 0).astype(F32)
        for e_id in range(EXPERTS):
            here = slot + float(e_id * CAP)
            sel0 = jnp.where(here == lane_ref[0, 0:1, :], 1.0, 0.0)
            sel1 = jnp.where(here == lane_ref[0, 1:2, :], 1.0, 0.0)
            xd_ref[e_id, 0, 0] = mm((sel0 + sel1).astype(BF), mixed).astype(BF)
            xd_ref[e_id, 1, 0] = (
                mm(sel0.astype(BF), weighted[0]) + mm(sel1.astype(BF), weighted[1])
            ).astype(BF)


def full_block(shape):
    return pl.BlockSpec(shape, lambda i: (0,) * len(shape))


def forward_call(m0, mbc, images, cotangent, count, lane_t, meta, weights, small):
    seq_len, width = images.shape[1], images.shape[2]
    rows = meta.shape[1]
    pad_len = rows // 2
    at = lambda i: i + m0
    mb = images.shape[0] // MICRO
    return pl.pallas_call(
        functools.partial(forward_kernel, m0, seq_len, pad_len),
        grid=(mbc,),
        in_specs=[
            pl.BlockSpec(memory_space=pltpu.SMEM),
            pl.BlockSpec((mb, seq_len, width), lambda i: (at(i), 0, 0)),
            pl.BlockSpec((mb, seq_len, width), lambda i: (at(i), 0, 0)),
            pl.BlockSpec((1, 8, rows), lambda i: (at(i), 0, 0)),
            pl.BlockSpec((1, rows, 8), lambda i: (at(i), 0, 0)),
            full_block(weights.shape),
            full_block(small.shape),
        ],
        out_specs=[
            pl.BlockSpec((EXPERTS, 2, 1, CAP, width), lambda i: (0, 0, i, 0, 0)),
            pl.BlockSpec((1, rows, 3 * width), lambda i: (i, 0, 0)),
            pl.BlockSpec((1, 2, HEADS // 2, rows, pad_len), lambda i: (i, 0, 0, 0, 0)),
            pl.BlockSpec((1, rows, width), lambda i: (i, 0, 0)),
            pl.BlockSpec((1, rows, width), lambda i: (i, 0, 0)),
            pl.BlockSpec((1, rows, SMALL), lambda i: (i, 0, 0)),
            full_block((8, SMALL)),
        ],
        out_shape=[
            jax.ShapeDtypeStruct((EXPERTS, 2, mbc, CAP, width), BF),
            jax.ShapeDtypeStruct((mbc, rows, 3 * width), BF),
            jax.ShapeDtypeStruct((mbc, 2, HEADS // 2, rows, pad_len), BF),
            jax.ShapeDtypeStruct((mbc, rows, width), BF),
            jax.ShapeDtypeStruct((mbc, rows, width), F32),
            jax.ShapeDtypeStruct((mbc, rows, SMALL), F32),
            jax.ShapeDtypeStruct((8, SMALL), F32),
        ],
        scratch_shapes=[pltpu.VMEM((rows, width), F32), pltpu.VMEM((rows, width), F32)],
        compiler_params=pltpu.CompilerParams(vmem_limit_bytes=VMEM_LIMIT),
        cost_estimate=pl.CostEstimate(
            flops=mbc * 12 * 10**9, bytes_accessed=mbc * 10 * 10**6, transcendentals=0
        ),
        name="dense_forward",
    )(count, images, cotangent, lane_t, meta, weights, small)


GROUP = 4


def expert_kernel(
    m0,
    mbc,
    has_acc,
    last,
    cnt_ref,
    x_ref,
    w_ref,
    b1_ref,
    b2_ref,
    *rest,
):
    if has_acc:
        a1_ref, a2_ref, ab1_ref, ab2_ref = rest[:4]
        rest = rest[4:]
    if last:
        y_ref, pack_ref, gb1_ref, gb2_ref, s1, s2, order, xin, din, xout, dout = rest
    else:
        y_ref, s1, s2, gb1_ref, gb2_ref, order, xin, din, xout, dout = rest
    width = x_ref.shape[-1]
    ff = b1_ref.shape[1]
    half = w_ref.shape[1] // 2
    per_tile = width // half
    if has_acc:
        s1[...] = a1_ref[...]
        s2[...] = a2_ref[...]
        gb1_ref[...] = ab1_ref[...]
        gb2_ref[...] = ab2_ref[...]
    else:
        s1[...] = jnp.zeros_like(s1)
        s2[...] = jnp.zeros_like(s2)
        gb1_ref[...] = jnp.zeros_like(gb1_ref)
        gb2_ref[...] = jnp.zeros_like(gb2_ref)
    blocks = EXPERTS * mbc

    def is_live(b):
        return (cnt_ref[b // mbc] > 2 * (m0 + b % mbc)).astype(jnp.int32)

    live_total = jnp.int32(0)
    for b in range(blocks):
        live_total = live_total + is_live(b)
    head, tail = jnp.int32(0), live_total
    for b in range(blocks):
        flag = is_live(b)
        order[jnp.where(flag == 1, head, tail)] = b
        head = head + flag
        tail = tail + (1 - flag)

    def one_group(g, carry):
        for j in range(GROUP):
            b = order[g * GROUP + j]
            xin[j * CAP : (j + 1) * CAP, :] = x_ref[b // mbc, 0, b % mbc]
            din[j * CAP : (j + 1) * CAP, :] = x_ref[b // mbc, 1, b % mbc]
        rows_in, d_res = xin[...], din[...]
        gb2_ref[0:1, :] += jnp.sum(d_res.astype(F32), 0, keepdims=True)
        for f in range(ff // width):
            cols = slice(f * width, (f + 1) * width)
            w1 = w_ref[:, f * BLOCK : (f + 1) * BLOCK, :].reshape(width, width)
            w2 = w_ref[f * per_tile : (f + 1) * per_tile, half:, :].reshape(width, width)
            h = mm(rows_in, w1) + b1_ref[0:1, cols]
            bell = jnp.exp(-0.5 * h * h)
            t = 1.0 / (1.0 + (0.3275911 / math.sqrt(2.0)) * jnp.abs(h))
            poly = t * (
                0.5 * 0.254829592
                + t
                * (
                    0.5 * -0.284496736
                    + t * (0.5 * 1.421413741 + t * (0.5 * -1.453152027 + t * (0.5 * 1.061405429)))
                )
            )
            upper = poly * bell
            cdf = jnp.where(h < 0.0, upper, 1.0 - upper)
            act = (h * cdf).astype(BF)
            slope = cdf + h * bell * (1.0 / math.sqrt(2.0 * math.pi))
            d_act = mm_nt(d_res, w2)
            d_hid_f = (d_act * slope).astype(BF)
            gb1_ref[0:1, cols] += jnp.sum(d_hid_f.astype(F32), 0, keepdims=True)
            res = mm(act, w2)
            d_rows = mm_nt(d_hid_f, w1)
            if f == 0:
                xout[...] = res
                dout[...] = d_rows
            else:
                xout[...] += res
                dout[...] += d_rows
            s1[:, cols] += mm_tn(rows_in, d_hid_f)
            s2[cols, :] += mm_tn(act, d_res)
        for j in range(GROUP):
            b = order[g * GROUP + j]
            y_ref[b // mbc, 0, b % mbc] = (
                xout[j * CAP : (j + 1) * CAP, :] + b2_ref[0:1, :]
            ).astype(BF)
            y_ref[b // mbc, 1, b % mbc] = dout[j * CAP : (j + 1) * CAP, :].astype(BF)
        return carry

    lax.fori_loop(0, (live_total + GROUP - 1) // GROUP, one_group, 0)
    if last:
        blocks_of = width // BLOCK
        for f in range(ff // width):
            tile = s1[:, f * width : (f + 1) * width].astype(BF)
            pack_ref[:, f * BLOCK : (f + 1) * BLOCK, :] = tile.reshape(blocks_of, BLOCK, width)
        pack_ref[:, half:, :] = s2[...].astype(BF).reshape(blocks_of, half, width)


def expert_call(m0, mbc, last, counts, x, weights, b1, b2, acc):
    width, ff = weights.shape[2], b1.shape[1]
    if last:
        grads = [jax.ShapeDtypeStruct(weights.shape, BF)]
    else:
        grads = [jax.ShapeDtypeStruct((width, ff), F32), jax.ShapeDtypeStruct((ff, width), F32)]
    vm = pl.BlockSpec(memory_space=pltpu.VMEM)
    scratch = []
    if last:
        scratch += [pltpu.VMEM((width, ff), F32), pltpu.VMEM((ff, width), F32)]
    scratch += [
        pltpu.SMEM((EXPERTS * mbc,), jnp.int32),
        pltpu.VMEM((GROUP * CAP, width), BF),
        pltpu.VMEM((GROUP * CAP, width), BF),
        pltpu.VMEM((GROUP * CAP, width), F32),
        pltpu.VMEM((GROUP * CAP, width), F32),
    ]
    return pl.pallas_call(
        functools.partial(expert_kernel, m0, mbc, acc is not None, last),
        in_specs=[pl.BlockSpec(memory_space=pltpu.SMEM)] + [vm] * (4 + (0 if acc is None else 4)),
        out_specs=[vm] * (len(grads) + 3),
        out_shape=[
            jax.ShapeDtypeStruct(x.shape, BF),
            *grads,
            jax.ShapeDtypeStruct((8, ff), F32),
            jax.ShapeDtypeStruct((8, width), F32),
        ],
        scratch_shapes=scratch,
        compiler_params=pltpu.CompilerParams(vmem_limit_bytes=VMEM_LIMIT),
        cost_estimate=pl.CostEstimate(
            flops=mbc * 20 * 10**9, bytes_accessed=mbc * 10 * 10**6, transcendentals=0
        ),
        name="expert_both",
    )(counts, x, weights, b1, b2, *(() if acc is None else acc))


def backward_kernel(
    m0,
    seq_len,
    pad_len,
    has_acc,
    last,
    cnt_ref,
    img_ref,
    cot_ref,
    meta_ref,
    y_ref,
    qkv_ref,
    p_ref,
    att_ref,
    mid_ref,
    rp_ref,
    coef_ref,
    w_ref,
    small_ref,
    extra_ref,
    *rest,
):
    if has_acc:
        accw_ref, accs_ref = rest[:2]
        rest = rest[4:]
    if last:
        out_ref, grad_ref, pack_ref, xs, cs, dq, gw_ref, gs_ref = rest
    else:
        out_ref, grad_ref, gw_ref, gs_ref, xs, cs, dq = rest
    step = pl.program_id(0)
    width = xs.shape[1]
    alive = cnt_ref[0] > 2 * (m0 + step)

    @pl.when(step == 0)
    def _():
        if has_acc:
            gw_ref[...] = accw_ref[...]
            gs_ref[...] = accs_ref[...]
        else:
            gw_ref[...] = jnp.zeros_like(gw_ref)
            gs_ref[...] = jnp.zeros_like(gs_ref)

    @pl.when(jnp.logical_not(alive))
    def _():
        out_ref[...] = jnp.zeros_like(out_ref)
        grad_ref[...] = jnp.zeros_like(grad_ref)

    def add_row(row, value):
        gs_ref[row : row + 1, :] += jnp.sum(value, 0, keepdims=True)

    @pl.when(alive)
    def _():
        load_padded(xs, img_ref, seq_len, pad_len)
        load_padded(cs, cot_ref, seq_len, pad_len)
        rows = xs.shape[0]
        live = meta_ref[0, :, COL_LIVE : COL_LIVE + 1]
        d_final = cs[...] * live
        middle = mid_ref[0]
        rp = rp_ref[0]
        lane = lax.broadcasted_iota(jnp.int32, (1, SMALL), 1)
        lane_f = lane.astype(F32)
        slot = lax.broadcasted_iota(jnp.int32, (1, EXPERTS * CAP), 1).astype(F32)
        res = y_ref[:, 0, 0].reshape(EXPERTS * CAP, width)
        d_rows = y_ref[:, 1, 0].reshape(EXPERTS * CAP, width)
        final = middle
        d_prob = coef_ref[0:1, :] * live
        sel_all = None
        for target, route, kept in ((COL_T0, COL_R0, COL_K0), (COL_T1, COL_R1, COL_K1)):
            sel = jnp.where(slot == meta_ref[0, :, target : target + 1], 1.0, 0.0).astype(BF)
            sel_all = sel if sel_all is None else sel_all + sel
            picked = mm(sel, res)
            keep = meta_ref[0, :, kept : kept + 1]
            hot = lane_f == meta_ref[0, :, route : route + 1]
            gate = jnp.sum(jnp.where(hot, rp, 0.0), -1, keepdims=True) * keep
            final = final + gate * picked
            d_gate = jnp.sum(picked * d_final, -1, keepdims=True) * keep
            d_prob = d_prob + jnp.where(hot, d_gate, 0.0)
        final = final * live
        for i in range(2):
            out_ref[i] = final[i * pad_len : i * pad_len + seq_len, :].astype(BF)
        d_mixed = mm(sel_all, d_rows)
        d_logits = (rp * (d_prob - jnp.sum(rp * d_prob, -1, keepdims=True))).astype(BF)
        d_mixed = d_mixed + mm_nt(d_logits, w_ref[:, 4 * width : 4 * width + SMALL])
        gain2 = small_ref[ROW_GAIN2 : ROW_GAIN2 + 1, :]
        xhat2, inv2 = norm_parts(middle)
        mixed = (xhat2 * gain2 + small_ref[ROW_BIAS2 : ROW_BIAS2 + 1, :]).astype(BF)
        gs_ref[0:EXPERTS, :] += mm_tn(d_logits, mixed)[0:EXPERTS, :]
        add_row(ROW_GAIN2, d_mixed * xhat2)
        add_row(ROW_BIAS2, d_mixed)
        d_middle = d_final + norm_back(d_mixed, xhat2, inv2, gain2)
        add_row(ROW_OBIAS, d_middle)
        cs[...] = d_middle
        d_branch = d_middle.astype(BF)
        gw_ref[:, 3 * width : 4 * width] += mm_tn(att_ref[0], d_branch)
        d_att_all = mm_nt(d_branch, w_ref[:, 3 * width : 4 * width]).astype(BF)
        low, high, low_mask = half_masks()
        scale = HEAD_DIM**-0.5
        for i in range(2):
            span = slice(i * pad_len, (i + 1) * pad_len)
            for hp in range(HEADS // 2):
                at = hp * PAIR
                q = qkv_ref[0, span, at : at + PAIR]
                k = qkv_ref[0, span, width + at : width + at + PAIR]
                v = qkv_ref[0, span, 2 * width + at : 2 * width + at + PAIR]
                d_att = stack_heads(d_att_all[span, at : at + PAIR], low, high)
                p = p_ref[0, i, hp]
                pf = p.astype(F32)
                d_attn = mm_nt(d_att, v)
                d_s = (pf * (d_attn - jnp.sum(pf * d_attn, -1, keepdims=True))).astype(BF)
                d_v = mm_tn(p, d_att)
                d_k = mm_tn(d_s, stack_heads(q, low, high)) * scale
                d_q = mm(d_s, k) * scale
                dq[span, at : at + PAIR] = jnp.where(
                    low_mask, d_q[:pad_len], d_q[pad_len:]
                ).astype(BF)
                dq[span, width + at : width + at + PAIR] = d_k.astype(BF)
                dq[span, 2 * width + at : 2 * width + at + PAIR] = d_v.astype(BF)
        gain1 = small_ref[ROW_GAIN1 : ROW_GAIN1 + 1, :]
        xhat, inv = norm_parts(xs[...])
        normed = (xhat * gain1 + small_ref[ROW_BIAS1 : ROW_BIAS1 + 1, :]).astype(BF)
        add_row(ROW_QBIAS, dq[:, 0:width].astype(F32))
        add_row(ROW_VBIAS, dq[:, 2 * width : 3 * width].astype(F32))
        gw_ref[:, 0 : 3 * width] += mm_tn(normed, dq[...])
        d_normed = mm_nt(dq[...], w_ref[:, 0 : 3 * width])
        add_row(ROW_GAIN1, d_normed * xhat)
        add_row(ROW_BIAS1, d_normed)
        d_tok = cs[...] + norm_back(d_normed, xhat, inv, gain1)
        for i in range(2):
            grad_ref[i] = d_tok[i * pad_len : i * pad_len + seq_len, :].astype(BF)

    if last:

        @pl.when(step == pl.num_programs(0) - 1)
        def _():
            small_part = (gs_ref[...] + extra_ref[...]).T.astype(BF)
            _, blocks, rows_of, wide = pack_ref.shape
            for b in range(blocks):
                for p in range(pack_ref.shape[0]):
                    at = (b * pack_ref.shape[0] + p) * rows_of
                    pack_ref[p, b, :, 0 : 4 * width] = gw_ref[at : at + rows_of, :].astype(BF)
                    pack_ref[p, b, :, 4 * width :] = small_part[at : at + rows_of, :]


def backward_call(
    m0,
    mbc,
    last,
    own_rows,
    images,
    cotangent,
    count,
    meta,
    back,
    saved,
    coef,
    weights,
    small,
    extra,
    acc,
):
    lanes_of = EXPERTS if own_rows == BLOCK else 1
    own_rows = own_rows if own_rows == BLOCK else BLOCK
    seq_len, width = images.shape[1], images.shape[2]
    rows = meta.shape[1]
    pad_len = rows // 2
    mb = images.shape[0] // MICRO
    qkv, probs, att, mid, rp = saved
    at = lambda i: i + m0
    image_block = pl.BlockSpec((mb, seq_len, width), lambda i: (at(i), 0, 0))
    in_specs = [
        pl.BlockSpec(memory_space=pltpu.SMEM),
        image_block,
        image_block,
        pl.BlockSpec((1, rows, 8), lambda i: (at(i), 0, 0)),
        pl.BlockSpec((EXPERTS, 2, 1, CAP, width), lambda i: (0, 0, i, 0, 0)),
        pl.BlockSpec((1, rows, 3 * width), lambda i: (i, 0, 0)),
        pl.BlockSpec((1, 2, HEADS // 2, rows, pad_len), lambda i: (i, 0, 0, 0, 0)),
        pl.BlockSpec((1, rows, width), lambda i: (i, 0, 0)),
        pl.BlockSpec((1, rows, width), lambda i: (i, 0, 0)),
        pl.BlockSpec((1, rows, SMALL), lambda i: (i, 0, 0)),
        full_block(coef.shape),
        full_block(weights.shape),
        full_block(small.shape),
        full_block(extra.shape),
    ]
    args = [count, images, cotangent, meta, back, qkv, probs, att, mid, rp]
    args += [coef, weights, small, extra]
    aliases = {}
    if acc is not None:
        base = len(args)
        in_specs += [full_block(acc[0].shape), full_block(acc[1].shape)]
        in_specs += [pl.BlockSpec(memory_space=pl.ANY)] * 2
        args += list(acc)
        aliases = {base + 2: 0, base + 3: 1}
    sums = [(width, 4 * width), (SMALL, width)]
    pack_shape = (lanes_of, width // (lanes_of * own_rows), own_rows, weights.shape[1])
    if last:
        grads = [jax.ShapeDtypeStruct(pack_shape, BF)]
        held = [pltpu.VMEM(shape, F32) for shape in sums]
    else:
        grads = [jax.ShapeDtypeStruct(shape, F32) for shape in sums]
        held = []
    return pl.pallas_call(
        functools.partial(backward_kernel, m0, seq_len, pad_len, acc is not None, last),
        grid=(mbc,),
        in_specs=in_specs,
        out_specs=[
            image_block,
            image_block,
        ]
        + [full_block(g.shape) for g in grads],
        out_shape=[
            jax.ShapeDtypeStruct(images.shape, BF),
            jax.ShapeDtypeStruct(images.shape, BF),
        ]
        + grads,
        scratch_shapes=[
            pltpu.VMEM((rows, width), F32),
            pltpu.VMEM((rows, width), F32),
            pltpu.VMEM((rows, 3 * width), BF),
        ]
        + held,
        input_output_aliases=aliases,
        compiler_params=pltpu.CompilerParams(vmem_limit_bytes=VMEM_LIMIT),
        cost_estimate=pl.CostEstimate(
            flops=mbc * 20 * 10**9, bytes_accessed=mbc * 10 * 10**6, transcendentals=0
        ),
        name="dense_backward",
    )(*args)


def finish_kernel(
    got_ref,
    bal_ref,
    qkv_ref,
    out_ref,
    router_ref,
    gain1_ref,
    bias1_ref,
    qv_ref,
    obias_ref,
    gain2_ref,
    bias2_ref,
    ein_ref,
    eout_ref,
    balance_ref,
    turned,
):
    planes, rows, wide = got_ref.shape
    width = out_ref.shape[1]
    whole = got_ref[0]
    for z in range(1, planes):
        whole = whole + got_ref[z]
    qkv_ref[...] = whole[:, : 3 * width]
    out_ref[...] = whole[:, 3 * width : 4 * width]
    turned[...] = jnp.zeros_like(turned)
    turned[0:rows, :] = whole[:, 4 * width :]
    balance_ref[...] = jnp.sum(turned[0:1, :] * bal_ref[0:1, :], -1, keepdims=True)
    turned[...] = turned[...].T
    router_ref[...] = turned[0:EXPERTS, 0:rows]
    for row, ref in (
        (ROW_GAIN1, gain1_ref),
        (ROW_BIAS1, bias1_ref),
        (ROW_OBIAS, obias_ref),
        (ROW_GAIN2, gain2_ref),
        (ROW_BIAS2, bias2_ref),
    ):
        ref[...] = turned[row : row + 1, 0:rows]
    qv_ref[...] = turned[ROW_QBIAS : ROW_VBIAS + 1, 0:rows]
    eout_ref[...] = turned[ROW_EOUT : ROW_EOUT + EXPERTS, 0:rows]
    for c in range(ein_ref.shape[1] // rows):
        at = ROW_EIN + c * EXPERTS
        ein_ref[:, c * rows : (c + 1) * rows] = turned[at : at + EXPERTS, 0:rows]


def finish_call(got, bal, width, ff_rows):
    rows = got.shape[1]
    shapes = [
        (rows, 3 * width),
        (rows, width),
        (EXPERTS, rows),
        (1, rows),
        (1, rows),
        (2, rows),
        (1, rows),
        (1, rows),
        (1, rows),
        (EXPERTS, ff_rows),
        (EXPERTS, rows),
        (1, 1),
    ]
    vm = pl.BlockSpec(memory_space=pltpu.VMEM)
    return pl.pallas_call(
        finish_kernel,
        in_specs=[vm] * 2,
        out_specs=[vm] * len(shapes),
        out_shape=[jax.ShapeDtypeStruct(shape, F32) for shape in shapes],
        scratch_shapes=[pltpu.VMEM((SMALL, SMALL), F32)],
        name="finish",
    )(got, bal)


def shards(
    total,
    images,
    image_count,
    expert_index,
    expert_slot,
    keep,
    cotangent,
    ln1_gain,
    ln1_bias,
    qkv_weight,
    qv_bias,
    out_weight,
    out_bias,
    ln2_gain,
    ln2_bias,
    router_weight,
    expert_in,
    expert_in_bias,
    expert_out,
    expert_out_bias,
):
    slots, seq_len, width = images.shape
    planes = total // EXPERTS
    rows = width // total
    ff = expert_in.shape[2]
    ff_rows = ff // total
    mb = slots // MICRO
    pad_len = -(-seq_len // 16) * 16
    plane_groups = [[z * EXPERTS + p for p in range(EXPERTS)] for z in range(planes)]
    z_groups = [[z * EXPERTS + p for z in range(planes)] for p in range(EXPERTS)]

    def plane_swap(v):
        return lax.all_to_all(v, "dp", 0, 0, tiled=True, axis_index_groups=plane_groups)

    def z_swap(v):
        return lax.all_to_all(v, "dp", 0, 0, tiled=True, axis_index_groups=z_groups)

    def z_gather(v):
        return lax.all_gather(v, "dp", axis=0, tiled=True, axis_index_groups=z_groups)

    parts = ff // width
    expert_pack = jnp.concatenate(
        [
            expert_in.reshape(EXPERTS, rows, parts, width)
            .transpose(0, 2, 1, 3)
            .reshape(EXPERTS, ff_rows, width),
            expert_out,
        ],
        1,
    )
    expert_pack = plane_swap(expert_pack)

    live_img = (jnp.arange(slots) < image_count[0]).astype(F32)
    live_tok = jnp.broadcast_to(live_img[:, None, None], (slots, seq_len, 1))
    hits = (expert_index[..., None] == jnp.arange(EXPERTS)).astype(F32) * live_tok[..., None]
    local_counts = jnp.sum(hits, axis=(0, 1, 2))
    high = jnp.floor(local_counts * (1.0 / 128.0))
    told = jnp.concatenate([high, local_counts - 128.0 * high, image_count.astype(F32)]).astype(BF)
    small_cols = jnp.concatenate(
        [
            router_weight,
            ln1_gain[:, None],
            ln1_bias[:, None],
            qv_bias.T,
            out_bias[:, None],
            ln2_gain[:, None],
            ln2_bias[:, None],
            jnp.zeros((rows, 1), BF),
            expert_in_bias.reshape(EXPERTS, parts, rows).transpose(2, 0, 1).reshape(rows, -1),
            expert_out_bias.T,
            jnp.broadcast_to(told[None], (rows, 2 * EXPERTS + 1)),
        ],
        1,
    )
    col_in_bias = 2 * EXPERTS
    col_out_bias = col_in_bias + EXPERTS * parts
    col_counts = col_out_bias + EXPERTS
    col_images = col_counts + 2 * EXPERTS
    small_cols = jnp.pad(small_cols, ((0, 0), (0, SMALL - small_cols.shape[1])))
    packed = jnp.concatenate([qkv_weight, out_weight, small_cols], 1)
    wide = packed.shape[1]
    packed = z_gather(packed)
    packed = plane_swap(jnp.broadcast_to(packed[None], (EXPERTS,) + packed.shape))
    weights = (
        packed.reshape(EXPERTS, planes, rows, wide).transpose(1, 0, 2, 3).reshape(width, wide)
    )
    small = weights[:, 4 * width :].astype(F32).T

    target = jnp.where(keep == 1, expert_index * CAP + expert_slot, -1).astype(F32)
    meta = jnp.concatenate(
        [
            target,
            expert_index.astype(F32),
            keep.astype(F32),
            live_tok,
            jnp.zeros((slots, seq_len, 1), F32),
        ],
        -1,
    )
    fill = jnp.array([-1.0, -1.0, 0.0, 0.0, 0.0, 0.0, 0.0, 0.0], F32)
    meta = jnp.concatenate(
        [meta, jnp.broadcast_to(fill, (slots, pad_len - seq_len, 8))], 1
    ).reshape(MICRO, mb * pad_len, 8)
    lane_t = meta.transpose(0, 2, 1)

    me = lax.axis_index("dp")
    in_bias = lax.dynamic_slice_in_dim(small, col_in_bias + parts * (me % EXPERTS), parts, 0)
    in_bias = in_bias.reshape(parts, total, rows).transpose(1, 0, 2).reshape(1, ff)
    out_bias_e = lax.dynamic_slice_in_dim(small, col_out_bias + me % EXPERTS, 1, 0)
    sums = jnp.sum(small[col_counts : col_images + 1], 1) * (1.0 / rows)
    counts_all = sums[:EXPERTS] * 128.0 + sums[EXPERTS : 2 * EXPERTS]
    live_total = sums[2 * EXPERTS] * float(seq_len)
    plane_counts = lax.dynamic_slice_in_dim(
        small[col_images], (me // EXPERTS) * (EXPERTS * rows), EXPERTS * rows, 0
    )
    plane_counts = plane_counts.reshape(EXPERTS, rows)[:, 0].astype(jnp.int32)
    coef = jnp.pad(BALANCE_WEIGHT * EXPERTS * counts_all / live_total, (0, SMALL - EXPERTS))
    coef = jnp.broadcast_to(coef[None], (8, SMALL))
    in_bias = jnp.broadcast_to(in_bias, (8, ff))
    out_bias_e = jnp.broadcast_to(out_bias_e, (8, width))

    expert_pack = z_gather(expert_pack)
    if rows != BLOCK:
        blocks = width // BLOCK
        expert_pack = jnp.concatenate(
            [
                expert_pack[:, :ff_rows]
                .reshape(blocks, total // blocks, parts, rows, width)
                .transpose(0, 2, 1, 3, 4)
                .reshape(blocks, parts * BLOCK, width),
                expert_pack[:, ff_rows:].reshape(blocks, parts * BLOCK, width),
            ],
            1,
        )

    spans = []
    for size in CHUNKS:
        spans.append((sum(span[1] for span in spans), size))
    saved, sent, prob_sums = [], [], []
    for m0, mbc in spans:
        xd, qkv, probs, att, mid, rp, prob = forward_call(
            m0, mbc, images, cotangent, image_count, lane_t, meta, weights, small
        )
        saved.append((qkv, probs, att, mid, rp))
        prob_sums.append(prob[0, :EXPERTS])
        sent.append(plane_swap(xd))
    acc = None
    back = []
    for (m0, mbc), rows_in in zip(spans, sent):
        y, *acc = expert_call(
            m0,
            mbc,
            m0 + mbc == MICRO,
            plane_counts,
            rows_in,
            expert_pack,
            in_bias,
            out_bias_e,
            acc,
        )
        back.append(plane_swap(y))
    expert_grads, gb1, gb2 = acc

    if rows != BLOCK:
        expert_grads = jnp.concatenate(
            [
                expert_grads[:, : parts * BLOCK]
                .reshape(blocks, parts, total // blocks, rows, width)
                .transpose(0, 2, 1, 3, 4)
                .reshape(total, ff_rows, width),
                expert_grads[:, parts * BLOCK :].reshape(total, ff_rows, width),
            ],
            1,
        )
    expert_grads = lax.psum_scatter(
        expert_grads, "dp", scatter_dimension=0, tiled=True, axis_index_groups=z_groups
    )
    expert_grads = plane_swap(expert_grads).astype(F32)
    expert_in_grad = (
        expert_grads[:, :ff_rows]
        .reshape(EXPERTS, parts, rows, width)
        .transpose(0, 2, 1, 3)
        .reshape(EXPERTS, rows, ff)
    )
    expert_out_grad = expert_grads[:, ff_rows:]

    prob_sum = prob_sums[0]
    for piece in prob_sums[1:]:
        prob_sum = prob_sum + piece
    p_hi = prob_sum.astype(BF).astype(F32)
    mine = (jnp.arange(EXPERTS) == me % EXPERTS).astype(F32)
    e_in = gb1[0].reshape(total, parts, rows).transpose(1, 0, 2).reshape(parts, 1, width)
    extra = jnp.concatenate(
        [
            jnp.zeros((ROW_PROB, width), F32),
            jnp.broadcast_to(
                jnp.concatenate([p_hi, prob_sum - p_hi])[:, None], (2 * EXPERTS, width)
            ),
            mine[:, None] * gb2[0:1],
            (mine[None, :, None] * e_in).reshape(parts * EXPERTS, width),
            jnp.zeros((SMALL - ROW_EIN - parts * EXPERTS, width), F32),
        ],
        0,
    )

    acc = None
    for (m0, mbc), returned, kept in zip(spans, back, saved):
        block_out, image_grad, *acc = backward_call(
            m0,
            mbc,
            m0 + mbc == MICRO,
            rows,
            images,
            cotangent,
            image_count,
            meta,
            returned,
            kept,
            coef,
            weights,
            small,
            extra,
            None if acc is None else (*acc, block_out, image_grad),
        )

    grads = acc[0]
    if rows != BLOCK:
        grads = grads.reshape(planes, EXPERTS, rows, wide).transpose(1, 0, 2, 3)
    grads = plane_swap(grads.reshape(EXPERTS, planes * rows, wide))
    grads = lax.psum_scatter(
        jnp.sum(grads.astype(F32), 0),
        "dp",
        scatter_dimension=0,
        tiled=True,
        axis_index_groups=z_groups,
    )
    bal = EXPERTS * counts_all / live_total / live_total
    bal = jnp.concatenate([jnp.zeros((ROW_PROB,), F32), bal, bal])
    bal = jnp.broadcast_to(jnp.pad(bal, (0, SMALL - bal.shape[0]))[None], (8, SMALL))
    (
        qkv_grad,
        out_grad,
        router_grad,
        gain1_grad,
        bias1_grad,
        qv_grad,
        obias_grad,
        gain2_grad,
        bias2_grad,
        ein_grad,
        eout_grad,
        balance,
    ) = finish_call(grads[None], bal, width, ff_rows)
    return (
        block_out,
        image_grad,
        balance.reshape(()),
        gain1_grad.reshape(rows),
        bias1_grad.reshape(rows),
        qkv_grad,
        qv_grad,
        out_grad,
        obias_grad.reshape(rows),
        gain2_grad.reshape(rows),
        bias2_grad.reshape(rows),
        router_grad.T,
        expert_in_grad,
        ein_grad,
        expert_out_grad,
        eout_grad,
    )


def solution(mesh):
    placed = (
        P("dp", None, None),
        P("dp"),
        P("dp", None, None),
        P("dp", None, None),
        P("dp", None, None),
        P("dp", None, None),
        P("dp"),
        P("dp"),
        P("dp", None),
        P(None, "dp"),
        P("dp", None),
        P("dp"),
        P("dp"),
        P("dp"),
        P("dp", None),
        P(None, "dp", None),
        P(None, "dp"),
        P(None, "dp", None),
        P(None, "dp"),
    )
    return jax.shard_map(
        functools.partial(shards, mesh.shape["dp"]),
        mesh=mesh,
        in_specs=placed,
        out_specs=(
            P("dp", None, None),
            P("dp", None, None),
            P(),
            P("dp"),
            P("dp"),
            P("dp", None),
            P(None, "dp"),
            P("dp", None),
            P("dp"),
            P("dp"),
            P("dp"),
            P("dp", None),
            P(None, "dp", None),
            P(None, "dp"),
            P(None, "dp", None),
            P(None, "dp"),
        ),
        check_vma=False,
    )
```

```python
import functools
import math

import jax
import jax.numpy as jnp
from jax import lax
from jax.experimental import pallas as pl
from jax.experimental.pallas import tpu as pltpu
from jax.sharding import PartitionSpec as P

HEADS = 8
HEAD_DIM = 64
EXPERTS = 8
MICRO = 4
CAP = 128
CHUNKS = (2, 2)
PAIR = 2 * HEAD_DIM

EPSILON = 1e-06
BALANCE_WEIGHT = 8.0

BF = jnp.bfloat16
F32 = jnp.float32

ROW_GAIN1, ROW_BIAS1, ROW_QBIAS, ROW_VBIAS, ROW_OBIAS, ROW_GAIN2, ROW_BIAS2 = range(8, 15)
SMALL = 128
ROW_PROB, ROW_EOUT, ROW_EIN = 16, 32, 40
AT_EIN, AT_EOUT, AT_HIGH, AT_LOW, AT_IMAGES = 16, 48, 56, 64, 72
CORES = 2
CHIPS = EXPERTS // CORES
BLOCK = 16
COL_T0, COL_T1, COL_R0, COL_R1, COL_K0, COL_K1, COL_LIVE = range(7)
VMEM_LIMIT = 60 * 1024 * 1024


def mm(a, b):
    return lax.dot_general(a, b, (((1,), (0,)), ((), ())), preferred_element_type=F32)


def mm_nt(a, b):
    return lax.dot_general(a, b, (((1,), (1,)), ((), ())), preferred_element_type=F32)


def mm_tn(a, b):
    return lax.dot_general(a, b, (((0,), (0,)), ((), ())), preferred_element_type=F32)


def load_padded(dst, src, seq_len, pad_len):
    for i in range(2):
        tail = (seq_len // 16) * 16
        dst[i * pad_len + tail : (i + 1) * pad_len, :] = jnp.zeros(
            (pad_len - tail, dst.shape[1]), dst.dtype
        )
        dst[i * pad_len : i * pad_len + seq_len, :] = src[i].astype(dst.dtype)


def norm_parts(x):
    mean = jnp.mean(x, -1, keepdims=True)
    centered = x - mean
    spread = jnp.mean(centered * centered, -1, keepdims=True)
    inv = lax.rsqrt(spread + EPSILON)
    return centered * inv, inv


def norm_back(d_out, xhat, inv, gain):
    d_hat = d_out * gain
    first = jnp.mean(d_hat, -1, keepdims=True)
    second = jnp.mean(d_hat * xhat, -1, keepdims=True)
    return inv * (d_hat - first - xhat * second)


def half_masks():
    lane = lax.broadcasted_iota(jnp.int32, (1, PAIR), 1)
    low = jnp.where(lane < HEAD_DIM, 1.0, 0.0)
    return low.astype(BF), (1.0 - low).astype(BF), lane < HEAD_DIM


def stack_heads(block, low, high):
    return jnp.concatenate([block * low, block * high], 0)


def forward_kernel(
    m0,
    seq_len,
    pad_len,
    assemble,
    cnt_ref,
    img_ref,
    cot_ref,
    lane_ref,
    meta_ref,
    first_ref,
    second_ref,
    xd_ref,
    qkv_ref,
    p_ref,
    att_ref,
    mid_ref,
    rp_ref,
    psum_ref,
    *rest,
):
    if assemble:
        w_ref, small_ref, xs, cs = rest
    else:
        w_ref, small_ref = first_ref, second_ref
        xs, cs = rest
    step = pl.program_id(0)
    width = xs.shape[1]
    alive = cnt_ref[0] > 2 * (m0 + step)

    @pl.when(step == 0)
    def _():
        psum_ref[...] = jnp.zeros_like(psum_ref)
        if assemble:
            core = lax.rem(cnt_ref[1], CORES)
            for ref, owner in ((first_ref, core), (second_ref, 1 - core)):
                for chip in range(CHIPS):
                    for z in range(ref.shape[1] // BLOCK):
                        at = pl.multiple_of((z * EXPERTS + chip * CORES + owner) * BLOCK, BLOCK)
                        w_ref[pl.ds(at, BLOCK), :] = ref[chip, z * BLOCK : (z + 1) * BLOCK, :]
            small_ref[...] = w_ref[:, 4 * width :].astype(F32).T

    @pl.when(jnp.logical_not(alive))
    def _():
        xd_ref[...] = jnp.zeros_like(xd_ref)

    @pl.when(alive)
    def _():
        load_padded(xs, img_ref, seq_len, pad_len)
        load_padded(cs, cot_ref, seq_len, pad_len)
        xhat, inv = norm_parts(xs[...])
        normed = (
            xhat * small_ref[ROW_GAIN1 : ROW_GAIN1 + 1, :] + small_ref[ROW_BIAS1 : ROW_BIAS1 + 1, :]
        ).astype(BF)
        for part, row in ((0, ROW_QBIAS), (1, None), (2, ROW_VBIAS)):
            cols = slice(part * width, (part + 1) * width)
            value = mm(normed, w_ref[:, cols])
            if row is not None:
                value = value + small_ref[row : row + 1, :]
            qkv_ref[0, :, cols] = value.astype(BF)
        low, high, low_mask = half_masks()
        key_ok = lax.broadcasted_iota(jnp.int32, (1, pad_len), 1) < seq_len
        for i in range(2):
            rows = slice(i * pad_len, (i + 1) * pad_len)
            for hp in range(HEADS // 2):
                at = hp * PAIR
                q = qkv_ref[0, rows, at : at + PAIR]
                k = qkv_ref[0, rows, width + at : width + at + PAIR]
                v = qkv_ref[0, rows, 2 * width + at : 2 * width + at + PAIR]
                s = mm_nt(stack_heads(q, low, high), k) * (HEAD_DIM**-0.5)
                s = jnp.where(key_ok, s, -1e30)
                e = jnp.exp(s - jnp.max(s, -1, keepdims=True))
                p = (e * (1.0 / jnp.sum(e, -1, keepdims=True))).astype(BF)
                p_ref[0, i, hp] = p
                o = mm(p, v)
                att_ref[0, rows, at : at + PAIR] = jnp.where(
                    low_mask, o[:pad_len], o[pad_len:]
                ).astype(BF)
        middle = (
            xs[...]
            + mm(att_ref[0], w_ref[:, 3 * width : 4 * width])
            + small_ref[ROW_OBIAS : ROW_OBIAS + 1, :]
        )
        mid_ref[0] = middle
        xhat2, inv2 = norm_parts(middle)
        mixed = (
            xhat2 * small_ref[ROW_GAIN2 : ROW_GAIN2 + 1, :]
            + small_ref[ROW_BIAS2 : ROW_BIAS2 + 1, :]
        ).astype(BF)
        logits = mm(mixed, w_ref[:, 4 * width : 4 * width + SMALL])
        lane = lax.broadcasted_iota(jnp.int32, (1, SMALL), 1)
        logits = jnp.where(lane < EXPERTS, logits, -1e30)
        e = jnp.exp(logits - jnp.max(logits, -1, keepdims=True))
        rp = e * (1.0 / jnp.sum(e, -1, keepdims=True))
        rp_ref[0] = rp
        live = meta_ref[0, :, COL_LIVE : COL_LIVE + 1]
        psum_ref[0:1, :] += jnp.sum(rp * live, 0, keepdims=True)
        d_final = cs[...] * live
        lane_f = lane.astype(F32)
        weighted = []
        for route, kept in ((COL_R0, COL_K0), (COL_R1, COL_K1)):
            hot = lane_f == meta_ref[0, :, route : route + 1]
            gate = jnp.sum(jnp.where(hot, rp, 0.0), -1, keepdims=True)
            gate = gate * meta_ref[0, :, kept : kept + 1]
            weighted.append((gate * d_final).astype(BF))
        slot = lax.broadcasted_iota(jnp.int32, (CAP, 1), 0).astype(F32)
        for e_id in range(EXPERTS):
            here = slot + float(e_id * CAP)
            sel0 = jnp.where(here == lane_ref[0, 0:1, :], 1.0, 0.0)
            sel1 = jnp.where(here == lane_ref[0, 1:2, :], 1.0, 0.0)
            xd_ref[e_id, 0, 0] = mm((sel0 + sel1).astype(BF), mixed).astype(BF)
            xd_ref[e_id, 1, 0] = (
                mm(sel0.astype(BF), weighted[0]) + mm(sel1.astype(BF), weighted[1])
            ).astype(BF)


def full_block(shape):
    return pl.BlockSpec(shape, lambda i: (0,) * len(shape))


def pack_kernel(in_ref, out_ref, pack_ref):
    width = out_ref.shape[2]
    half = out_ref.shape[1]
    for c in range(half // BLOCK):
        pack_ref[:, c * BLOCK : (c + 1) * BLOCK, :] = in_ref[:, :, c * width : (c + 1) * width]
    pack_ref[:, half:, :] = out_ref[...]


def pack_call(expert_in, expert_out):
    vm = pl.BlockSpec(memory_space=pltpu.VMEM)
    shape = (expert_out.shape[0], 2 * expert_out.shape[1], expert_out.shape[2])
    return pl.pallas_call(
        pack_kernel,
        in_specs=[vm] * 2,
        out_specs=vm,
        out_shape=jax.ShapeDtypeStruct(shape, BF),
        name="pack",
    )(expert_in, expert_out)


def prepare_kernel(
    cnt_ref,
    index_ref,
    qkv_ref,
    out_ref,
    router_ref,
    gain1_ref,
    bias1_ref,
    qv_ref,
    obias_ref,
    gain2_ref,
    bias2_ref,
    ein_ref,
    eout_ref,
    packed_ref,
    turned,
):
    rows, width = out_ref.shape
    packed_ref[:, 0 : 3 * width] = qkv_ref[...]
    packed_ref[:, 3 * width : 4 * width] = out_ref[...]
    turned[...] = jnp.zeros_like(turned)
    turned[0:EXPERTS, 0:rows] = router_ref[...].astype(F32)
    for row, ref in (
        (ROW_GAIN1, gain1_ref),
        (ROW_BIAS1, bias1_ref),
        (ROW_OBIAS, obias_ref),
        (ROW_GAIN2, gain2_ref),
        (ROW_BIAS2, bias2_ref),
    ):
        turned[row : row + 1, 0:rows] = ref[...].astype(F32)
    turned[ROW_QBIAS : ROW_VBIAS + 1, 0:rows] = qv_ref[...].astype(F32)
    turned[AT_EOUT : AT_EOUT + EXPERTS, 0:rows] = eout_ref[...].astype(F32)
    ein = ein_ref[...].astype(F32)
    for c in range(ein.shape[1] // rows):
        at = AT_EIN + c * EXPERTS
        turned[at : at + EXPERTS, 0:rows] = ein[:, c * rows : (c + 1) * rows]
    slots, top, seq_len = index_ref.shape
    chosen = index_ref[...]
    slot = lax.broadcasted_iota(jnp.int32, (slots, top, seq_len), 0)
    chosen = jnp.where(slot < cnt_ref[0], chosen, -1)
    for e in range(EXPERTS):
        hits = jnp.where(chosen == e, 1.0, 0.0)
        hits = jnp.sum(jnp.sum(hits, 0), -1, keepdims=True)
        hits = jnp.sum(hits, 0, keepdims=True)
        high = jnp.floor(hits * (1.0 / 128.0))
        turned[AT_HIGH + e : AT_HIGH + e + 1, :] = jnp.broadcast_to(high, (1, SMALL))
        turned[AT_LOW + e : AT_LOW + e + 1, :] = jnp.broadcast_to(hits - 128.0 * high, (1, SMALL))
    turned[AT_IMAGES : AT_IMAGES + 1, :] = jnp.full((1, SMALL), cnt_ref[0].astype(F32))
    turned[...] = turned[...].T
    packed_ref[:, 4 * width :] = turned[0:rows, :].astype(BF)


def prepare_call(count, *args):
    vm = pl.BlockSpec(memory_space=pltpu.VMEM)
    rows, width = args[2].shape
    return pl.pallas_call(
        prepare_kernel,
        in_specs=[pl.BlockSpec(memory_space=pltpu.SMEM)] + [vm] * len(args),
        out_specs=vm,
        out_shape=jax.ShapeDtypeStruct((rows, 4 * width + SMALL), BF),
        scratch_shapes=[pltpu.VMEM((SMALL, SMALL), F32)],
        name="prepare",
    )(count, *args)


def forward_call(m0, mbc, assemble, images, cotangent, count, lane_t, meta, weights, small):
    seq_len, width = images.shape[1], images.shape[2]
    rows = meta.shape[1]
    pad_len = rows // 2
    at = lambda i: i + m0
    mb = images.shape[0] // MICRO
    made_here = []
    if assemble:
        made_here = [
            jax.ShapeDtypeStruct((width, weights.shape[2]), BF),
            jax.ShapeDtypeStruct((SMALL, width), F32),
        ]
    return pl.pallas_call(
        functools.partial(forward_kernel, m0, seq_len, pad_len, assemble),
        grid=(mbc,),
        in_specs=[
            pl.BlockSpec(memory_space=pltpu.SMEM),
            pl.BlockSpec((mb, seq_len, width), lambda i: (at(i), 0, 0)),
            pl.BlockSpec((mb, seq_len, width), lambda i: (at(i), 0, 0)),
            pl.BlockSpec((1, 8, rows), lambda i: (at(i), 0, 0)),
            pl.BlockSpec((1, rows, 8), lambda i: (at(i), 0, 0)),
            full_block(weights.shape),
            full_block(small.shape),
        ],
        out_specs=[
            pl.BlockSpec((EXPERTS, 2, 1, CAP, width), lambda i: (0, 0, i, 0, 0)),
            pl.BlockSpec((1, rows, 3 * width), lambda i: (i, 0, 0)),
            pl.BlockSpec((1, 2, HEADS // 2, rows, pad_len), lambda i: (i, 0, 0, 0, 0)),
            pl.BlockSpec((1, rows, width), lambda i: (i, 0, 0)),
            pl.BlockSpec((1, rows, width), lambda i: (i, 0, 0)),
            pl.BlockSpec((1, rows, SMALL), lambda i: (i, 0, 0)),
            full_block((8, SMALL)),
        ]
        + [full_block(made.shape) for made in made_here],
        out_shape=[
            jax.ShapeDtypeStruct((EXPERTS, 2, mbc, CAP, width), BF),
            jax.ShapeDtypeStruct((mbc, rows, 3 * width), BF),
            jax.ShapeDtypeStruct((mbc, 2, HEADS // 2, rows, pad_len), BF),
            jax.ShapeDtypeStruct((mbc, rows, width), BF),
            jax.ShapeDtypeStruct((mbc, rows, width), F32),
            jax.ShapeDtypeStruct((mbc, rows, SMALL), F32),
            jax.ShapeDtypeStruct((8, SMALL), F32),
        ]
        + made_here,
        scratch_shapes=[pltpu.VMEM((rows, width), F32), pltpu.VMEM((rows, width), F32)],
        compiler_params=pltpu.CompilerParams(vmem_limit_bytes=VMEM_LIMIT),
        cost_estimate=pl.CostEstimate(
            flops=mbc * 12 * 10**9, bytes_accessed=mbc * 10 * 10**6, transcendentals=0
        ),
        name="dense_forward",
    )(count, images, cotangent, lane_t, meta, weights, small)


GROUP = 4


def expert_kernel(
    m0,
    mbc,
    has_acc,
    last,
    cnt_ref,
    x_ref,
    w_ref,
    b1_ref,
    b2_ref,
    *rest,
):
    if has_acc:
        a1_ref, a2_ref, ab1_ref, ab2_ref = rest[:4]
        rest = rest[4:]
    if last:
        y_ref, pack_ref, gb1_ref, gb2_ref, s1, s2, order, xin, din, xout, dout = rest
    else:
        y_ref, s1, s2, gb1_ref, gb2_ref, order, xin, din, xout, dout = rest
    width = x_ref.shape[-1]
    ff = b1_ref.shape[1]
    half = w_ref.shape[1] // 2
    per_tile = width // half
    if has_acc:
        s1[...] = a1_ref[...]
        s2[...] = a2_ref[...]
        gb1_ref[...] = ab1_ref[...]
        gb2_ref[...] = ab2_ref[...]
    else:
        s1[...] = jnp.zeros_like(s1)
        s2[...] = jnp.zeros_like(s2)
        gb1_ref[...] = jnp.zeros_like(gb1_ref)
        gb2_ref[...] = jnp.zeros_like(gb2_ref)
    blocks = EXPERTS * mbc

    def is_live(b):
        return (cnt_ref[b // mbc] > 2 * (m0 + b % mbc)).astype(jnp.int32)

    live_total = jnp.int32(0)
    for b in range(blocks):
        live_total = live_total + is_live(b)
    head, tail = jnp.int32(0), live_total
    for b in range(blocks):
        flag = is_live(b)
        order[jnp.where(flag == 1, head, tail)] = b
        head = head + flag
        tail = tail + (1 - flag)

    def one_group(g, carry):
        for j in range(GROUP):
            b = order[g * GROUP + j]
            xin[j * CAP : (j + 1) * CAP, :] = x_ref[b // mbc, 0, b % mbc]
            din[j * CAP : (j + 1) * CAP, :] = x_ref[b // mbc, 1, b % mbc]
        rows_in, d_res = xin[...], din[...]
        gb2_ref[0:1, :] += jnp.sum(d_res.astype(F32), 0, keepdims=True)
        for f in range(ff // width):
            cols = slice(f * width, (f + 1) * width)
            w1 = w_ref[:, f * BLOCK : (f + 1) * BLOCK, :].reshape(width, width)
            w2 = w_ref[f * per_tile : (f + 1) * per_tile, half:, :].reshape(width, width)
            h = mm(rows_in, w1) + b1_ref[0:1, cols]
            bell = jnp.exp(-0.5 * h * h)
            t = 1.0 / (1.0 + (0.3275911 / math.sqrt(2.0)) * jnp.abs(h))
            poly = t * (
                0.5 * 0.254829592
                + t
                * (
                    0.5 * -0.284496736
                    + t * (0.5 * 1.421413741 + t * (0.5 * -1.453152027 + t * (0.5 * 1.061405429)))
                )
            )
            upper = poly * bell
            cdf = jnp.where(h < 0.0, upper, 1.0 - upper)
            act = (h * cdf).astype(BF)
            slope = cdf + h * bell * (1.0 / math.sqrt(2.0 * math.pi))
            d_act = mm_nt(d_res, w2)
            d_hid_f = (d_act * slope).astype(BF)
            gb1_ref[0:1, cols] += jnp.sum(d_hid_f.astype(F32), 0, keepdims=True)
            res = mm(act, w2)
            d_rows = mm_nt(d_hid_f, w1)
            if f == 0:
                xout[...] = res
                dout[...] = d_rows
            else:
                xout[...] += res
                dout[...] += d_rows
            s1[:, cols] += mm_tn(rows_in, d_hid_f)
            s2[cols, :] += mm_tn(act, d_res)
        for j in range(GROUP):
            b = order[g * GROUP + j]
            y_ref[b // mbc, 0, b % mbc] = (
                xout[j * CAP : (j + 1) * CAP, :] + b2_ref[0:1, :]
            ).astype(BF)
            y_ref[b // mbc, 1, b % mbc] = dout[j * CAP : (j + 1) * CAP, :].astype(BF)
        return carry

    lax.fori_loop(0, (live_total + GROUP - 1) // GROUP, one_group, 0)
    if last:
        blocks_of = width // BLOCK
        for f in range(ff // width):
            tile = s1[:, f * width : (f + 1) * width].astype(BF)
            pack_ref[:, f * BLOCK : (f + 1) * BLOCK, :] = tile.reshape(blocks_of, BLOCK, width)
        pack_ref[:, half:, :] = s2[...].astype(BF).reshape(blocks_of, half, width)


def expert_call(m0, mbc, last, counts, x, weights, b1, b2, acc):
    width, ff = weights.shape[2], b1.shape[1]
    if last:
        grads = [jax.ShapeDtypeStruct(weights.shape, BF)]
    else:
        grads = [jax.ShapeDtypeStruct((width, ff), F32), jax.ShapeDtypeStruct((ff, width), F32)]
    vm = pl.BlockSpec(memory_space=pltpu.VMEM)
    scratch = []
    if last:
        scratch += [pltpu.VMEM((width, ff), F32), pltpu.VMEM((ff, width), F32)]
    scratch += [
        pltpu.SMEM((EXPERTS * mbc,), jnp.int32),
        pltpu.VMEM((GROUP * CAP, width), BF),
        pltpu.VMEM((GROUP * CAP, width), BF),
        pltpu.VMEM((GROUP * CAP, width), F32),
        pltpu.VMEM((GROUP * CAP, width), F32),
    ]
    return pl.pallas_call(
        functools.partial(expert_kernel, m0, mbc, acc is not None, last),
        in_specs=[pl.BlockSpec(memory_space=pltpu.SMEM)] + [vm] * (4 + (0 if acc is None else 4)),
        out_specs=[vm] * (len(grads) + 3),
        out_shape=[
            jax.ShapeDtypeStruct(x.shape, BF),
            *grads,
            jax.ShapeDtypeStruct((8, ff), F32),
            jax.ShapeDtypeStruct((8, width), F32),
        ],
        scratch_shapes=scratch,
        compiler_params=pltpu.CompilerParams(vmem_limit_bytes=VMEM_LIMIT),
        cost_estimate=pl.CostEstimate(
            flops=mbc * 20 * 10**9, bytes_accessed=mbc * 10 * 10**6, transcendentals=0
        ),
        name="expert_both",
    )(counts, x, weights, b1, b2, *(() if acc is None else acc))


def backward_kernel(
    m0,
    seq_len,
    pad_len,
    has_acc,
    last,
    cnt_ref,
    img_ref,
    cot_ref,
    meta_ref,
    y_ref,
    qkv_ref,
    p_ref,
    att_ref,
    mid_ref,
    rp_ref,
    coef_ref,
    w_ref,
    small_ref,
    extra_ref,
    *rest,
):
    if has_acc:
        accw_ref, accs_ref = rest[:2]
        rest = rest[4:]
    if last:
        out_ref, grad_ref, pack_ref, xs, cs, dq, gw_ref, gs_ref = rest
    else:
        out_ref, grad_ref, gw_ref, gs_ref, xs, cs, dq = rest
    step = pl.program_id(0)
    width = xs.shape[1]
    alive = cnt_ref[0] > 2 * (m0 + step)

    @pl.when(step == 0)
    def _():
        if has_acc:
            gw_ref[...] = accw_ref[...]
            gs_ref[...] = accs_ref[...]
        else:
            gw_ref[...] = jnp.zeros_like(gw_ref)
            gs_ref[...] = jnp.zeros_like(gs_ref)

    @pl.when(jnp.logical_not(alive))
    def _():
        out_ref[...] = jnp.zeros_like(out_ref)
        grad_ref[...] = jnp.zeros_like(grad_ref)

    def add_row(row, value):
        gs_ref[row : row + 1, :] += jnp.sum(value, 0, keepdims=True)

    @pl.when(alive)
    def _():
        load_padded(xs, img_ref, seq_len, pad_len)
        load_padded(cs, cot_ref, seq_len, pad_len)
        rows = xs.shape[0]
        live = meta_ref[0, :, COL_LIVE : COL_LIVE + 1]
        d_final = cs[...] * live
        middle = mid_ref[0]
        rp = rp_ref[0]
        lane = lax.broadcasted_iota(jnp.int32, (1, SMALL), 1)
        lane_f = lane.astype(F32)
        slot = lax.broadcasted_iota(jnp.int32, (1, EXPERTS * CAP), 1).astype(F32)
        res = y_ref[:, 0, 0].reshape(EXPERTS * CAP, width)
        d_rows = y_ref[:, 1, 0].reshape(EXPERTS * CAP, width)
        final = middle
        d_prob = coef_ref[0:1, :] * live
        sel_all = None
        for target, route, kept in ((COL_T0, COL_R0, COL_K0), (COL_T1, COL_R1, COL_K1)):
            sel = jnp.where(slot == meta_ref[0, :, target : target + 1], 1.0, 0.0).astype(BF)
            sel_all = sel if sel_all is None else sel_all + sel
            picked = mm(sel, res)
            keep = meta_ref[0, :, kept : kept + 1]
            hot = lane_f == meta_ref[0, :, route : route + 1]
            gate = jnp.sum(jnp.where(hot, rp, 0.0), -1, keepdims=True) * keep
            final = final + gate * picked
            d_gate = jnp.sum(picked * d_final, -1, keepdims=True) * keep
            d_prob = d_prob + jnp.where(hot, d_gate, 0.0)
        final = final * live
        for i in range(2):
            out_ref[i] = final[i * pad_len : i * pad_len + seq_len, :].astype(BF)
        d_mixed = mm(sel_all, d_rows)
        d_logits = (rp * (d_prob - jnp.sum(rp * d_prob, -1, keepdims=True))).astype(BF)
        d_mixed = d_mixed + mm_nt(d_logits, w_ref[:, 4 * width : 4 * width + SMALL])
        gain2 = small_ref[ROW_GAIN2 : ROW_GAIN2 + 1, :]
        xhat2, inv2 = norm_parts(middle)
        mixed = (xhat2 * gain2 + small_ref[ROW_BIAS2 : ROW_BIAS2 + 1, :]).astype(BF)
        gs_ref[0:EXPERTS, :] += mm_tn(d_logits, mixed)[0:EXPERTS, :]
        add_row(ROW_GAIN2, d_mixed * xhat2)
        add_row(ROW_BIAS2, d_mixed)
        d_middle = d_final + norm_back(d_mixed, xhat2, inv2, gain2)
        add_row(ROW_OBIAS, d_middle)
        cs[...] = d_middle
        d_branch = d_middle.astype(BF)
        gw_ref[:, 3 * width : 4 * width] += mm_tn(att_ref[0], d_branch)
        d_att_all = mm_nt(d_branch, w_ref[:, 3 * width : 4 * width]).astype(BF)
        low, high, low_mask = half_masks()
        scale = HEAD_DIM**-0.5
        for i in range(2):
            span = slice(i * pad_len, (i + 1) * pad_len)
            for hp in range(HEADS // 2):
                at = hp * PAIR
                q = qkv_ref[0, span, at : at + PAIR]
                k = qkv_ref[0, span, width + at : width + at + PAIR]
                v = qkv_ref[0, span, 2 * width + at : 2 * width + at + PAIR]
                d_att = stack_heads(d_att_all[span, at : at + PAIR], low, high)
                p = p_ref[0, i, hp]
                pf = p.astype(F32)
                d_attn = mm_nt(d_att, v)
                d_s = (pf * (d_attn - jnp.sum(pf * d_attn, -1, keepdims=True))).astype(BF)
                d_v = mm_tn(p, d_att)
                d_k = mm_tn(d_s, stack_heads(q, low, high)) * scale
                d_q = mm(d_s, k) * scale
                dq[span, at : at + PAIR] = jnp.where(
                    low_mask, d_q[:pad_len], d_q[pad_len:]
                ).astype(BF)
                dq[span, width + at : width + at + PAIR] = d_k.astype(BF)
                dq[span, 2 * width + at : 2 * width + at + PAIR] = d_v.astype(BF)
        gain1 = small_ref[ROW_GAIN1 : ROW_GAIN1 + 1, :]
        xhat, inv = norm_parts(xs[...])
        normed = (xhat * gain1 + small_ref[ROW_BIAS1 : ROW_BIAS1 + 1, :]).astype(BF)
        add_row(ROW_QBIAS, dq[:, 0:width].astype(F32))
        add_row(ROW_VBIAS, dq[:, 2 * width : 3 * width].astype(F32))
        gw_ref[:, 0 : 3 * width] += mm_tn(normed, dq[...])
        d_normed = mm_nt(dq[...], w_ref[:, 0 : 3 * width])
        add_row(ROW_GAIN1, d_normed * xhat)
        add_row(ROW_BIAS1, d_normed)
        d_tok = cs[...] + norm_back(d_normed, xhat, inv, gain1)
        for i in range(2):
            grad_ref[i] = d_tok[i * pad_len : i * pad_len + seq_len, :].astype(BF)

    if last:

        @pl.when(step == pl.num_programs(0) - 1)
        def _():
            small_part = (gs_ref[...] + extra_ref[...]).T.astype(BF)
            for b in range(width // BLOCK):
                at = slice(b * BLOCK, (b + 1) * BLOCK)
                core = b % CORES
                if len(pack_ref.shape) == 4:
                    ref = pack_ref.at[core, b // CORES]
                else:
                    ref = pack_ref.at[at]
                ref[:, 0 : 4 * width] = gw_ref[at, :].astype(BF)
                ref[:, 4 * width :] = small_part[at, :]


def backward_call(
    m0,
    mbc,
    last,
    own_rows,
    images,
    cotangent,
    count,
    meta,
    back,
    saved,
    coef,
    weights,
    small,
    extra,
    acc,
):
    seq_len, width = images.shape[1], images.shape[2]
    rows = meta.shape[1]
    pad_len = rows // 2
    mb = images.shape[0] // MICRO
    qkv, probs, att, mid, rp = saved
    at = lambda i: i + m0
    image_block = pl.BlockSpec((mb, seq_len, width), lambda i: (at(i), 0, 0))
    in_specs = [
        pl.BlockSpec(memory_space=pltpu.SMEM),
        image_block,
        image_block,
        pl.BlockSpec((1, rows, 8), lambda i: (at(i), 0, 0)),
        pl.BlockSpec((EXPERTS, 2, 1, CAP, width), lambda i: (0, 0, i, 0, 0)),
        pl.BlockSpec((1, rows, 3 * width), lambda i: (i, 0, 0)),
        pl.BlockSpec((1, 2, HEADS // 2, rows, pad_len), lambda i: (i, 0, 0, 0, 0)),
        pl.BlockSpec((1, rows, width), lambda i: (i, 0, 0)),
        pl.BlockSpec((1, rows, width), lambda i: (i, 0, 0)),
        pl.BlockSpec((1, rows, SMALL), lambda i: (i, 0, 0)),
        full_block(coef.shape),
        full_block(weights.shape),
        full_block(small.shape),
        full_block(extra.shape),
    ]
    args = [count, images, cotangent, meta, back, qkv, probs, att, mid, rp]
    args += [coef, weights, small, extra]
    aliases = {}
    if acc is not None:
        base = len(args)
        in_specs += [full_block(acc[0].shape), full_block(acc[1].shape)]
        in_specs += [pl.BlockSpec(memory_space=pl.ANY)] * 2
        args += list(acc)
        aliases = {base + 2: 0, base + 3: 1}
    sums = [(width, 4 * width), (SMALL, width)]
    pack_shape = (width, weights.shape[1])
    if own_rows == BLOCK:
        pack_shape = (CORES, width // (CORES * BLOCK), BLOCK, weights.shape[1])
    if last:
        grads = [jax.ShapeDtypeStruct(pack_shape, BF)]
        held = [pltpu.VMEM(shape, F32) for shape in sums]
    else:
        grads = [jax.ShapeDtypeStruct(shape, F32) for shape in sums]
        held = []
    return pl.pallas_call(
        functools.partial(backward_kernel, m0, seq_len, pad_len, acc is not None, last),
        grid=(mbc,),
        in_specs=in_specs,
        out_specs=[
            image_block,
            image_block,
        ]
        + [full_block(g.shape) for g in grads],
        out_shape=[
            jax.ShapeDtypeStruct(images.shape, BF),
            jax.ShapeDtypeStruct(images.shape, BF),
        ]
        + grads,
        scratch_shapes=[
            pltpu.VMEM((rows, width), F32),
            pltpu.VMEM((rows, width), F32),
            pltpu.VMEM((rows, 3 * width), BF),
        ]
        + held,
        input_output_aliases=aliases,
        compiler_params=pltpu.CompilerParams(vmem_limit_bytes=VMEM_LIMIT),
        cost_estimate=pl.CostEstimate(
            flops=mbc * 20 * 10**9, bytes_accessed=mbc * 10 * 10**6, transcendentals=0
        ),
        name="dense_backward",
    )(*args)


def finish_kernel(
    got_ref,
    bal_ref,
    qkv_ref,
    out_ref,
    router_ref,
    gain1_ref,
    bias1_ref,
    qv_ref,
    obias_ref,
    gain2_ref,
    bias2_ref,
    ein_ref,
    eout_ref,
    balance_ref,
    turned,
):
    sources, rows, wide = got_ref.shape
    width = out_ref.shape[1]
    whole = got_ref[0].astype(F32)
    for source in range(1, sources):
        whole = whole + got_ref[source].astype(F32)
    qkv_ref[...] = whole[:, : 3 * width]
    out_ref[...] = whole[:, 3 * width : 4 * width]
    turned[...] = jnp.zeros_like(turned)
    turned[0:rows, :] = whole[:, 4 * width :]
    balance_ref[...] = jnp.sum(turned[0:1, :] * bal_ref[0:1, :], -1, keepdims=True)
    turned[...] = turned[...].T
    router_ref[...] = turned[0:EXPERTS, 0:rows]
    for row, ref in (
        (ROW_GAIN1, gain1_ref),
        (ROW_BIAS1, bias1_ref),
        (ROW_OBIAS, obias_ref),
        (ROW_GAIN2, gain2_ref),
        (ROW_BIAS2, bias2_ref),
    ):
        ref[...] = turned[row : row + 1, 0:rows]
    qv_ref[...] = turned[ROW_QBIAS : ROW_VBIAS + 1, 0:rows]
    eout_ref[...] = turned[ROW_EOUT : ROW_EOUT + EXPERTS, 0:rows]
    for c in range(ein_ref.shape[1] // rows):
        at = ROW_EIN + c * EXPERTS
        ein_ref[:, c * rows : (c + 1) * rows] = turned[at : at + EXPERTS, 0:rows]


def finish_call(got, bal, width, ff_rows):
    rows = got.shape[1]
    shapes = [
        (rows, 3 * width),
        (rows, width),
        (EXPERTS, rows),
        (1, rows),
        (1, rows),
        (2, rows),
        (1, rows),
        (1, rows),
        (1, rows),
        (EXPERTS, ff_rows),
        (EXPERTS, rows),
        (1, 1),
    ]
    vm = pl.BlockSpec(memory_space=pltpu.VMEM)
    return pl.pallas_call(
        finish_kernel,
        in_specs=[vm] * 2,
        out_specs=[vm] * len(shapes),
        out_shape=[jax.ShapeDtypeStruct(shape, F32) for shape in shapes],
        scratch_shapes=[pltpu.VMEM((SMALL, SMALL), F32)],
        name="finish",
    )(got, bal)


def unpack_kernel(cnt_ref, *refs):
    blocks, (in_ref, out_ref) = refs[:-2], refs[-2:]
    width = out_ref.shape[2]
    half = out_ref.shape[1]
    for r, block in enumerate(blocks):
        e = lax.bitwise_xor(cnt_ref[1], r)
        for c in range(half // BLOCK):
            in_ref[e, :, c * width : (c + 1) * width] = block[
                c * BLOCK : (c + 1) * BLOCK, :
            ].astype(F32)
        out_ref[e] = block[half:, :].astype(F32)


def unpack_call(count, blocks, parts):
    rows, width = blocks[0].shape
    vm = pl.BlockSpec(memory_space=pltpu.VMEM)
    return pl.pallas_call(
        unpack_kernel,
        in_specs=[pl.BlockSpec(memory_space=pltpu.SMEM)] + [vm] * EXPERTS,
        out_specs=[vm] * 2,
        out_shape=[
            jax.ShapeDtypeStruct((EXPERTS, BLOCK, parts * width), F32),
            jax.ShapeDtypeStruct((EXPERTS, rows // 2, width), F32),
        ],
        name="unpack",
    )(count, *blocks)


def shards(
    total,
    images,
    image_count,
    expert_index,
    expert_slot,
    keep,
    cotangent,
    ln1_gain,
    ln1_bias,
    qkv_weight,
    qv_bias,
    out_weight,
    out_bias,
    ln2_gain,
    ln2_bias,
    router_weight,
    expert_in,
    expert_in_bias,
    expert_out,
    expert_out_bias,
):
    slots, seq_len, width = images.shape
    planes = total // EXPERTS
    rows = width // total
    ff = expert_in.shape[2]
    ff_rows = ff // total
    mb = slots // MICRO
    pad_len = -(-seq_len // 16) * 16
    plane_groups = [[z * EXPERTS + p for p in range(EXPERTS)] for z in range(planes)]
    core_groups = [
        [z * EXPERTS + c * CORES + k for c in range(CHIPS)]
        for z in range(planes)
        for k in range(CORES)
    ]
    far_groups = [[CORES * i + k for i in range(total // CORES)] for k in range(CORES)]
    chip_groups = [[CORES * i + k for k in range(CORES)] for i in range(total // CORES)]
    z_groups = [[z * EXPERTS + p for z in range(planes)] for p in range(EXPERTS)]

    def plane_swap(v):
        return lax.all_to_all(v, "dp", 0, 0, tiled=True, axis_index_groups=plane_groups)

    def z_swap(v):
        return lax.all_to_all(v, "dp", 0, 0, tiled=True, axis_index_groups=z_groups)

    def z_gather(v):
        return lax.all_gather(v, "dp", axis=0, tiled=True, axis_index_groups=z_groups)

    parts = ff // width
    if rows == BLOCK:
        expert_pack = pack_call(expert_in, expert_out)
    else:
        expert_pack = jnp.concatenate(
            [
                expert_in.reshape(EXPERTS, rows, parts, width)
                .transpose(0, 2, 1, 3)
                .reshape(EXPERTS, ff_rows, width),
                expert_out,
            ],
            1,
        )
    expert_pack = plane_swap(expert_pack)

    live_img = (jnp.arange(slots) < image_count[0]).astype(F32)
    live_tok = jnp.broadcast_to(live_img[:, None, None], (slots, seq_len, 1))
    if rows == BLOCK:
        vectors = [v[None] for v in (ln1_gain, ln1_bias, out_bias, ln2_gain, ln2_bias)]
        packed = prepare_call(
            image_count,
            expert_index.transpose(0, 2, 1),
            qkv_weight,
            out_weight,
            router_weight.T,
            vectors[0],
            vectors[1],
            qv_bias,
            *vectors[2:],
            expert_in_bias,
            expert_out_bias,
        )
    else:
        hits = (expert_index[..., None] == jnp.arange(EXPERTS)).astype(F32) * live_tok[..., None]
        local_counts = jnp.sum(hits, axis=(0, 1, 2))
        high = jnp.floor(local_counts * (1.0 / 128.0))
        told = jnp.concatenate([high, local_counts - 128.0 * high, image_count.astype(F32)])
        small_cols = jnp.concatenate(
            [
                router_weight,
                ln1_gain[:, None],
                ln1_bias[:, None],
                qv_bias.T,
                out_bias[:, None],
                ln2_gain[:, None],
                ln2_bias[:, None],
                jnp.zeros((rows, 1), BF),
                expert_in_bias.reshape(EXPERTS, parts, rows).transpose(2, 1, 0).reshape(rows, -1),
                expert_out_bias.T,
                jnp.broadcast_to(told.astype(BF)[None], (rows, 2 * EXPERTS + 1)),
            ],
            1,
        )
        small_cols = jnp.pad(small_cols, ((0, 0), (0, SMALL - small_cols.shape[1])))
        packed = jnp.concatenate([qkv_weight, out_weight, small_cols], 1)
    wide = packed.shape[1]
    packed = z_gather(packed)
    packed = jnp.broadcast_to(packed[None], (CHIPS,) + packed.shape)
    packed, expert_pack = lax.optimization_barrier((packed, expert_pack))
    first = lax.all_to_all(
        packed,
        "dp",
        0,
        0,
        tiled=True,
        axis_index_groups=core_groups,
    )
    second = lax.ppermute(first, "dp", [(i, i ^ 1) for i in range(total)])
    me = lax.axis_index("dp")
    own_count = jnp.concatenate([image_count, (me % EXPERTS)[None]])
    if rows != BLOCK:
        even = me % CORES == 0
        both = jnp.stack([jnp.where(even, first, second), jnp.where(even, second, first)], 1)
        first = (
            both.reshape(CHIPS, CORES, planes, rows, wide)
            .transpose(2, 0, 1, 3, 4)
            .reshape(width, wide)
        )
        second = first[:, 4 * width :].astype(F32).T

    target = jnp.where(keep == 1, expert_index * CAP + expert_slot, -1).astype(F32)
    meta = jnp.concatenate(
        [
            target,
            expert_index.astype(F32),
            keep.astype(F32),
            live_tok,
            jnp.zeros((slots, seq_len, 1), F32),
        ],
        -1,
    )
    fill = jnp.array([-1.0, -1.0, 0.0, 0.0, 0.0, 0.0, 0.0, 0.0], F32)
    meta = jnp.concatenate(
        [meta, jnp.broadcast_to(fill, (slots, pad_len - seq_len, 8))], 1
    ).reshape(MICRO, mb * pad_len, 8)
    lane_t = meta.transpose(0, 2, 1)

    expert_pack = z_gather(expert_pack)
    if rows != BLOCK:
        blocks = width // BLOCK
        expert_pack = jnp.concatenate(
            [
                expert_pack[:, :ff_rows]
                .reshape(blocks, total // blocks, parts, rows, width)
                .transpose(0, 2, 1, 3, 4)
                .reshape(blocks, parts * BLOCK, width),
                expert_pack[:, ff_rows:].reshape(blocks, parts * BLOCK, width),
            ],
            1,
        )

    spans = []
    for size in CHUNKS:
        spans.append((sum(span[1] for span in spans), size))
    saved, sent, prob_sums = [], [], []
    for m0, mbc in spans:
        assemble = m0 == 0 and rows == BLOCK
        xd, qkv, probs, att, mid, rp, prob, *made = forward_call(
            m0, mbc, assemble, images, cotangent, own_count, lane_t, meta, first, second
        )
        if assemble:
            first, second = made
        saved.append((qkv, probs, att, mid, rp))
        prob_sums.append(prob[0, :EXPERTS])
        sent.append(plane_swap(xd))
    weights = first
    small, _ = lax.optimization_barrier((second, prob_sums[-1]))

    in_bias = small[AT_EIN : AT_EIN + parts * EXPERTS].reshape(parts, EXPERTS, width)
    in_bias = lax.dynamic_index_in_dim(in_bias, me % EXPERTS, 1, keepdims=False)
    in_bias = in_bias.reshape(parts, total, rows).transpose(1, 0, 2).reshape(1, ff)
    out_bias_e = lax.dynamic_slice_in_dim(small, AT_EOUT + me % EXPERTS, 1, 0)
    sums = jnp.sum(small[AT_HIGH : AT_IMAGES + 1], 1) * (1.0 / rows)
    counts_all = sums[:EXPERTS] * 128.0 + sums[EXPERTS : 2 * EXPERTS]
    live_total = sums[2 * EXPERTS] * float(seq_len)
    plane_counts = lax.dynamic_slice_in_dim(
        small[AT_IMAGES], (me // EXPERTS) * (EXPERTS * rows), EXPERTS * rows, 0
    )
    plane_counts = plane_counts.reshape(EXPERTS, rows)[:, 0].astype(jnp.int32)
    coef = jnp.pad(BALANCE_WEIGHT * EXPERTS * counts_all / live_total, (0, SMALL - EXPERTS))
    coef = jnp.broadcast_to(coef[None], (8, SMALL))
    in_bias = jnp.broadcast_to(in_bias, (8, ff))
    out_bias_e = jnp.broadcast_to(out_bias_e, (8, width))

    acc = None
    back = []
    for (m0, mbc), rows_in in zip(spans, sent):
        y, *acc = expert_call(
            m0,
            mbc,
            m0 + mbc == MICRO,
            plane_counts,
            rows_in,
            expert_pack,
            in_bias,
            out_bias_e,
            acc,
        )
        back.append(plane_swap(y))
    expert_grads, gb1, gb2 = acc

    if rows != BLOCK:
        expert_grads = jnp.concatenate(
            [
                expert_grads[:, : parts * BLOCK]
                .reshape(blocks, parts, total // blocks, rows, width)
                .transpose(0, 2, 1, 3, 4)
                .reshape(total, ff_rows, width),
                expert_grads[:, parts * BLOCK :].reshape(total, ff_rows, width),
            ],
            1,
        )
    expert_grads = lax.psum_scatter(
        expert_grads, "dp", scatter_dimension=0, tiled=True, axis_index_groups=z_groups
    )
    if rows == BLOCK:
        place = me % EXPERTS
        blocks_in = []
        for r in range(EXPERTS):
            block = lax.dynamic_index_in_dim(expert_grads, place ^ r, 0, keepdims=False)
            if r:
                block = lax.ppermute(block, "dp", [(i, i ^ r) for i in range(total)])
            blocks_in.append(block)
        expert_in_grad, expert_out_grad = unpack_call(own_count, blocks_in, parts)
    else:
        expert_grads = plane_swap(expert_grads).astype(F32)
        expert_in_grad = (
            expert_grads[:, :ff_rows]
            .reshape(EXPERTS, parts, rows, width)
            .transpose(0, 2, 1, 3)
            .reshape(EXPERTS, rows, ff)
        )
        expert_out_grad = expert_grads[:, ff_rows:]

    prob_sum = prob_sums[0]
    for piece in prob_sums[1:]:
        prob_sum = prob_sum + piece
    p_hi = prob_sum.astype(BF).astype(F32)
    mine = (jnp.arange(EXPERTS) == me % EXPERTS).astype(F32)
    e_in = gb1[0].reshape(total, parts, rows).transpose(1, 0, 2).reshape(parts, 1, width)
    extra = jnp.concatenate(
        [
            jnp.zeros((ROW_PROB, width), F32),
            jnp.broadcast_to(
                jnp.concatenate([p_hi, prob_sum - p_hi])[:, None], (2 * EXPERTS, width)
            ),
            mine[:, None] * gb2[0:1],
            (mine[None, :, None] * e_in).reshape(parts * EXPERTS, width),
            jnp.zeros((SMALL - ROW_EIN - parts * EXPERTS, width), F32),
        ],
        0,
    )

    acc = None
    for (m0, mbc), returned, kept in zip(spans, back, saved):
        block_out, image_grad, *acc = backward_call(
            m0,
            mbc,
            m0 + mbc == MICRO,
            rows,
            images,
            cotangent,
            image_count,
            meta,
            returned,
            kept,
            coef,
            weights,
            small,
            extra,
            None if acc is None else (*acc, block_out, image_grad),
        )

    grads = acc[0]
    if rows != BLOCK:
        grads = grads.reshape(total // CORES, CORES, rows, wide).transpose(1, 0, 2, 3)
    grads = lax.all_to_all(grads, "dp", 0, 0, tiled=True, axis_index_groups=chip_groups)
    grads = jnp.sum(grads.astype(F32), 0).astype(BF)
    grads = lax.all_to_all(
        grads.reshape(total // CORES, rows, wide),
        "dp",
        0,
        0,
        tiled=True,
        axis_index_groups=far_groups,
    )
    bal = EXPERTS * counts_all / live_total / live_total
    bal = jnp.concatenate([jnp.zeros((ROW_PROB,), F32), bal, bal])
    bal = jnp.broadcast_to(jnp.pad(bal, (0, SMALL - bal.shape[0]))[None], (8, SMALL))
    (
        qkv_grad,
        out_grad,
        router_grad,
        gain1_grad,
        bias1_grad,
        qv_grad,
        obias_grad,
        gain2_grad,
        bias2_grad,
        ein_grad,
        eout_grad,
        balance,
    ) = finish_call(grads, bal, width, ff_rows)
    return (
        block_out,
        image_grad,
        balance.reshape(()),
        gain1_grad.reshape(rows),
        bias1_grad.reshape(rows),
        qkv_grad,
        qv_grad,
        out_grad,
        obias_grad.reshape(rows),
        gain2_grad.reshape(rows),
        bias2_grad.reshape(rows),
        router_grad.T,
        expert_in_grad,
        ein_grad,
        expert_out_grad,
        eout_grad,
    )


def solution(mesh):
    placed = (
        P("dp", None, None),
        P("dp"),
        P("dp", None, None),
        P("dp", None, None),
        P("dp", None, None),
        P("dp", None, None),
        P("dp"),
        P("dp"),
        P("dp", None),
        P(None, "dp"),
        P("dp", None),
        P("dp"),
        P("dp"),
        P("dp"),
        P("dp", None),
        P(None, "dp", None),
        P(None, "dp"),
        P(None, "dp", None),
        P(None, "dp"),
    )
    return jax.shard_map(
        functools.partial(shards, mesh.shape["dp"]),
        mesh=mesh,
        in_specs=placed,
        out_specs=(
            P("dp", None, None),
            P("dp", None, None),
            P(),
            P("dp"),
            P("dp"),
            P("dp", None),
            P(None, "dp"),
            P("dp", None),
            P("dp"),
            P("dp"),
            P("dp"),
            P("dp", None),
            P(None, "dp", None),
            P(None, "dp"),
            P(None, "dp", None),
            P(None, "dp"),
        ),
        check_vma=False,
    )
```

```python
import functools
import math

import jax
import jax.numpy as jnp
from jax import lax
from jax.experimental import pallas as pl
from jax.experimental.pallas import tpu as pltpu
from jax.sharding import PartitionSpec as P

HEADS = 8
HEAD_DIM = 64
EXPERTS = 8
MICRO = 4
CAP = 128
CHUNKS = (2, 2)
PAIR = 2 * HEAD_DIM
DISPATCH = 4

EPSILON = 1e-06
BALANCE_WEIGHT = 8.0

BF = jnp.bfloat16
F32 = jnp.float32

ROW_GAIN1, ROW_BIAS1, ROW_QBIAS, ROW_VBIAS, ROW_OBIAS, ROW_GAIN2, ROW_BIAS2 = range(8, 15)
SMALL = 128
ROW_PROB, ROW_EOUT, ROW_EIN = 16, 32, 40
AT_EIN, AT_EOUT, AT_HIGH, AT_LOW, AT_IMAGES = 16, 48, 56, 64, 72
CORES = 2
CHIPS = EXPERTS // CORES
BLOCK = 16
COL_T0, COL_T1, COL_R0, COL_R1, COL_K0, COL_K1, COL_LIVE = range(7)
VMEM_LIMIT = 60 * 1024 * 1024


def mm(a, b):
    return lax.dot_general(a, b, (((1,), (0,)), ((), ())), preferred_element_type=F32)


def mm_nt(a, b):
    return lax.dot_general(a, b, (((1,), (1,)), ((), ())), preferred_element_type=F32)


def mm_tn(a, b):
    return lax.dot_general(a, b, (((0,), (0,)), ((), ())), preferred_element_type=F32)


def load_padded(dst, src, seq_len, pad_len):
    for i in range(2):
        tail = (seq_len // 16) * 16
        dst[i * pad_len + tail : (i + 1) * pad_len, :] = jnp.zeros(
            (pad_len - tail, dst.shape[1]), dst.dtype
        )
        dst[i * pad_len : i * pad_len + seq_len, :] = src[i].astype(dst.dtype)


def load_table(facts, table, meta_ref, pad_len):
    for i in range(2):
        table[0 : meta_ref.shape[1], :] = meta_ref[i]
        facts[i * pad_len : (i + 1) * pad_len, :] = table[...].T


def norm_parts(x):
    mean = jnp.mean(x, -1, keepdims=True)
    centered = x - mean
    spread = jnp.mean(centered * centered, -1, keepdims=True)
    inv = lax.rsqrt(spread + EPSILON)
    return centered * inv, inv


def norm_back(d_out, xhat, inv, gain):
    d_hat = d_out * gain
    first = jnp.mean(d_hat, -1, keepdims=True)
    second = jnp.mean(d_hat * xhat, -1, keepdims=True)
    return inv * (d_hat - first - xhat * second)


def half_masks():
    lane = lax.broadcasted_iota(jnp.int32, (1, PAIR), 1)
    low = jnp.where(lane < HEAD_DIM, 1.0, 0.0)
    return low.astype(BF), (1.0 - low).astype(BF), lane < HEAD_DIM


def stack_heads(block, low, high):
    return jnp.concatenate([block * low, block * high], 0)


def forward_kernel(
    m0,
    seq_len,
    pad_len,
    assemble,
    cnt_ref,
    img_ref,
    cot_ref,
    meta_ref,
    first_ref,
    second_ref,
    xd_ref,
    qkv_ref,
    p_ref,
    att_ref,
    mid_ref,
    rp_ref,
    psum_ref,
    *rest,
):
    if assemble:
        w_ref, small_ref, xs, cs, facts, table = rest
    else:
        w_ref, small_ref = first_ref, second_ref
        xs, cs, facts, table = rest
    step = pl.program_id(0)
    width = xs.shape[1]
    alive = cnt_ref[0] > 2 * (m0 + step)

    @pl.when(step == 0)
    def _():
        psum_ref[...] = jnp.zeros_like(psum_ref)
        table[...] = jnp.zeros_like(table)
        if assemble:
            core = lax.rem(lax.axis_index("dp"), CORES)
            for ref, owner in ((first_ref, core), (second_ref, 1 - core)):
                for chip in range(CHIPS):
                    for z in range(ref.shape[1] // BLOCK):
                        plane = lax.bitwise_xor(lax.axis_index("dp") // EXPERTS, z)
                        at = plane * EXPERTS + chip * CORES + owner
                        at = pl.multiple_of(at * BLOCK, BLOCK)
                        w_ref[pl.ds(at, BLOCK), :] = ref[chip, z * BLOCK : (z + 1) * BLOCK, :]
            small_ref[...] = w_ref[:, 4 * width :].astype(F32).T

    @pl.when(jnp.logical_not(alive))
    def _():
        xd_ref[...] = jnp.zeros_like(xd_ref)

    @pl.when(alive)
    def _():
        load_padded(xs, img_ref, seq_len, pad_len)
        load_padded(cs, cot_ref, seq_len, pad_len)
        load_table(facts, table, meta_ref, pad_len)
        xhat, inv = norm_parts(xs[...])
        normed = (
            xhat * small_ref[ROW_GAIN1 : ROW_GAIN1 + 1, :] + small_ref[ROW_BIAS1 : ROW_BIAS1 + 1, :]
        ).astype(BF)
        for part, row in ((0, ROW_QBIAS), (1, None), (2, ROW_VBIAS)):
            cols = slice(part * width, (part + 1) * width)
            value = mm(normed, w_ref[:, cols])
            if row is not None:
                value = value + small_ref[row : row + 1, :]
            qkv_ref[0, :, cols] = value.astype(BF)
        low, high, low_mask = half_masks()
        key_ok = lax.broadcasted_iota(jnp.int32, (1, pad_len), 1) < seq_len
        for i in range(2):
            rows = slice(i * pad_len, (i + 1) * pad_len)
            for hp in range(HEADS // 2):
                at = hp * PAIR
                q = qkv_ref[0, rows, at : at + PAIR]
                k = qkv_ref[0, rows, width + at : width + at + PAIR]
                v = qkv_ref[0, rows, 2 * width + at : 2 * width + at + PAIR]
                s = mm_nt(stack_heads(q, low, high), k) * (HEAD_DIM**-0.5)
                s = jnp.where(key_ok, s, -1e30)
                e = jnp.exp(s - jnp.max(s, -1, keepdims=True))
                p = (e * (1.0 / jnp.sum(e, -1, keepdims=True))).astype(BF)
                p_ref[0, i, hp] = p
                o = mm(p, v)
                att_ref[0, rows, at : at + PAIR] = jnp.where(
                    low_mask, o[:pad_len], o[pad_len:]
                ).astype(BF)
        middle = (
            xs[...]
            + mm(att_ref[0], w_ref[:, 3 * width : 4 * width])
            + small_ref[ROW_OBIAS : ROW_OBIAS + 1, :]
        )
        mid_ref[0] = middle
        xhat2, inv2 = norm_parts(middle)
        mixed = (
            xhat2 * small_ref[ROW_GAIN2 : ROW_GAIN2 + 1, :]
            + small_ref[ROW_BIAS2 : ROW_BIAS2 + 1, :]
        ).astype(BF)
        logits = mm(mixed, w_ref[:, 4 * width : 4 * width + SMALL])
        lane = lax.broadcasted_iota(jnp.int32, (1, SMALL), 1)
        logits = jnp.where(lane < EXPERTS, logits, -1e30)
        e = jnp.exp(logits - jnp.max(logits, -1, keepdims=True))
        rp = e * (1.0 / jnp.sum(e, -1, keepdims=True))
        rp_ref[0] = rp
        live = facts[:, COL_LIVE : COL_LIVE + 1]
        psum_ref[0:1, :] += jnp.sum(rp * live, 0, keepdims=True)
        d_final = cs[...] * live
        lane_f = lane.astype(F32)
        weighted = []
        for route, kept in ((COL_R0, COL_K0), (COL_R1, COL_K1)):
            hot = lane_f == facts[:, route : route + 1]
            gate = jnp.sum(jnp.where(hot, rp, 0.0), -1, keepdims=True)
            gate = gate * facts[:, kept : kept + 1]
            weighted.append((gate * d_final).astype(BF))
        slot = lax.broadcasted_iota(jnp.int32, (DISPATCH * CAP, 1), 0).astype(F32)
        targets = facts[...].T
        for e_id in range(0, EXPERTS, DISPATCH):
            here = slot + float(e_id * CAP)
            sel0 = jnp.where(here == targets[COL_T0 : COL_T0 + 1, :], 1.0, 0.0)
            sel1 = jnp.where(here == targets[COL_T1 : COL_T1 + 1, :], 1.0, 0.0)
            shape = (DISPATCH, CAP, width)
            at = slice(e_id, e_id + DISPATCH)
            xd_ref[at, 0, 0] = mm((sel0 + sel1).astype(BF), mixed).astype(BF).reshape(shape)
            xd_ref[at, 1, 0] = (
                (mm(sel0.astype(BF), weighted[0]) + mm(sel1.astype(BF), weighted[1]))
                .astype(BF)
                .reshape(shape)
            )


def full_block(shape):
    return pl.BlockSpec(shape, lambda i: (0,) * len(shape))


def pack_kernel(in_ref, out_ref, pack_ref):
    width = out_ref.shape[2]
    half = out_ref.shape[1]
    for c in range(half // BLOCK):
        pack_ref[:, c * BLOCK : (c + 1) * BLOCK, :] = in_ref[:, :, c * width : (c + 1) * width]
    pack_ref[:, half:, :] = out_ref[...]


def pack_call(expert_in, expert_out):
    vm = pl.BlockSpec(memory_space=pltpu.VMEM)
    shape = (expert_out.shape[0], 2 * expert_out.shape[1], expert_out.shape[2])
    return pl.pallas_call(
        pack_kernel,
        in_specs=[vm] * 2,
        out_specs=vm,
        out_shape=jax.ShapeDtypeStruct(shape, BF),
        name="pack",
    )(expert_in, expert_out)


def prepare_kernel(
    cnt_ref,
    index_ref,
    qkv_ref,
    out_ref,
    router_ref,
    gain1_ref,
    bias1_ref,
    qv_ref,
    obias_ref,
    gain2_ref,
    bias2_ref,
    ein_ref,
    eout_ref,
    packed_ref,
    turned,
):
    rows, width = out_ref.shape
    packed_ref[:, 0 : 3 * width] = qkv_ref[...]
    packed_ref[:, 3 * width : 4 * width] = out_ref[...]
    turned[...] = jnp.zeros_like(turned)
    turned[0:EXPERTS, 0:rows] = router_ref[...].astype(F32)
    for row, ref in (
        (ROW_GAIN1, gain1_ref),
        (ROW_BIAS1, bias1_ref),
        (ROW_OBIAS, obias_ref),
        (ROW_GAIN2, gain2_ref),
        (ROW_BIAS2, bias2_ref),
    ):
        turned[row : row + 1, 0:rows] = ref[...].astype(F32)
    turned[ROW_QBIAS : ROW_VBIAS + 1, 0:rows] = qv_ref[...].astype(F32)
    turned[AT_EOUT : AT_EOUT + EXPERTS, 0:rows] = eout_ref[...].astype(F32)
    ein = ein_ref[...].astype(F32)
    for c in range(ein.shape[1] // rows):
        at = AT_EIN + c * EXPERTS
        turned[at : at + EXPERTS, 0:rows] = ein[:, c * rows : (c + 1) * rows]
    slots, top, seq_len = index_ref.shape
    chosen = index_ref[...]
    slot = lax.broadcasted_iota(jnp.int32, (slots, top, seq_len), 0)
    chosen = jnp.where(slot < cnt_ref[0], chosen, -1)
    for e in range(EXPERTS):
        hits = jnp.where(chosen == e, 1.0, 0.0)
        hits = jnp.sum(jnp.sum(hits, 0), -1, keepdims=True)
        hits = jnp.sum(hits, 0, keepdims=True)
        high = jnp.floor(hits * (1.0 / 128.0))
        turned[AT_HIGH + e : AT_HIGH + e + 1, :] = jnp.broadcast_to(high, (1, SMALL))
        turned[AT_LOW + e : AT_LOW + e + 1, :] = jnp.broadcast_to(hits - 128.0 * high, (1, SMALL))
    turned[AT_IMAGES : AT_IMAGES + 1, :] = jnp.full((1, SMALL), cnt_ref[0].astype(F32))
    turned[...] = turned[...].T
    packed_ref[:, 4 * width :] = turned[0:rows, :].astype(BF)


def prepare_call(count, *args):
    vm = pl.BlockSpec(memory_space=pltpu.VMEM)
    rows, width = args[2].shape
    return pl.pallas_call(
        prepare_kernel,
        in_specs=[pl.BlockSpec(memory_space=pltpu.SMEM)] + [vm] * len(args),
        out_specs=vm,
        out_shape=jax.ShapeDtypeStruct((rows, 4 * width + SMALL), BF),
        scratch_shapes=[pltpu.VMEM((SMALL, SMALL), F32)],
        name="prepare",
    )(count, *args)


def forward_call(m0, mbc, assemble, images, cotangent, count, meta, weights, small):
    seq_len, width = images.shape[1], images.shape[2]
    pad_len = meta.shape[2]
    rows = 2 * pad_len
    at = lambda i: i + m0
    mb = images.shape[0] // mbc
    made_here = []
    if assemble:
        made_here = [
            jax.ShapeDtypeStruct((width, weights.shape[2]), BF),
            jax.ShapeDtypeStruct((SMALL, width), F32),
        ]
    return pl.pallas_call(
        functools.partial(forward_kernel, m0, seq_len, pad_len, assemble),
        grid=(mbc,),
        in_specs=[
            pl.BlockSpec(memory_space=pltpu.SMEM),
            pl.BlockSpec((mb, seq_len, width), lambda i: (i, 0, 0)),
            pl.BlockSpec((mb, seq_len, width), lambda i: (i, 0, 0)),
            pl.BlockSpec((mb, 8, pad_len), lambda i: (at(i), 0, 0)),
            full_block(weights.shape),
            full_block(small.shape),
        ],
        out_specs=[
            pl.BlockSpec((EXPERTS, 2, 1, CAP, width), lambda i: (0, 0, i, 0, 0)),
            pl.BlockSpec((1, rows, 3 * width), lambda i: (i, 0, 0)),
            pl.BlockSpec((1, 2, HEADS // 2, rows, pad_len), lambda i: (i, 0, 0, 0, 0)),
            pl.BlockSpec((1, rows, width), lambda i: (i, 0, 0)),
            pl.BlockSpec((1, rows, width), lambda i: (i, 0, 0)),
            pl.BlockSpec((1, rows, SMALL), lambda i: (i, 0, 0)),
            full_block((8, SMALL)),
        ]
        + [full_block(made.shape) for made in made_here],
        out_shape=[
            jax.ShapeDtypeStruct((EXPERTS, 2, mbc, CAP, width), BF),
            jax.ShapeDtypeStruct((mbc, rows, 3 * width), BF),
            jax.ShapeDtypeStruct((mbc, 2, HEADS // 2, rows, pad_len), BF),
            jax.ShapeDtypeStruct((mbc, rows, width), BF),
            jax.ShapeDtypeStruct((mbc, rows, width), F32),
            jax.ShapeDtypeStruct((mbc, rows, SMALL), F32),
            jax.ShapeDtypeStruct((8, SMALL), F32),
        ]
        + made_here,
        scratch_shapes=[
            pltpu.VMEM((rows, width), F32),
            pltpu.VMEM((rows, width), F32),
            pltpu.VMEM((rows, SMALL), F32),
            pltpu.VMEM((SMALL, pad_len), F32),
        ],
        compiler_params=pltpu.CompilerParams(vmem_limit_bytes=VMEM_LIMIT),
        cost_estimate=pl.CostEstimate(
            flops=mbc * 8 * 10**9, bytes_accessed=mbc * 10 * 10**6, transcendentals=0
        ),
        name="dense_forward",
    )(count, images, cotangent, meta, weights, small)


GROUP = 4


def expert_kernel(
    m0,
    mbc,
    has_acc,
    last,
    cnt_ref,
    x_ref,
    w_ref,
    b1_ref,
    b2_ref,
    *rest,
):
    if has_acc:
        a1_ref, a2_ref, ab1_ref, ab2_ref = rest[:4]
        rest = rest[4:]
    if last:
        y_ref, pack_ref, gb1_ref, gb2_ref, s1, s2, order, xin, din, xout, dout = rest
    else:
        y_ref, s1, s2, gb1_ref, gb2_ref, order, xin, din, xout, dout = rest
    width = x_ref.shape[-1]
    ff = b1_ref.shape[1]
    half = w_ref.shape[1] // 2
    per_tile = width // half
    if has_acc:
        s1[...] = a1_ref[...]
        s2[...] = a2_ref[...]
        gb1_ref[...] = ab1_ref[...]
        gb2_ref[...] = ab2_ref[...]
    else:
        s1[...] = jnp.zeros_like(s1)
        s2[...] = jnp.zeros_like(s2)
        gb1_ref[...] = jnp.zeros_like(gb1_ref)
        gb2_ref[...] = jnp.zeros_like(gb2_ref)
    blocks = EXPERTS * mbc

    def is_live(b):
        return (cnt_ref[b // mbc] > 2 * (m0 + b % mbc)).astype(jnp.int32)

    live_total = jnp.int32(0)
    for b in range(blocks):
        live_total = live_total + is_live(b)
    head, tail = jnp.int32(0), live_total
    for b in range(blocks):
        flag = is_live(b)
        order[jnp.where(flag == 1, head, tail)] = b
        head = head + flag
        tail = tail + (1 - flag)

    def one_group(g, carry):
        for j in range(GROUP):
            b = order[g * GROUP + j]
            xin[j * CAP : (j + 1) * CAP, :] = x_ref[b // mbc, 0, b % mbc]
            din[j * CAP : (j + 1) * CAP, :] = x_ref[b // mbc, 1, b % mbc]
        rows_in, d_res = xin[...], din[...]
        gb2_ref[0:1, :] += jnp.sum(d_res.astype(F32), 0, keepdims=True)
        for f in range(ff // width):
            cols = slice(f * width, (f + 1) * width)
            w1 = w_ref[:, f * BLOCK : (f + 1) * BLOCK, :].reshape(width, width)
            w2 = w_ref[f * per_tile : (f + 1) * per_tile, half:, :].reshape(width, width)
            h = mm(rows_in, w1) + b1_ref[0:1, cols]
            bell = jnp.exp(-0.5 * h * h)
            t = 1.0 / (1.0 + (0.3275911 / math.sqrt(2.0)) * jnp.abs(h))
            poly = t * (
                0.5 * 0.254829592
                + t
                * (
                    0.5 * -0.284496736
                    + t * (0.5 * 1.421413741 + t * (0.5 * -1.453152027 + t * (0.5 * 1.061405429)))
                )
            )
            upper = poly * bell
            cdf = jnp.where(h < 0.0, upper, 1.0 - upper)
            act = (h * cdf).astype(BF)
            slope = cdf + h * bell * (1.0 / math.sqrt(2.0 * math.pi))
            d_act = mm_nt(d_res, w2)
            d_hid_f = (d_act * slope).astype(BF)
            gb1_ref[0:1, cols] += jnp.sum(d_hid_f.astype(F32), 0, keepdims=True)
            res = mm(act, w2)
            d_rows = mm_nt(d_hid_f, w1)
            if f == 0:
                xout[...] = res
                dout[...] = d_rows
            else:
                xout[...] += res
                dout[...] += d_rows
            s1[:, cols] += mm_tn(rows_in, d_hid_f)
            s2[cols, :] += mm_tn(act, d_res)
        for j in range(GROUP):
            b = order[g * GROUP + j]
            y_ref[b // mbc, 0, b % mbc] = (
                xout[j * CAP : (j + 1) * CAP, :] + b2_ref[0:1, :]
            ).astype(BF)
            y_ref[b // mbc, 1, b % mbc] = dout[j * CAP : (j + 1) * CAP, :].astype(BF)
        return carry

    lax.fori_loop(0, (live_total + GROUP - 1) // GROUP, one_group, 0)
    if last:
        blocks_of = width // BLOCK
        for f in range(ff // width):
            tile = s1[:, f * width : (f + 1) * width].astype(BF)
            pack_ref[:, f * BLOCK : (f + 1) * BLOCK, :] = tile.reshape(blocks_of, BLOCK, width)
        pack_ref[:, half:, :] = s2[...].astype(BF).reshape(blocks_of, half, width)


def expert_call(m0, mbc, last, counts, x, weights, b1, b2, acc):
    width, ff = weights.shape[2], b1.shape[1]
    if last:
        grads = [jax.ShapeDtypeStruct(weights.shape, BF)]
    else:
        grads = [jax.ShapeDtypeStruct((width, ff), F32), jax.ShapeDtypeStruct((ff, width), F32)]
    vm = pl.BlockSpec(memory_space=pltpu.VMEM)
    scratch = []
    if last:
        scratch += [pltpu.VMEM((width, ff), F32), pltpu.VMEM((ff, width), F32)]
    scratch += [
        pltpu.SMEM((EXPERTS * mbc,), jnp.int32),
        pltpu.VMEM((GROUP * CAP, width), BF),
        pltpu.VMEM((GROUP * CAP, width), BF),
        pltpu.VMEM((GROUP * CAP, width), F32),
        pltpu.VMEM((GROUP * CAP, width), F32),
    ]
    return pl.pallas_call(
        functools.partial(expert_kernel, m0, mbc, acc is not None, last),
        in_specs=[pl.BlockSpec(memory_space=pltpu.SMEM)] + [vm] * (4 + (0 if acc is None else 4)),
        out_specs=[vm] * (len(grads) + 3),
        out_shape=[
            jax.ShapeDtypeStruct(x.shape, BF),
            *grads,
            jax.ShapeDtypeStruct((8, ff), F32),
            jax.ShapeDtypeStruct((8, width), F32),
        ],
        scratch_shapes=scratch,
        compiler_params=pltpu.CompilerParams(vmem_limit_bytes=VMEM_LIMIT),
        cost_estimate=pl.CostEstimate(
            flops=mbc * 20 * 10**9, bytes_accessed=mbc * 10 * 10**6, transcendentals=0
        ),
        name="expert_both",
    )(counts, x, weights, b1, b2, *(() if acc is None else acc))


def backward_kernel(
    m0,
    seq_len,
    pad_len,
    has_acc,
    last,
    cnt_ref,
    img_ref,
    cot_ref,
    meta_ref,
    y_ref,
    qkv_ref,
    p_ref,
    att_ref,
    mid_ref,
    rp_ref,
    coef_ref,
    w_ref,
    small_ref,
    extra_ref,
    *rest,
):
    if has_acc:
        accw_ref, accs_ref = rest[:2]
        rest = rest[4:]
    if last:
        out_ref, grad_ref, pack_ref, xs, cs, dq, facts, table, gw_ref, gs_ref, earlier, sem = rest
    else:
        out_ref, grad_ref, gw_ref, gs_ref, xs, cs, dq, facts, table = rest
    step = pl.program_id(0)
    width = xs.shape[1]
    alive = cnt_ref[0] > 2 * (m0 + step)

    @pl.when(step == 0)
    def _():
        table[...] = jnp.zeros_like(table)
        gw_ref[...] = jnp.zeros_like(gw_ref)
        if has_acc:
            pltpu.make_async_copy(accw_ref, earlier, sem).start()
            gs_ref[...] = accs_ref[...]
        else:
            gs_ref[...] = jnp.zeros_like(gs_ref)

    @pl.when(jnp.logical_not(alive))
    def _():
        out_ref[...] = jnp.zeros_like(out_ref)
        grad_ref[...] = jnp.zeros_like(grad_ref)

    def add_row(row, value):
        gs_ref[row : row + 1, :] += jnp.sum(value, 0, keepdims=True)

    @pl.when(alive)
    def _():
        load_padded(xs, img_ref, seq_len, pad_len)
        load_padded(cs, cot_ref, seq_len, pad_len)
        load_table(facts, table, meta_ref, pad_len)
        rows = xs.shape[0]
        live = facts[:, COL_LIVE : COL_LIVE + 1]
        d_final = cs[...] * live
        middle = mid_ref[0]
        rp = rp_ref[0]
        lane = lax.broadcasted_iota(jnp.int32, (1, SMALL), 1)
        lane_f = lane.astype(F32)
        slot = lax.broadcasted_iota(jnp.int32, (1, EXPERTS * CAP), 1).astype(F32)
        res = y_ref[:, 0, 0].reshape(EXPERTS * CAP, width)
        d_rows = y_ref[:, 1, 0].reshape(EXPERTS * CAP, width)
        final = middle
        d_prob = coef_ref[0:1, :] * live
        sel_all = None
        for target, route, kept in ((COL_T0, COL_R0, COL_K0), (COL_T1, COL_R1, COL_K1)):
            sel = jnp.where(slot == facts[:, target : target + 1], 1.0, 0.0).astype(BF)
            sel_all = sel if sel_all is None else sel_all + sel
            picked = mm(sel, res)
            keep = facts[:, kept : kept + 1]
            hot = lane_f == facts[:, route : route + 1]
            gate = jnp.sum(jnp.where(hot, rp, 0.0), -1, keepdims=True) * keep
            final = final + gate * picked
            d_gate = jnp.sum(picked * d_final, -1, keepdims=True) * keep
            d_prob = d_prob + jnp.where(hot, d_gate, 0.0)
        final = final * live
        for i in range(2):
            out_ref[i] = final[i * pad_len : i * pad_len + seq_len, :].astype(BF)
        d_mixed = mm(sel_all, d_rows)
        d_logits = (rp * (d_prob - jnp.sum(rp * d_prob, -1, keepdims=True))).astype(BF)
        d_mixed = d_mixed + mm_nt(d_logits, w_ref[:, 4 * width : 4 * width + SMALL])
        gain2 = small_ref[ROW_GAIN2 : ROW_GAIN2 + 1, :]
        xhat2, inv2 = norm_parts(middle)
        mixed = (xhat2 * gain2 + small_ref[ROW_BIAS2 : ROW_BIAS2 + 1, :]).astype(BF)
        gs_ref[0:EXPERTS, :] += mm_tn(d_logits, mixed)[0:EXPERTS, :]
        add_row(ROW_GAIN2, d_mixed * xhat2)
        add_row(ROW_BIAS2, d_mixed)
        d_middle = d_final + norm_back(d_mixed, xhat2, inv2, gain2)
        add_row(ROW_OBIAS, d_middle)
        cs[...] = d_middle
        d_branch = d_middle.astype(BF)
        gw_ref[:, 3 * width : 4 * width] += mm_tn(att_ref[0], d_branch)
        d_att_all = mm_nt(d_branch, w_ref[:, 3 * width : 4 * width]).astype(BF)
        low, high, low_mask = half_masks()
        scale = HEAD_DIM**-0.5
        for i in range(2):
            span = slice(i * pad_len, (i + 1) * pad_len)
            for hp in range(HEADS // 2):
                at = hp * PAIR
                q = qkv_ref[0, span, at : at + PAIR]
                k = qkv_ref[0, span, width + at : width + at + PAIR]
                v = qkv_ref[0, span, 2 * width + at : 2 * width + at + PAIR]
                d_att = stack_heads(d_att_all[span, at : at + PAIR], low, high)
                p = p_ref[0, i, hp]
                pf = p.astype(F32)
                d_attn = mm_nt(d_att, v)
                d_s = (pf * (d_attn - jnp.sum(pf * d_attn, -1, keepdims=True))).astype(BF)
                d_v = mm_tn(p, d_att)
                d_k = mm_tn(d_s, stack_heads(q, low, high)) * scale
                d_q = mm(d_s, k) * scale
                dq[span, at : at + PAIR] = jnp.where(
                    low_mask, d_q[:pad_len], d_q[pad_len:]
                ).astype(BF)
                dq[span, width + at : width + at + PAIR] = d_k.astype(BF)
                dq[span, 2 * width + at : 2 * width + at + PAIR] = d_v.astype(BF)
        gain1 = small_ref[ROW_GAIN1 : ROW_GAIN1 + 1, :]
        xhat, inv = norm_parts(xs[...])
        normed = (xhat * gain1 + small_ref[ROW_BIAS1 : ROW_BIAS1 + 1, :]).astype(BF)
        add_row(ROW_QBIAS, dq[:, 0:width].astype(F32))
        add_row(ROW_VBIAS, dq[:, 2 * width : 3 * width].astype(F32))
        gw_ref[:, 0 : 3 * width] += mm_tn(normed, dq[...])
        d_normed = mm_nt(dq[...], w_ref[:, 0 : 3 * width])
        add_row(ROW_GAIN1, d_normed * xhat)
        add_row(ROW_BIAS1, d_normed)
        d_tok = cs[...] + norm_back(d_normed, xhat, inv, gain1)
        for i in range(2):
            grad_ref[i] = d_tok[i * pad_len : i * pad_len + seq_len, :].astype(BF)

    if last:

        @pl.when(step == pl.num_programs(0) - 1)
        def _():
            if has_acc:
                pltpu.make_async_copy(accw_ref, earlier, sem).wait()
                gw_ref[...] += earlier[...]
            small_part = (gs_ref[...] + extra_ref[...]).T.astype(BF)
            for b in range(width // BLOCK):
                at = slice(b * BLOCK, (b + 1) * BLOCK)
                core = b % CORES
                if len(pack_ref.shape) == 4:
                    ref = pack_ref.at[core, b // CORES]
                else:
                    ref = pack_ref.at[at]
                ref[:, 0 : 4 * width] = gw_ref[at, :].astype(BF)
                ref[:, 4 * width :] = small_part[at, :]


def backward_call(
    m0,
    mbc,
    last,
    own_rows,
    images,
    cotangent,
    count,
    meta,
    back,
    saved,
    coef,
    weights,
    small,
    extra,
    acc,
):
    seq_len, width = images.shape[1], images.shape[2]
    pad_len = meta.shape[2]
    rows = 2 * pad_len
    mb = images.shape[0] // mbc
    qkv, probs, att, mid, rp = saved
    at = lambda i: i + m0
    image_block = pl.BlockSpec((mb, seq_len, width), lambda i: (i, 0, 0))
    made_block = pl.BlockSpec((mb, seq_len, width), lambda i: (at(i), 0, 0))
    made = jax.ShapeDtypeStruct((mb * MICRO, seq_len, width), BF)
    in_specs = [
        pl.BlockSpec(memory_space=pltpu.SMEM),
        image_block,
        image_block,
        pl.BlockSpec((mb, 8, pad_len), lambda i: (at(i), 0, 0)),
        pl.BlockSpec((EXPERTS, 2, 1, CAP, width), lambda i: (0, 0, i, 0, 0)),
        pl.BlockSpec((1, rows, 3 * width), lambda i: (i, 0, 0)),
        pl.BlockSpec((1, 2, HEADS // 2, rows, pad_len), lambda i: (i, 0, 0, 0, 0)),
        pl.BlockSpec((1, rows, width), lambda i: (i, 0, 0)),
        pl.BlockSpec((1, rows, width), lambda i: (i, 0, 0)),
        pl.BlockSpec((1, rows, SMALL), lambda i: (i, 0, 0)),
        full_block(coef.shape),
        full_block(weights.shape),
        full_block(small.shape),
        full_block(extra.shape),
    ]
    args = [count, images, cotangent, meta, back, qkv, probs, att, mid, rp]
    args += [coef, weights, small, extra]
    aliases = {}
    if acc is not None:
        base = len(args)
        in_specs += [pl.BlockSpec(memory_space=pl.ANY), full_block(acc[1].shape)]
        in_specs += [pl.BlockSpec(memory_space=pl.ANY)] * 2
        args += list(acc)
        aliases = {base + 2: 0, base + 3: 1}
    sums = [(width, 4 * width), (SMALL, width)]
    pack_shape = (width, weights.shape[1])
    if own_rows == BLOCK:
        pack_shape = (CORES, width // (CORES * BLOCK), BLOCK, weights.shape[1])
    if last:
        grads = [jax.ShapeDtypeStruct(pack_shape, BF)]
        held = [pltpu.VMEM(shape, F32) for shape in sums]
        held += [pltpu.VMEM(sums[0], F32), pltpu.SemaphoreType.DMA]
    else:
        grads = [jax.ShapeDtypeStruct(shape, F32) for shape in sums]
        held = []
    return pl.pallas_call(
        functools.partial(backward_kernel, m0, seq_len, pad_len, acc is not None, last),
        grid=(mbc,),
        in_specs=in_specs,
        out_specs=[
            made_block,
            made_block,
        ]
        + [full_block(g.shape) for g in grads],
        out_shape=[
            made,
            made,
        ]
        + grads,
        scratch_shapes=[
            pltpu.VMEM((rows, width), F32),
            pltpu.VMEM((rows, width), F32),
            pltpu.VMEM((rows, 3 * width), BF),
            pltpu.VMEM((rows, SMALL), F32),
            pltpu.VMEM((SMALL, pad_len), F32),
        ]
        + held,
        input_output_aliases=aliases,
        compiler_params=pltpu.CompilerParams(vmem_limit_bytes=VMEM_LIMIT),
        cost_estimate=pl.CostEstimate(
            flops=mbc * 20 * 10**9, bytes_accessed=mbc * 10 * 10**6, transcendentals=0
        ),
        name="dense_backward",
    )(*args)


def finish_kernel(count, got_ref, bal_ref, *refs):
    experts, refs = refs[:count], refs[count:]
    qkv_ref, out_ref, router_ref, gain1_ref, bias1_ref, qv_ref, obias_ref = refs[:7]
    gain2_ref, bias2_ref, ein_ref, eout_ref, balance_ref, *refs = refs[7:]
    turned = refs[-1]
    if experts:
        in_ref, back_ref = refs[:2]
        half, wide_of = back_ref.shape[1:]
        for r, block in enumerate(experts):
            e = lax.bitwise_xor(lax.rem(lax.axis_index("dp"), EXPERTS), r)
            for c in range(half // BLOCK):
                in_ref[e, :, c * wide_of : (c + 1) * wide_of] = block[
                    c * BLOCK : (c + 1) * BLOCK, :
                ].astype(F32)
            back_ref[e] = block[half:, :].astype(F32)
    sources, rows, wide = got_ref.shape
    width = out_ref.shape[1]
    whole = got_ref[0].astype(F32)
    for source in range(1, sources):
        whole = whole + got_ref[source].astype(F32)
    qkv_ref[...] = whole[:, : 3 * width]
    out_ref[...] = whole[:, 3 * width : 4 * width]
    turned[...] = jnp.zeros_like(turned)
    turned[0:rows, :] = whole[:, 4 * width :]
    balance_ref[...] = jnp.sum(turned[0:1, :] * bal_ref[0:1, :], -1, keepdims=True)
    turned[...] = turned[...].T
    router_ref[...] = turned[0:EXPERTS, 0:rows]
    for row, ref in (
        (ROW_GAIN1, gain1_ref),
        (ROW_BIAS1, bias1_ref),
        (ROW_OBIAS, obias_ref),
        (ROW_GAIN2, gain2_ref),
        (ROW_BIAS2, bias2_ref),
    ):
        ref[...] = turned[row : row + 1, 0:rows]
    qv_ref[...] = turned[ROW_QBIAS : ROW_VBIAS + 1, 0:rows]
    eout_ref[...] = turned[ROW_EOUT : ROW_EOUT + EXPERTS, 0:rows]
    for c in range(ein_ref.shape[1] // rows):
        at = ROW_EIN + c * EXPERTS
        ein_ref[:, c * rows : (c + 1) * rows] = turned[at : at + EXPERTS, 0:rows]


def finish_call(got, bal, experts, width, ff_rows):
    rows = got.shape[1]
    shapes = [
        (rows, 3 * width),
        (rows, width),
        (EXPERTS, rows),
        (1, rows),
        (1, rows),
        (2, rows),
        (1, rows),
        (1, rows),
        (1, rows),
        (EXPERTS, ff_rows),
        (EXPERTS, rows),
        (1, 1),
    ]
    if experts:
        half = experts[0].shape[0] // 2
        shapes += [(EXPERTS, BLOCK, half // BLOCK * width), (EXPERTS, half, width)]
    vm = pl.BlockSpec(memory_space=pltpu.VMEM)
    return pl.pallas_call(
        functools.partial(finish_kernel, len(experts)),
        in_specs=[vm] * (2 + len(experts)),
        out_specs=[vm] * len(shapes),
        out_shape=[jax.ShapeDtypeStruct(shape, F32) for shape in shapes],
        scratch_shapes=[pltpu.VMEM((SMALL, SMALL), F32)],
        name="finish",
    )(got, bal, *experts)


def shards(
    total,
    images,
    image_count,
    expert_index,
    expert_slot,
    keep,
    cotangent,
    ln1_gain,
    ln1_bias,
    qkv_weight,
    qv_bias,
    out_weight,
    out_bias,
    ln2_gain,
    ln2_bias,
    router_weight,
    expert_in,
    expert_in_bias,
    expert_out,
    expert_out_bias,
):
    slots, seq_len, width = images.shape
    planes = total // EXPERTS
    rows = width // total
    ff = expert_in.shape[2]
    ff_rows = ff // total
    mb = slots // MICRO
    pad_len = -(-seq_len // 16) * 16
    plane_groups = [[z * EXPERTS + p for p in range(EXPERTS)] for z in range(planes)]
    core_groups = [
        [z * EXPERTS + c * CORES + k for c in range(CHIPS)]
        for z in range(planes)
        for k in range(CORES)
    ]
    far_groups = [[CORES * i + k for i in range(total // CORES)] for k in range(CORES)]
    chip_groups = [[CORES * i + k for k in range(CORES)] for i in range(total // CORES)]
    z_groups = [[z * EXPERTS + p for z in range(planes)] for p in range(EXPERTS)]

    def plane_swap(v):
        return lax.all_to_all(v, "dp", 0, 0, tiled=True, axis_index_groups=plane_groups)

    def z_swap(v):
        return lax.all_to_all(v, "dp", 0, 0, tiled=True, axis_index_groups=z_groups)

    def z_gather(v):
        return lax.all_gather(v, "dp", axis=0, tiled=True, axis_index_groups=z_groups)

    parts = ff // width
    if rows == BLOCK:
        expert_pack = pack_call(expert_in, expert_out)
    else:
        expert_pack = jnp.concatenate(
            [
                expert_in.reshape(EXPERTS, rows, parts, width)
                .transpose(0, 2, 1, 3)
                .reshape(EXPERTS, ff_rows, width),
                expert_out,
            ],
            1,
        )
    expert_pack = plane_swap(expert_pack)

    live_img = (jnp.arange(slots) < image_count[0]).astype(F32)
    live_tok = jnp.broadcast_to(live_img[:, None, None], (slots, seq_len, 1))
    if rows == BLOCK:
        vectors = [v[None] for v in (ln1_gain, ln1_bias, out_bias, ln2_gain, ln2_bias)]
        packed = prepare_call(
            image_count,
            expert_index.transpose(0, 2, 1),
            qkv_weight,
            out_weight,
            router_weight.T,
            vectors[0],
            vectors[1],
            qv_bias,
            *vectors[2:],
            expert_in_bias,
            expert_out_bias,
        )
    else:
        hits = (expert_index[..., None] == jnp.arange(EXPERTS)).astype(F32) * live_tok[..., None]
        local_counts = jnp.sum(hits, axis=(0, 1, 2))
        high = jnp.floor(local_counts * (1.0 / 128.0))
        told = jnp.concatenate([high, local_counts - 128.0 * high, image_count.astype(F32)])
        small_cols = jnp.concatenate(
            [
                router_weight,
                ln1_gain[:, None],
                ln1_bias[:, None],
                qv_bias.T,
                out_bias[:, None],
                ln2_gain[:, None],
                ln2_bias[:, None],
                jnp.zeros((rows, 1), BF),
                expert_in_bias.reshape(EXPERTS, parts, rows).transpose(2, 1, 0).reshape(rows, -1),
                expert_out_bias.T,
                jnp.broadcast_to(told.astype(BF)[None], (rows, 2 * EXPERTS + 1)),
            ],
            1,
        )
        small_cols = jnp.pad(small_cols, ((0, 0), (0, SMALL - small_cols.shape[1])))
        packed = jnp.concatenate([qkv_weight, out_weight, small_cols], 1)
    wide = packed.shape[1]
    if rows == BLOCK:
        pieces = [packed]
        for z in range(1, planes):
            pieces.append(
                lax.ppermute(packed, "dp", [(i, i ^ (z * EXPERTS)) for i in range(total)])
            )
        packed = jnp.concatenate(pieces, 0)
    else:
        packed = z_gather(packed)
    spans = []
    for size in CHUNKS:
        spans.append((sum(span[1] for span in spans), size))
    held = {
        m0: [v[m0 * mb : (m0 + mbc) * mb] for v in (images, cotangent)] for m0, mbc in spans
    }
    packed = jnp.broadcast_to(packed[None], (CHIPS,) + packed.shape)
    packed, expert_pack = lax.optimization_barrier((packed, expert_pack))
    first = lax.all_to_all(
        packed,
        "dp",
        0,
        0,
        tiled=True,
        axis_index_groups=core_groups,
    )
    second = lax.ppermute(first, "dp", [(i, i ^ 1) for i in range(total)])
    me = lax.axis_index("dp")
    if rows != BLOCK:
        even = me % CORES == 0
        both = jnp.stack([jnp.where(even, first, second), jnp.where(even, second, first)], 1)
        first = (
            both.reshape(CHIPS, CORES, planes, rows, wide)
            .transpose(2, 0, 1, 3, 4)
            .reshape(width, wide)
        )
        second = first[:, 4 * width :].astype(F32).T

    index_t, slot_t, keep_t = (v.transpose(0, 2, 1) for v in (expert_index, expert_slot, keep))
    target = jnp.where(keep_t == 1, index_t * CAP + slot_t, -1).astype(F32)
    live_row = jnp.broadcast_to(live_img[:, None, None], (slots, 1, seq_len))
    flags = jnp.concatenate(
        [index_t.astype(F32), keep_t.astype(F32), live_row, jnp.zeros_like(live_row)], 1
    )
    beyond = ((0, 0), (0, 0), (0, pad_len - seq_len))
    meta = jnp.concatenate(
        [jnp.pad(target, beyond, constant_values=-1.0), jnp.pad(flags, beyond)], 1
    )

    expert_pack = z_gather(expert_pack)
    if rows != BLOCK:
        blocks = width // BLOCK
        expert_pack = jnp.concatenate(
            [
                expert_pack[:, :ff_rows]
                .reshape(blocks, total // blocks, parts, rows, width)
                .transpose(0, 2, 1, 3, 4)
                .reshape(blocks, parts * BLOCK, width),
                expert_pack[:, ff_rows:].reshape(blocks, parts * BLOCK, width),
            ],
            1,
        )

    saved, sent, prob_sums = [], [], []
    for m0, mbc in spans:
        assemble = m0 == 0 and rows == BLOCK
        xd, qkv, probs, att, mid, rp, prob, *made = forward_call(
            m0, mbc, assemble, *held[m0], image_count, meta, first, second
        )
        if assemble:
            first, second = made
        saved.append((qkv, probs, att, mid, rp))
        prob_sums.append(prob[0, :EXPERTS])
        sent.append(plane_swap(xd))
    weights = first
    small, _ = lax.optimization_barrier((second, prob_sums[-1]))

    in_bias = small[AT_EIN : AT_EIN + parts * EXPERTS].reshape(parts, EXPERTS, width)
    in_bias = lax.dynamic_index_in_dim(in_bias, me % EXPERTS, 1, keepdims=False)
    in_bias = in_bias.reshape(parts, total, rows).transpose(1, 0, 2).reshape(1, ff)
    out_bias_e = lax.dynamic_slice_in_dim(small, AT_EOUT + me % EXPERTS, 1, 0)
    sums = jnp.sum(small[AT_HIGH : AT_IMAGES + 1], 1) * (1.0 / rows)
    counts_all = sums[:EXPERTS] * 128.0 + sums[EXPERTS : 2 * EXPERTS]
    live_total = sums[2 * EXPERTS] * float(seq_len)
    plane_counts = lax.dynamic_slice_in_dim(
        small[AT_IMAGES], (me // EXPERTS) * (EXPERTS * rows), EXPERTS * rows, 0
    )
    plane_counts = plane_counts.reshape(EXPERTS, rows)[:, 0].astype(jnp.int32)
    coef = jnp.pad(BALANCE_WEIGHT * EXPERTS * counts_all / live_total, (0, SMALL - EXPERTS))
    coef = jnp.broadcast_to(coef[None], (8, SMALL))
    in_bias = jnp.broadcast_to(in_bias, (8, ff))
    out_bias_e = jnp.broadcast_to(out_bias_e, (8, width))

    acc = None
    back = []
    for (m0, mbc), rows_in in zip(spans, sent):
        y, *acc = expert_call(
            m0,
            mbc,
            m0 + mbc == MICRO,
            plane_counts,
            rows_in,
            expert_pack,
            in_bias,
            out_bias_e,
            acc,
        )
        back.append(plane_swap(y))
    expert_grads, gb1, gb2 = acc

    if rows != BLOCK:
        expert_grads = jnp.concatenate(
            [
                expert_grads[:, : parts * BLOCK]
                .reshape(blocks, parts, total // blocks, rows, width)
                .transpose(0, 2, 1, 3, 4)
                .reshape(total, ff_rows, width),
                expert_grads[:, parts * BLOCK :].reshape(total, ff_rows, width),
            ],
            1,
        )
    expert_grads = lax.psum_scatter(
        expert_grads, "dp", scatter_dimension=0, tiled=True, axis_index_groups=z_groups
    )
    if rows == BLOCK:
        place = me % EXPERTS
        blocks_in = []
        for r in range(EXPERTS):
            block = lax.dynamic_index_in_dim(expert_grads, place ^ r, 0, keepdims=False)
            if r:
                block = lax.ppermute(block, "dp", [(i, i ^ r) for i in range(total)])
            blocks_in.append(block)
    else:
        blocks_in = []
        expert_grads = plane_swap(expert_grads).astype(F32)
        expert_in_grad = (
            expert_grads[:, :ff_rows]
            .reshape(EXPERTS, parts, rows, width)
            .transpose(0, 2, 1, 3)
            .reshape(EXPERTS, rows, ff)
        )
        expert_out_grad = expert_grads[:, ff_rows:]

    prob_sum = prob_sums[0]
    for piece in prob_sums[1:]:
        prob_sum = prob_sum + piece
    p_hi = prob_sum.astype(BF).astype(F32)
    mine = (jnp.arange(EXPERTS) == me % EXPERTS).astype(F32)
    e_in = gb1[0].reshape(total, parts, rows).transpose(1, 0, 2).reshape(parts, 1, width)
    extra = jnp.concatenate(
        [
            jnp.zeros((ROW_PROB, width), F32),
            jnp.broadcast_to(
                jnp.concatenate([p_hi, prob_sum - p_hi])[:, None], (2 * EXPERTS, width)
            ),
            mine[:, None] * gb2[0:1],
            (mine[None, :, None] * e_in).reshape(parts * EXPERTS, width),
            jnp.zeros((SMALL - ROW_EIN - parts * EXPERTS, width), F32),
        ],
        0,
    )

    bal = EXPERTS * counts_all / live_total / live_total
    bal = jnp.concatenate([jnp.zeros((ROW_PROB,), F32), bal, bal])
    bal = jnp.broadcast_to(jnp.pad(bal, (0, SMALL - bal.shape[0]))[None], (8, SMALL))
    extra, bal = lax.optimization_barrier((extra, bal))

    acc = None
    for (m0, mbc), returned, kept in zip(spans, back, saved):
        block_out, image_grad, *acc = backward_call(
            m0,
            mbc,
            m0 + mbc == MICRO,
            rows,
            *held[m0],
            image_count,
            meta,
            returned,
            kept,
            coef,
            weights,
            small,
            extra,
            None if acc is None else (*acc, block_out, image_grad),
        )

    grads = acc[0]
    if rows != BLOCK:
        grads = grads.reshape(total // CORES, CORES, rows, wide).transpose(1, 0, 2, 3)
    grads = lax.all_to_all(grads, "dp", 0, 0, tiled=True, axis_index_groups=chip_groups)
    grads = jnp.sum(grads.astype(F32), 0).astype(BF)
    grads = lax.all_to_all(
        grads.reshape(total // CORES, rows, wide),
        "dp",
        0,
        0,
        tiled=True,
        axis_index_groups=far_groups,
    )
    (
        qkv_grad,
        out_grad,
        router_grad,
        gain1_grad,
        bias1_grad,
        qv_grad,
        obias_grad,
        gain2_grad,
        bias2_grad,
        ein_grad,
        eout_grad,
        balance,
        *expert_pair,
    ) = finish_call(grads, bal, blocks_in, width, ff_rows)
    if blocks_in:
        expert_in_grad, expert_out_grad = expert_pair
    return (
        block_out,
        image_grad,
        balance.reshape(()),
        gain1_grad.reshape(rows),
        bias1_grad.reshape(rows),
        qkv_grad,
        qv_grad,
        out_grad,
        obias_grad.reshape(rows),
        gain2_grad.reshape(rows),
        bias2_grad.reshape(rows),
        router_grad.T,
        expert_in_grad,
        ein_grad,
        expert_out_grad,
        eout_grad,
    )


def solution(mesh):
    placed = (
        P("dp", None, None),
        P("dp"),
        P("dp", None, None),
        P("dp", None, None),
        P("dp", None, None),
        P("dp", None, None),
        P("dp"),
        P("dp"),
        P("dp", None),
        P(None, "dp"),
        P("dp", None),
        P("dp"),
        P("dp"),
        P("dp"),
        P("dp", None),
        P(None, "dp", None),
        P(None, "dp"),
        P(None, "dp", None),
        P(None, "dp"),
    )
    return jax.shard_map(
        functools.partial(shards, mesh.shape["dp"]),
        mesh=mesh,
        in_specs=placed,
        out_specs=(
            P("dp", None, None),
            P("dp", None, None),
            P(),
            P("dp"),
            P("dp"),
            P("dp", None),
            P(None, "dp"),
            P("dp", None),
            P("dp"),
            P("dp"),
            P("dp"),
            P("dp", None),
            P(None, "dp", None),
            P(None, "dp"),
            P(None, "dp", None),
            P(None, "dp"),
        ),
        check_vma=False,
    )
```

```python
import functools
import math

import jax
import jax.numpy as jnp
from jax import lax
from jax.experimental import pallas as pl
from jax.experimental.pallas import tpu as pltpu
from jax.sharding import PartitionSpec as P

HEADS = 8
HEAD_DIM = 64
EXPERTS = 8
MICRO = 4
CAP = 128
CHUNKS = (2, 2)
PAIR = 2 * HEAD_DIM
DISPATCH = 4

EPSILON = 1e-06
BALANCE_WEIGHT = 8.0

BF = jnp.bfloat16
F32 = jnp.float32

ROW_GAIN1, ROW_BIAS1, ROW_QBIAS, ROW_VBIAS, ROW_OBIAS, ROW_GAIN2, ROW_BIAS2 = range(8, 15)
SMALL = 128
ROW_PROB, ROW_EOUT, ROW_EIN = 16, 32, 40
AT_EIN, AT_EOUT, AT_HIGH, AT_LOW, AT_IMAGES = 16, 48, 56, 64, 72
CORES = 2
CHIPS = EXPERTS // CORES
BLOCK = 16
COL_T0, COL_T1, COL_R0, COL_R1, COL_K0, COL_K1, COL_LIVE = range(7)
VMEM_LIMIT = 60 * 1024 * 1024


def mm(a, b):
    return lax.dot_general(a, b, (((1,), (0,)), ((), ())), preferred_element_type=F32)


def mm_nt(a, b):
    return lax.dot_general(a, b, (((1,), (1,)), ((), ())), preferred_element_type=F32)


def mm_tn(a, b):
    return lax.dot_general(a, b, (((0,), (0,)), ((), ())), preferred_element_type=F32)


def load_padded(dst, src, seq_len, pad_len):
    for i in range(2):
        tail = (seq_len // 16) * 16
        dst[i * pad_len + tail : (i + 1) * pad_len, :] = jnp.zeros(
            (pad_len - tail, dst.shape[1]), dst.dtype
        )
        dst[i * pad_len : i * pad_len + seq_len, :] = src[i].astype(dst.dtype)


def load_table(facts, table, meta_ref, pad_len):
    for i in range(2):
        table[0 : meta_ref.shape[1], :] = meta_ref[i]
        facts[i * pad_len : (i + 1) * pad_len, :] = table[...].T


def norm_parts(x):
    mean = jnp.mean(x, -1, keepdims=True)
    centered = x - mean
    spread = jnp.mean(centered * centered, -1, keepdims=True)
    inv = lax.rsqrt(spread + EPSILON)
    return centered * inv, inv


def norm_back(d_out, xhat, inv, gain):
    d_hat = d_out * gain
    first = jnp.mean(d_hat, -1, keepdims=True)
    second = jnp.mean(d_hat * xhat, -1, keepdims=True)
    return inv * (d_hat - first - xhat * second)


def half_masks():
    lane = lax.broadcasted_iota(jnp.int32, (1, PAIR), 1)
    low = jnp.where(lane < HEAD_DIM, 1.0, 0.0)
    return low.astype(BF), (1.0 - low).astype(BF), lane < HEAD_DIM


def stack_heads(block, low, high):
    return jnp.concatenate([block * low, block * high], 0)


def forward_kernel(
    m0,
    seq_len,
    pad_len,
    assemble,
    cnt_ref,
    img_ref,
    cot_ref,
    meta_ref,
    first_ref,
    second_ref,
    xd_ref,
    qkv_ref,
    p_ref,
    att_ref,
    mid_ref,
    rp_ref,
    psum_ref,
    *rest,
):
    if assemble:
        w_ref, small_ref, xs, cs, facts, table = rest
    else:
        w_ref, small_ref = first_ref, second_ref
        xs, cs, facts, table = rest
    step = pl.program_id(0)
    width = xs.shape[1]
    alive = cnt_ref[0] > 2 * (m0 + step)

    @pl.when(step == 0)
    def _():
        psum_ref[...] = jnp.zeros_like(psum_ref)
        table[...] = jnp.zeros_like(table)
        if assemble:
            core = lax.rem(lax.axis_index("dp"), CORES)
            for ref, owner in ((first_ref, core), (second_ref, 1 - core)):
                for chip in range(CHIPS):
                    for z in range(ref.shape[1] // BLOCK):
                        plane = lax.bitwise_xor(lax.axis_index("dp") // EXPERTS, z)
                        at = plane * EXPERTS + chip * CORES + owner
                        at = pl.multiple_of(at * BLOCK, BLOCK)
                        w_ref[pl.ds(at, BLOCK), :] = ref[chip, z * BLOCK : (z + 1) * BLOCK, :]
            small_ref[...] = w_ref[:, 4 * width :].astype(F32).T

    @pl.when(jnp.logical_not(alive))
    def _():
        xd_ref[...] = jnp.zeros_like(xd_ref)

    @pl.when(alive)
    def _():
        load_padded(xs, img_ref, seq_len, pad_len)
        load_padded(cs, cot_ref, seq_len, pad_len)
        load_table(facts, table, meta_ref, pad_len)
        xhat, inv = norm_parts(xs[...])
        normed = (
            xhat * small_ref[ROW_GAIN1 : ROW_GAIN1 + 1, :] + small_ref[ROW_BIAS1 : ROW_BIAS1 + 1, :]
        ).astype(BF)
        for part, row in ((0, ROW_QBIAS), (1, None), (2, ROW_VBIAS)):
            cols = slice(part * width, (part + 1) * width)
            value = mm(normed, w_ref[:, cols])
            if row is not None:
                value = value + small_ref[row : row + 1, :]
            qkv_ref[0, :, cols] = value.astype(BF)
        low, high, low_mask = half_masks()
        key_ok = lax.broadcasted_iota(jnp.int32, (1, pad_len), 1) < seq_len
        for i in range(2):
            rows = slice(i * pad_len, (i + 1) * pad_len)
            for hp in range(HEADS // 2):
                at = hp * PAIR
                q = qkv_ref[0, rows, at : at + PAIR]
                k = qkv_ref[0, rows, width + at : width + at + PAIR]
                v = qkv_ref[0, rows, 2 * width + at : 2 * width + at + PAIR]
                s = mm_nt(stack_heads(q, low, high), k) * (HEAD_DIM**-0.5)
                s = jnp.where(key_ok, s, -1e30)
                e = jnp.exp(s - jnp.max(s, -1, keepdims=True))
                p = (e * (1.0 / jnp.sum(e, -1, keepdims=True))).astype(BF)
                p_ref[0, i, hp] = p
                o = mm(p, v)
                att_ref[0, rows, at : at + PAIR] = jnp.where(
                    low_mask, o[:pad_len], o[pad_len:]
                ).astype(BF)
        middle = (
            xs[...]
            + mm(att_ref[0], w_ref[:, 3 * width : 4 * width])
            + small_ref[ROW_OBIAS : ROW_OBIAS + 1, :]
        )
        mid_ref[0] = middle
        xhat2, inv2 = norm_parts(middle)
        mixed = (
            xhat2 * small_ref[ROW_GAIN2 : ROW_GAIN2 + 1, :]
            + small_ref[ROW_BIAS2 : ROW_BIAS2 + 1, :]
        ).astype(BF)
        logits = mm(mixed, w_ref[:, 4 * width : 4 * width + SMALL])
        lane = lax.broadcasted_iota(jnp.int32, (1, SMALL), 1)
        logits = jnp.where(lane < EXPERTS, logits, -1e30)
        e = jnp.exp(logits - jnp.max(logits, -1, keepdims=True))
        rp = e * (1.0 / jnp.sum(e, -1, keepdims=True))
        rp_ref[0] = rp
        live = facts[:, COL_LIVE : COL_LIVE + 1]
        psum_ref[0:1, :] += jnp.sum(rp * live, 0, keepdims=True)
        d_final = cs[...] * live
        lane_f = lane.astype(F32)
        weighted = []
        for route, kept in ((COL_R0, COL_K0), (COL_R1, COL_K1)):
            hot = lane_f == facts[:, route : route + 1]
            gate = jnp.sum(jnp.where(hot, rp, 0.0), -1, keepdims=True)
            gate = gate * facts[:, kept : kept + 1]
            weighted.append((gate * d_final).astype(BF))
        slot = lax.broadcasted_iota(jnp.int32, (DISPATCH * CAP, 1), 0).astype(F32)
        targets = facts[...].T
        for e_id in range(0, EXPERTS, DISPATCH):
            here = slot + float(e_id * CAP)
            sel0 = jnp.where(here == targets[COL_T0 : COL_T0 + 1, :], 1.0, 0.0)
            sel1 = jnp.where(here == targets[COL_T1 : COL_T1 + 1, :], 1.0, 0.0)
            shape = (DISPATCH, CAP, width)
            at = slice(e_id, e_id + DISPATCH)
            xd_ref[at, 0, 0] = mm((sel0 + sel1).astype(BF), mixed).astype(BF).reshape(shape)
            xd_ref[at, 1, 0] = (
                (mm(sel0.astype(BF), weighted[0]) + mm(sel1.astype(BF), weighted[1]))
                .astype(BF)
                .reshape(shape)
            )


def full_block(shape):
    return pl.BlockSpec(shape, lambda i: (0,) * len(shape))


def pack_kernel(in_ref, out_ref, pack_ref):
    width = out_ref.shape[2]
    half = out_ref.shape[1]
    for c in range(half // BLOCK):
        pack_ref[:, c * BLOCK : (c + 1) * BLOCK, :] = in_ref[:, :, c * width : (c + 1) * width]
    pack_ref[:, half:, :] = out_ref[...]


def pack_call(expert_in, expert_out):
    vm = pl.BlockSpec(memory_space=pltpu.VMEM)
    shape = (expert_out.shape[0], 2 * expert_out.shape[1], expert_out.shape[2])
    return pl.pallas_call(
        pack_kernel,
        in_specs=[vm] * 2,
        out_specs=vm,
        out_shape=jax.ShapeDtypeStruct(shape, BF),
        name="pack",
    )(expert_in, expert_out)


def prepare_kernel(
    cnt_ref,
    index_ref,
    qkv_ref,
    out_ref,
    router_ref,
    gain1_ref,
    bias1_ref,
    qv_ref,
    obias_ref,
    gain2_ref,
    bias2_ref,
    ein_ref,
    eout_ref,
    packed_ref,
    turned,
):
    rows, width = out_ref.shape
    packed_ref[:, 0 : 3 * width] = qkv_ref[...]
    packed_ref[:, 3 * width : 4 * width] = out_ref[...]
    turned[...] = jnp.zeros_like(turned)
    turned[0:EXPERTS, 0:rows] = router_ref[...].astype(F32)
    for row, ref in (
        (ROW_GAIN1, gain1_ref),
        (ROW_BIAS1, bias1_ref),
        (ROW_OBIAS, obias_ref),
        (ROW_GAIN2, gain2_ref),
        (ROW_BIAS2, bias2_ref),
    ):
        turned[row : row + 1, 0:rows] = ref[...].astype(F32)
    turned[ROW_QBIAS : ROW_VBIAS + 1, 0:rows] = qv_ref[...].astype(F32)
    turned[AT_EOUT : AT_EOUT + EXPERTS, 0:rows] = eout_ref[...].astype(F32)
    ein = ein_ref[...].astype(F32)
    for c in range(ein.shape[1] // rows):
        at = AT_EIN + c * EXPERTS
        turned[at : at + EXPERTS, 0:rows] = ein[:, c * rows : (c + 1) * rows]
    slots, top, seq_len = index_ref.shape
    chosen = index_ref[...]
    slot = lax.broadcasted_iota(jnp.int32, (slots, top, seq_len), 0)
    chosen = jnp.where(slot < cnt_ref[0], chosen, -1)
    for e in range(EXPERTS):
        hits = jnp.where(chosen == e, 1.0, 0.0)
        hits = jnp.sum(jnp.sum(hits, 0), -1, keepdims=True)
        hits = jnp.sum(hits, 0, keepdims=True)
        high = jnp.floor(hits * (1.0 / 128.0))
        turned[AT_HIGH + e : AT_HIGH + e + 1, :] = jnp.broadcast_to(high, (1, SMALL))
        turned[AT_LOW + e : AT_LOW + e + 1, :] = jnp.broadcast_to(hits - 128.0 * high, (1, SMALL))
    turned[AT_IMAGES : AT_IMAGES + 1, :] = jnp.full((1, SMALL), cnt_ref[0].astype(F32))
    turned[...] = turned[...].T
    packed_ref[:, 4 * width :] = turned[0:rows, :].astype(BF)


def prepare_call(count, *args):
    vm = pl.BlockSpec(memory_space=pltpu.VMEM)
    rows, width = args[2].shape
    return pl.pallas_call(
        prepare_kernel,
        in_specs=[pl.BlockSpec(memory_space=pltpu.SMEM)] + [vm] * len(args),
        out_specs=vm,
        out_shape=jax.ShapeDtypeStruct((rows, 4 * width + SMALL), BF),
        scratch_shapes=[pltpu.VMEM((SMALL, SMALL), F32)],
        name="prepare",
    )(count, *args)


def forward_call(m0, mbc, assemble, images, cotangent, count, meta, weights, small):
    seq_len, width = images.shape[1], images.shape[2]
    pad_len = meta.shape[2]
    rows = 2 * pad_len
    at = lambda i: i + m0
    mb = images.shape[0] // mbc
    made_here = []
    if assemble:
        made_here = [
            jax.ShapeDtypeStruct((width, weights.shape[2]), BF),
            jax.ShapeDtypeStruct((SMALL, width), F32),
        ]
    return pl.pallas_call(
        functools.partial(forward_kernel, m0, seq_len, pad_len, assemble),
        grid=(mbc,),
        in_specs=[
            pl.BlockSpec(memory_space=pltpu.SMEM),
            pl.BlockSpec((mb, seq_len, width), lambda i: (i, 0, 0)),
            pl.BlockSpec((mb, seq_len, width), lambda i: (i, 0, 0)),
            pl.BlockSpec((mb, 8, pad_len), lambda i: (at(i), 0, 0)),
            full_block(weights.shape),
            full_block(small.shape),
        ],
        out_specs=[
            pl.BlockSpec((EXPERTS, 2, 1, CAP, width), lambda i: (0, 0, i, 0, 0)),
            pl.BlockSpec((1, rows, 3 * width), lambda i: (i, 0, 0)),
            pl.BlockSpec((1, 2, HEADS // 2, rows, pad_len), lambda i: (i, 0, 0, 0, 0)),
            pl.BlockSpec((1, rows, width), lambda i: (i, 0, 0)),
            pl.BlockSpec((1, rows, width), lambda i: (i, 0, 0)),
            pl.BlockSpec((1, rows, SMALL), lambda i: (i, 0, 0)),
            full_block((8, SMALL)),
        ]
        + [full_block(made.shape) for made in made_here],
        out_shape=[
            jax.ShapeDtypeStruct((EXPERTS, 2, mbc, CAP, width), BF),
            jax.ShapeDtypeStruct((mbc, rows, 3 * width), BF),
            jax.ShapeDtypeStruct((mbc, 2, HEADS // 2, rows, pad_len), BF),
            jax.ShapeDtypeStruct((mbc, rows, width), BF),
            jax.ShapeDtypeStruct((mbc, rows, width), F32),
            jax.ShapeDtypeStruct((mbc, rows, SMALL), F32),
            jax.ShapeDtypeStruct((8, SMALL), F32),
        ]
        + made_here,
        scratch_shapes=[
            pltpu.VMEM((rows, width), F32),
            pltpu.VMEM((rows, width), F32),
            pltpu.VMEM((rows, SMALL), F32),
            pltpu.VMEM((SMALL, pad_len), F32),
        ],
        compiler_params=pltpu.CompilerParams(vmem_limit_bytes=VMEM_LIMIT),
        cost_estimate=pl.CostEstimate(
            flops=mbc * 8 * 10**9, bytes_accessed=mbc * 10 * 10**6, transcendentals=0
        ),
        name="dense_forward",
    )(count, images, cotangent, meta, weights, small)


GROUP = 4


def expert_kernel(
    m0,
    mbc,
    has_acc,
    last,
    cnt_ref,
    x_ref,
    w_ref,
    b1_ref,
    b2_ref,
    *rest,
):
    if has_acc:
        a1_ref, a2_ref, ab1_ref, ab2_ref = rest[:4]
        rest = rest[4:]
    if last:
        y_ref, pack_ref, gb1_ref, gb2_ref, s1, s2, order, xin, din, xout, dout = rest
    else:
        y_ref, s1, s2, gb1_ref, gb2_ref, order, xin, din, xout, dout = rest
    width = x_ref.shape[-1]
    ff = b1_ref.shape[1]
    half = w_ref.shape[1] // 2
    per_tile = width // half
    if has_acc:
        s1[...] = a1_ref[...]
        s2[...] = a2_ref[...]
        gb1_ref[...] = ab1_ref[...]
        gb2_ref[...] = ab2_ref[...]
    else:
        s1[...] = jnp.zeros_like(s1)
        s2[...] = jnp.zeros_like(s2)
        gb1_ref[...] = jnp.zeros_like(gb1_ref)
        gb2_ref[...] = jnp.zeros_like(gb2_ref)
    blocks = EXPERTS * mbc

    def is_live(b):
        return (cnt_ref[b // mbc] > 2 * (m0 + b % mbc)).astype(jnp.int32)

    live_total = jnp.int32(0)
    for b in range(blocks):
        live_total = live_total + is_live(b)
    head, tail = jnp.int32(0), live_total
    for b in range(blocks):
        flag = is_live(b)
        order[jnp.where(flag == 1, head, tail)] = b
        head = head + flag
        tail = tail + (1 - flag)

    def one_group(g, carry):
        for j in range(GROUP):
            b = order[g * GROUP + j]
            xin[j * CAP : (j + 1) * CAP, :] = x_ref[b // mbc, 0, b % mbc]
            din[j * CAP : (j + 1) * CAP, :] = x_ref[b // mbc, 1, b % mbc]
        rows_in, d_res = xin[...], din[...]
        gb2_ref[0:1, :] += jnp.sum(d_res.astype(F32), 0, keepdims=True)
        for f in range(ff // width):
            cols = slice(f * width, (f + 1) * width)
            w1 = w_ref[:, f * BLOCK : (f + 1) * BLOCK, :].reshape(width, width)
            w2 = w_ref[f * per_tile : (f + 1) * per_tile, half:, :].reshape(width, width)
            h = mm(rows_in, w1) + b1_ref[0:1, cols]
            bell = jnp.exp(-0.5 * h * h)
            t = 1.0 / (1.0 + (0.3275911 / math.sqrt(2.0)) * jnp.abs(h))
            poly = t * (
                0.5 * 0.254829592
                + t
                * (
                    0.5 * -0.284496736
                    + t * (0.5 * 1.421413741 + t * (0.5 * -1.453152027 + t * (0.5 * 1.061405429)))
                )
            )
            upper = poly * bell
            cdf = jnp.where(h < 0.0, upper, 1.0 - upper)
            act = (h * cdf).astype(BF)
            slope = cdf + h * bell * (1.0 / math.sqrt(2.0 * math.pi))
            d_act = mm_nt(d_res, w2)
            d_hid_f = (d_act * slope).astype(BF)
            gb1_ref[0:1, cols] += jnp.sum(d_hid_f.astype(F32), 0, keepdims=True)
            res = mm(act, w2)
            d_rows = mm_nt(d_hid_f, w1)
            if f == 0:
                xout[...] = res
                dout[...] = d_rows
            else:
                xout[...] += res
                dout[...] += d_rows
            s1[:, cols] += mm_tn(rows_in, d_hid_f)
            s2[cols, :] += mm_tn(act, d_res)
        for j in range(GROUP):
            b = order[g * GROUP + j]
            y_ref[b // mbc, 0, b % mbc] = (
                xout[j * CAP : (j + 1) * CAP, :] + b2_ref[0:1, :]
            ).astype(BF)
            y_ref[b // mbc, 1, b % mbc] = dout[j * CAP : (j + 1) * CAP, :].astype(BF)
        return carry

    lax.fori_loop(0, (live_total + GROUP - 1) // GROUP, one_group, 0)
    if last:
        blocks_of = width // BLOCK
        for f in range(ff // width):
            tile = s1[:, f * width : (f + 1) * width].astype(BF)
            pack_ref[:, f * BLOCK : (f + 1) * BLOCK, :] = tile.reshape(blocks_of, BLOCK, width)
        pack_ref[:, half:, :] = s2[...].astype(BF).reshape(blocks_of, half, width)


def expert_call(m0, mbc, last, counts, x, weights, b1, b2, acc):
    width, ff = weights.shape[2], b1.shape[1]
    if last:
        grads = [jax.ShapeDtypeStruct(weights.shape, BF)]
    else:
        grads = [jax.ShapeDtypeStruct((width, ff), F32), jax.ShapeDtypeStruct((ff, width), F32)]
    vm = pl.BlockSpec(memory_space=pltpu.VMEM)
    scratch = []
    if last:
        scratch += [pltpu.VMEM((width, ff), F32), pltpu.VMEM((ff, width), F32)]
    scratch += [
        pltpu.SMEM((EXPERTS * mbc,), jnp.int32),
        pltpu.VMEM((GROUP * CAP, width), BF),
        pltpu.VMEM((GROUP * CAP, width), BF),
        pltpu.VMEM((GROUP * CAP, width), F32),
        pltpu.VMEM((GROUP * CAP, width), F32),
    ]
    return pl.pallas_call(
        functools.partial(expert_kernel, m0, mbc, acc is not None, last),
        in_specs=[pl.BlockSpec(memory_space=pltpu.SMEM)] + [vm] * (4 + (0 if acc is None else 4)),
        out_specs=[vm] * (len(grads) + 3),
        out_shape=[
            jax.ShapeDtypeStruct(x.shape, BF),
            *grads,
            jax.ShapeDtypeStruct((8, ff), F32),
            jax.ShapeDtypeStruct((8, width), F32),
        ],
        scratch_shapes=scratch,
        compiler_params=pltpu.CompilerParams(vmem_limit_bytes=VMEM_LIMIT),
        cost_estimate=pl.CostEstimate(
            flops=mbc * 20 * 10**9, bytes_accessed=mbc * 10 * 10**6, transcendentals=0
        ),
        name="expert_both",
    )(counts, x, weights, b1, b2, *(() if acc is None else acc))


def backward_kernel(
    m0,
    seq_len,
    pad_len,
    has_acc,
    last,
    cnt_ref,
    img_ref,
    cot_ref,
    meta_ref,
    y_ref,
    qkv_hbm,
    p_hbm,
    att_ref,
    mid_ref,
    rp_ref,
    coef_ref,
    w_hbm,
    small_ref,
    extra_ref,
    *rest,
):
    if has_acc:
        accw_ref, accs_ref = rest[:2]
        rest = rest[4:]
    if last:
        out_ref, grad_ref, pack_ref, *rest = rest
        gw_ref, gs_ref, earlier, sem = rest[-4:]
        rest = rest[:-4]
    else:
        out_ref, grad_ref, gw_ref, gs_ref, *rest = rest
    xs, cs, dq, facts, table, qkv_all, p_all, w_ref, sems = rest
    step = pl.program_id(0)
    width = xs.shape[1]
    alive = cnt_ref[0] > 2 * (m0 + step)
    qkv_ref, p_ref = qkv_all.at[pl.ds(step, 1)], p_all.at[pl.ds(step, 1)]
    steps = qkv_all.shape[0]

    def late(which, at):
        if which == "rest":
            cols = pl.ds(3 * width, width + SMALL)
            return pltpu.make_async_copy(w_hbm.at[:, cols], w_ref.at[:, cols], sems.at[2 * steps])
        if which == "first":
            cols = pl.ds(0, 3 * width)
            return pltpu.make_async_copy(
                w_hbm.at[:, cols], w_ref.at[:, cols], sems.at[2 * steps + 1]
            )
        if which == "qkv":
            return pltpu.make_async_copy(qkv_hbm.at[at], qkv_all.at[at], sems.at[at])
        return pltpu.make_async_copy(p_hbm.at[at], p_all.at[at], sems.at[steps + at])


    @pl.when(step == 0)
    def _():
        late("rest", 0).start()
        for at in range(steps):
            late("qkv", at).start()
            late("p", at).start()
        late("first", 0).start()
        table[...] = jnp.zeros_like(table)
        gw_ref[...] = jnp.zeros_like(gw_ref)
        if has_acc:
            pltpu.make_async_copy(accw_ref, earlier, sem).start()
            gs_ref[...] = accs_ref[...]
        else:
            gs_ref[...] = jnp.zeros_like(gs_ref)

    @pl.when(jnp.logical_not(alive))
    def _():
        out_ref[...] = jnp.zeros_like(out_ref)
        grad_ref[...] = jnp.zeros_like(grad_ref)
        late("qkv", step).wait()
        late("p", step).wait()

        @pl.when(step == 0)
        def _():
            late("rest", 0).wait()
            late("first", 0).wait()

    def add_row(row, value):
        gs_ref[row : row + 1, :] += jnp.sum(value, 0, keepdims=True)

    @pl.when(alive)
    def _():
        load_padded(xs, img_ref, seq_len, pad_len)
        load_padded(cs, cot_ref, seq_len, pad_len)
        load_table(facts, table, meta_ref, pad_len)
        rows = xs.shape[0]
        live = facts[:, COL_LIVE : COL_LIVE + 1]
        d_final = cs[...] * live
        middle = mid_ref[0]
        rp = rp_ref[0]
        lane = lax.broadcasted_iota(jnp.int32, (1, SMALL), 1)
        lane_f = lane.astype(F32)
        slot = lax.broadcasted_iota(jnp.int32, (1, EXPERTS * CAP), 1).astype(F32)
        res = y_ref[:, 0, 0].reshape(EXPERTS * CAP, width)
        d_rows = y_ref[:, 1, 0].reshape(EXPERTS * CAP, width)
        final = middle
        d_prob = coef_ref[0:1, :] * live
        sel_all = None
        for target, route, kept in ((COL_T0, COL_R0, COL_K0), (COL_T1, COL_R1, COL_K1)):
            sel = jnp.where(slot == facts[:, target : target + 1], 1.0, 0.0).astype(BF)
            sel_all = sel if sel_all is None else sel_all + sel
            picked = mm(sel, res)
            keep = facts[:, kept : kept + 1]
            hot = lane_f == facts[:, route : route + 1]
            gate = jnp.sum(jnp.where(hot, rp, 0.0), -1, keepdims=True) * keep
            final = final + gate * picked
            d_gate = jnp.sum(picked * d_final, -1, keepdims=True) * keep
            d_prob = d_prob + jnp.where(hot, d_gate, 0.0)
        final = final * live
        for i in range(2):
            out_ref[i] = final[i * pad_len : i * pad_len + seq_len, :].astype(BF)
        d_mixed = mm(sel_all, d_rows)

        @pl.when(step == 0)
        def _():
            late("rest", 0).wait()

        d_logits = (rp * (d_prob - jnp.sum(rp * d_prob, -1, keepdims=True))).astype(BF)
        d_mixed = d_mixed + mm_nt(d_logits, w_ref[:, 4 * width : 4 * width + SMALL])
        gain2 = small_ref[ROW_GAIN2 : ROW_GAIN2 + 1, :]
        xhat2, inv2 = norm_parts(middle)
        mixed = (xhat2 * gain2 + small_ref[ROW_BIAS2 : ROW_BIAS2 + 1, :]).astype(BF)
        gs_ref[0:EXPERTS, :] += mm_tn(d_logits, mixed)[0:EXPERTS, :]
        add_row(ROW_GAIN2, d_mixed * xhat2)
        add_row(ROW_BIAS2, d_mixed)
        d_middle = d_final + norm_back(d_mixed, xhat2, inv2, gain2)
        add_row(ROW_OBIAS, d_middle)
        cs[...] = d_middle
        d_branch = d_middle.astype(BF)
        gw_ref[:, 3 * width : 4 * width] += mm_tn(att_ref[0], d_branch)
        d_att_all = mm_nt(d_branch, w_ref[:, 3 * width : 4 * width]).astype(BF)
        late("qkv", step).wait()
        late("p", step).wait()
        low, high, low_mask = half_masks()
        scale = HEAD_DIM**-0.5
        for i in range(2):
            span = slice(i * pad_len, (i + 1) * pad_len)
            for hp in range(HEADS // 2):
                at = hp * PAIR
                q = qkv_ref[0, span, at : at + PAIR]
                k = qkv_ref[0, span, width + at : width + at + PAIR]
                v = qkv_ref[0, span, 2 * width + at : 2 * width + at + PAIR]
                d_att = stack_heads(d_att_all[span, at : at + PAIR], low, high)
                p = p_ref[0, i, hp]
                pf = p.astype(F32)
                d_attn = mm_nt(d_att, v)
                d_s = (pf * (d_attn - jnp.sum(pf * d_attn, -1, keepdims=True))).astype(BF)
                d_v = mm_tn(p, d_att)
                d_k = mm_tn(d_s, stack_heads(q, low, high)) * scale
                d_q = mm(d_s, k) * scale
                dq[span, at : at + PAIR] = jnp.where(
                    low_mask, d_q[:pad_len], d_q[pad_len:]
                ).astype(BF)
                dq[span, width + at : width + at + PAIR] = d_k.astype(BF)
                dq[span, 2 * width + at : 2 * width + at + PAIR] = d_v.astype(BF)
        gain1 = small_ref[ROW_GAIN1 : ROW_GAIN1 + 1, :]
        xhat, inv = norm_parts(xs[...])
        normed = (xhat * gain1 + small_ref[ROW_BIAS1 : ROW_BIAS1 + 1, :]).astype(BF)
        add_row(ROW_QBIAS, dq[:, 0:width].astype(F32))
        add_row(ROW_VBIAS, dq[:, 2 * width : 3 * width].astype(F32))
        gw_ref[:, 0 : 3 * width] += mm_tn(normed, dq[...])

        @pl.when(step == 0)
        def _():
            late("first", 0).wait()

        d_normed = mm_nt(dq[...], w_ref[:, 0 : 3 * width])
        add_row(ROW_GAIN1, d_normed * xhat)
        add_row(ROW_BIAS1, d_normed)
        d_tok = cs[...] + norm_back(d_normed, xhat, inv, gain1)
        for i in range(2):
            grad_ref[i] = d_tok[i * pad_len : i * pad_len + seq_len, :].astype(BF)

    if last:

        @pl.when(step == pl.num_programs(0) - 1)
        def _():
            if has_acc:
                pltpu.make_async_copy(accw_ref, earlier, sem).wait()
                gw_ref[...] += earlier[...]
            small_part = (gs_ref[...] + extra_ref[...]).T.astype(BF)
            for b in range(width // BLOCK):
                at = slice(b * BLOCK, (b + 1) * BLOCK)
                core = b % CORES
                if len(pack_ref.shape) == 4:
                    ref = pack_ref.at[core, b // CORES]
                else:
                    ref = pack_ref.at[at]
                ref[:, 0 : 4 * width] = gw_ref[at, :].astype(BF)
                ref[:, 4 * width :] = small_part[at, :]


def backward_call(
    m0,
    mbc,
    last,
    own_rows,
    images,
    cotangent,
    count,
    meta,
    back,
    saved,
    coef,
    weights,
    small,
    extra,
    acc,
):
    seq_len, width = images.shape[1], images.shape[2]
    pad_len = meta.shape[2]
    rows = 2 * pad_len
    mb = images.shape[0] // mbc
    qkv, probs, att, mid, rp = saved
    at = lambda i: i + m0
    image_block = pl.BlockSpec((mb, seq_len, width), lambda i: (i, 0, 0))
    made_block = pl.BlockSpec((mb, seq_len, width), lambda i: (at(i), 0, 0))
    made = jax.ShapeDtypeStruct((mb * MICRO, seq_len, width), BF)
    in_specs = [
        pl.BlockSpec(memory_space=pltpu.SMEM),
        image_block,
        image_block,
        pl.BlockSpec((mb, 8, pad_len), lambda i: (at(i), 0, 0)),
        pl.BlockSpec((EXPERTS, 2, 1, CAP, width), lambda i: (0, 0, i, 0, 0)),
        pl.BlockSpec(memory_space=pl.ANY),
        pl.BlockSpec(memory_space=pl.ANY),
        pl.BlockSpec((1, rows, width), lambda i: (i, 0, 0)),
        pl.BlockSpec((1, rows, width), lambda i: (i, 0, 0)),
        pl.BlockSpec((1, rows, SMALL), lambda i: (i, 0, 0)),
        full_block(coef.shape),
        pl.BlockSpec(memory_space=pl.ANY),
        full_block(small.shape),
        full_block(extra.shape),
    ]
    args = [count, images, cotangent, meta, back, qkv, probs, att, mid, rp]
    args += [coef, weights, small, extra]
    aliases = {}
    if acc is not None:
        base = len(args)
        in_specs += [pl.BlockSpec(memory_space=pl.ANY), full_block(acc[1].shape)]
        in_specs += [pl.BlockSpec(memory_space=pl.ANY)] * 2
        args += list(acc)
        aliases = {base + 2: 0, base + 3: 1}
    sums = [(width, 4 * width), (SMALL, width)]
    pack_shape = (width, weights.shape[1])
    if own_rows == BLOCK:
        pack_shape = (CORES, width // (CORES * BLOCK), BLOCK, weights.shape[1])
    if last:
        grads = [jax.ShapeDtypeStruct(pack_shape, BF)]
        held = [pltpu.VMEM(shape, F32) for shape in sums]
        held += [pltpu.VMEM(sums[0], F32), pltpu.SemaphoreType.DMA]
    else:
        grads = [jax.ShapeDtypeStruct(shape, F32) for shape in sums]
        held = []
    return pl.pallas_call(
        functools.partial(backward_kernel, m0, seq_len, pad_len, acc is not None, last),
        grid=(mbc,),
        in_specs=in_specs,
        out_specs=[
            made_block,
            made_block,
        ]
        + [full_block(g.shape) for g in grads],
        out_shape=[
            made,
            made,
        ]
        + grads,
        scratch_shapes=[
            pltpu.VMEM((rows, width), F32),
            pltpu.VMEM((rows, width), F32),
            pltpu.VMEM((rows, 3 * width), BF),
            pltpu.VMEM((rows, SMALL), F32),
            pltpu.VMEM((SMALL, pad_len), F32),
            pltpu.VMEM(qkv.shape, BF),
            pltpu.VMEM(probs.shape, BF),
            pltpu.VMEM(weights.shape, BF),
            pltpu.SemaphoreType.DMA((2 * mbc + 2,)),
        ]
        + held,
        input_output_aliases=aliases,
        compiler_params=pltpu.CompilerParams(vmem_limit_bytes=VMEM_LIMIT),
        cost_estimate=pl.CostEstimate(
            flops=mbc * 20 * 10**9, bytes_accessed=mbc * 10 * 10**6, transcendentals=0
        ),
        name="dense_backward",
    )(*args)


def finish_kernel(count, got_ref, bal_ref, *refs):
    experts, refs = refs[:count], refs[count:]
    qkv_ref, out_ref, router_ref, gain1_ref, bias1_ref, qv_ref, obias_ref = refs[:7]
    gain2_ref, bias2_ref, ein_ref, eout_ref, balance_ref, *refs = refs[7:]
    turned = refs[-1]
    if experts:
        in_ref, back_ref = refs[:2]
        half, wide_of = back_ref.shape[1:]
        for r, block in enumerate(experts):
            e = lax.bitwise_xor(lax.rem(lax.axis_index("dp"), EXPERTS), r)
            for c in range(half // BLOCK):
                in_ref[e, :, c * wide_of : (c + 1) * wide_of] = block[
                    c * BLOCK : (c + 1) * BLOCK, :
                ].astype(F32)
            back_ref[e] = block[half:, :].astype(F32)
    sources, rows, wide = got_ref.shape
    width = out_ref.shape[1]
    whole = got_ref[0].astype(F32)
    for source in range(1, sources):
        whole = whole + got_ref[source].astype(F32)
    qkv_ref[...] = whole[:, : 3 * width]
    out_ref[...] = whole[:, 3 * width : 4 * width]
    turned[...] = jnp.zeros_like(turned)
    turned[0:rows, :] = whole[:, 4 * width :]
    balance_ref[...] = jnp.sum(turned[0:1, :] * bal_ref[0:1, :], -1, keepdims=True)
    turned[...] = turned[...].T
    router_ref[...] = turned[0:EXPERTS, 0:rows]
    for row, ref in (
        (ROW_GAIN1, gain1_ref),
        (ROW_BIAS1, bias1_ref),
        (ROW_OBIAS, obias_ref),
        (ROW_GAIN2, gain2_ref),
        (ROW_BIAS2, bias2_ref),
    ):
        ref[...] = turned[row : row + 1, 0:rows]
    qv_ref[...] = turned[ROW_QBIAS : ROW_VBIAS + 1, 0:rows]
    eout_ref[...] = turned[ROW_EOUT : ROW_EOUT + EXPERTS, 0:rows]
    for c in range(ein_ref.shape[1] // rows):
        at = ROW_EIN + c * EXPERTS
        ein_ref[:, c * rows : (c + 1) * rows] = turned[at : at + EXPERTS, 0:rows]


def finish_call(got, bal, experts, width, ff_rows):
    rows = got.shape[1]
    shapes = [
        (rows, 3 * width),
        (rows, width),
        (EXPERTS, rows),
        (1, rows),
        (1, rows),
        (2, rows),
        (1, rows),
        (1, rows),
        (1, rows),
        (EXPERTS, ff_rows),
        (EXPERTS, rows),
        (1, 1),
    ]
    if experts:
        half = experts[0].shape[0] // 2
        shapes += [(EXPERTS, BLOCK, half // BLOCK * width), (EXPERTS, half, width)]
    vm = pl.BlockSpec(memory_space=pltpu.VMEM)
    return pl.pallas_call(
        functools.partial(finish_kernel, len(experts)),
        in_specs=[vm] * (2 + len(experts)),
        out_specs=[vm] * len(shapes),
        out_shape=[jax.ShapeDtypeStruct(shape, F32) for shape in shapes],
        scratch_shapes=[pltpu.VMEM((SMALL, SMALL), F32)],
        name="finish",
    )(got, bal, *experts)


def shards(
    total,
    images,
    image_count,
    expert_index,
    expert_slot,
    keep,
    cotangent,
    ln1_gain,
    ln1_bias,
    qkv_weight,
    qv_bias,
    out_weight,
    out_bias,
    ln2_gain,
    ln2_bias,
    router_weight,
    expert_in,
    expert_in_bias,
    expert_out,
    expert_out_bias,
):
    slots, seq_len, width = images.shape
    planes = total // EXPERTS
    rows = width // total
    ff = expert_in.shape[2]
    ff_rows = ff // total
    mb = slots // MICRO
    pad_len = -(-seq_len // 16) * 16
    plane_groups = [[z * EXPERTS + p for p in range(EXPERTS)] for z in range(planes)]
    core_groups = [
        [z * EXPERTS + c * CORES + k for c in range(CHIPS)]
        for z in range(planes)
        for k in range(CORES)
    ]
    far_groups = [[CORES * i + k for i in range(total // CORES)] for k in range(CORES)]
    chip_groups = [[CORES * i + k for k in range(CORES)] for i in range(total // CORES)]
    z_groups = [[z * EXPERTS + p for z in range(planes)] for p in range(EXPERTS)]

    def plane_swap(v):
        return lax.all_to_all(v, "dp", 0, 0, tiled=True, axis_index_groups=plane_groups)

    def z_swap(v):
        return lax.all_to_all(v, "dp", 0, 0, tiled=True, axis_index_groups=z_groups)

    def z_gather(v):
        return lax.all_gather(v, "dp", axis=0, tiled=True, axis_index_groups=z_groups)

    parts = ff // width
    if rows == BLOCK:
        expert_pack = pack_call(expert_in, expert_out)
    else:
        expert_pack = jnp.concatenate(
            [
                expert_in.reshape(EXPERTS, rows, parts, width)
                .transpose(0, 2, 1, 3)
                .reshape(EXPERTS, ff_rows, width),
                expert_out,
            ],
            1,
        )
    expert_pack = plane_swap(expert_pack)

    live_img = (jnp.arange(slots) < image_count[0]).astype(F32)
    live_tok = jnp.broadcast_to(live_img[:, None, None], (slots, seq_len, 1))
    if rows == BLOCK:
        vectors = [v[None] for v in (ln1_gain, ln1_bias, out_bias, ln2_gain, ln2_bias)]
        packed = prepare_call(
            image_count,
            expert_index.transpose(0, 2, 1),
            qkv_weight,
            out_weight,
            router_weight.T,
            vectors[0],
            vectors[1],
            qv_bias,
            *vectors[2:],
            expert_in_bias,
            expert_out_bias,
        )
    else:
        hits = (expert_index[..., None] == jnp.arange(EXPERTS)).astype(F32) * live_tok[..., None]
        local_counts = jnp.sum(hits, axis=(0, 1, 2))
        high = jnp.floor(local_counts * (1.0 / 128.0))
        told = jnp.concatenate([high, local_counts - 128.0 * high, image_count.astype(F32)])
        small_cols = jnp.concatenate(
            [
                router_weight,
                ln1_gain[:, None],
                ln1_bias[:, None],
                qv_bias.T,
                out_bias[:, None],
                ln2_gain[:, None],
                ln2_bias[:, None],
                jnp.zeros((rows, 1), BF),
                expert_in_bias.reshape(EXPERTS, parts, rows).transpose(2, 1, 0).reshape(rows, -1),
                expert_out_bias.T,
                jnp.broadcast_to(told.astype(BF)[None], (rows, 2 * EXPERTS + 1)),
            ],
            1,
        )
        small_cols = jnp.pad(small_cols, ((0, 0), (0, SMALL - small_cols.shape[1])))
        packed = jnp.concatenate([qkv_weight, out_weight, small_cols], 1)
    wide = packed.shape[1]
    if rows == BLOCK:
        pieces = [packed]
        for z in range(1, planes):
            pieces.append(
                lax.ppermute(packed, "dp", [(i, i ^ (z * EXPERTS)) for i in range(total)])
            )
        packed = jnp.concatenate(pieces, 0)
    else:
        packed = z_gather(packed)
    spans = []
    for size in CHUNKS:
        spans.append((sum(span[1] for span in spans), size))
    held = {
        m0: [v[m0 * mb : (m0 + mbc) * mb] for v in (images, cotangent)] for m0, mbc in spans
    }
    packed = jnp.broadcast_to(packed[None], (CHIPS,) + packed.shape)
    packed, expert_pack = lax.optimization_barrier((packed, expert_pack))
    first = lax.all_to_all(
        packed,
        "dp",
        0,
        0,
        tiled=True,
        axis_index_groups=core_groups,
    )
    second = lax.ppermute(first, "dp", [(i, i ^ 1) for i in range(total)])
    me = lax.axis_index("dp")
    if rows != BLOCK:
        even = me % CORES == 0
        both = jnp.stack([jnp.where(even, first, second), jnp.where(even, second, first)], 1)
        first = (
            both.reshape(CHIPS, CORES, planes, rows, wide)
            .transpose(2, 0, 1, 3, 4)
            .reshape(width, wide)
        )
        second = first[:, 4 * width :].astype(F32).T

    index_t, slot_t, keep_t = (v.transpose(0, 2, 1) for v in (expert_index, expert_slot, keep))
    target = jnp.where(keep_t == 1, index_t * CAP + slot_t, -1).astype(F32)
    live_row = jnp.broadcast_to(live_img[:, None, None], (slots, 1, seq_len))
    flags = jnp.concatenate(
        [index_t.astype(F32), keep_t.astype(F32), live_row, jnp.zeros_like(live_row)], 1
    )
    beyond = ((0, 0), (0, 0), (0, pad_len - seq_len))
    meta = jnp.concatenate(
        [jnp.pad(target, beyond, constant_values=-1.0), jnp.pad(flags, beyond)], 1
    )

    expert_pack = z_gather(expert_pack)
    if rows != BLOCK:
        blocks = width // BLOCK
        expert_pack = jnp.concatenate(
            [
                expert_pack[:, :ff_rows]
                .reshape(blocks, total // blocks, parts, rows, width)
                .transpose(0, 2, 1, 3, 4)
                .reshape(blocks, parts * BLOCK, width),
                expert_pack[:, ff_rows:].reshape(blocks, parts * BLOCK, width),
            ],
            1,
        )

    saved, sent, prob_sums = [], [], []
    for m0, mbc in spans:
        assemble = m0 == 0 and rows == BLOCK
        xd, qkv, probs, att, mid, rp, prob, *made = forward_call(
            m0, mbc, assemble, *held[m0], image_count, meta, first, second
        )
        if assemble:
            first, second = made
        saved.append((qkv, probs, att, mid, rp))
        prob_sums.append(prob[0, :EXPERTS])
        sent.append(plane_swap(xd))
    weights = first
    small, _ = lax.optimization_barrier((second, prob_sums[-1]))

    in_bias = small[AT_EIN : AT_EIN + parts * EXPERTS].reshape(parts, EXPERTS, width)
    in_bias = lax.dynamic_index_in_dim(in_bias, me % EXPERTS, 1, keepdims=False)
    in_bias = in_bias.reshape(parts, total, rows).transpose(1, 0, 2).reshape(1, ff)
    out_bias_e = lax.dynamic_slice_in_dim(small, AT_EOUT + me % EXPERTS, 1, 0)
    sums = jnp.sum(small[AT_HIGH : AT_IMAGES + 1], 1) * (1.0 / rows)
    counts_all = sums[:EXPERTS] * 128.0 + sums[EXPERTS : 2 * EXPERTS]
    live_total = sums[2 * EXPERTS] * float(seq_len)
    plane_counts = lax.dynamic_slice_in_dim(
        small[AT_IMAGES], (me // EXPERTS) * (EXPERTS * rows), EXPERTS * rows, 0
    )
    plane_counts = plane_counts.reshape(EXPERTS, rows)[:, 0].astype(jnp.int32)
    coef = jnp.pad(BALANCE_WEIGHT * EXPERTS * counts_all / live_total, (0, SMALL - EXPERTS))
    coef = jnp.broadcast_to(coef[None], (8, SMALL))
    in_bias = jnp.broadcast_to(in_bias, (8, ff))
    out_bias_e = jnp.broadcast_to(out_bias_e, (8, width))

    acc = None
    back = []
    for (m0, mbc), rows_in in zip(spans, sent):
        y, *acc = expert_call(
            m0,
            mbc,
            m0 + mbc == MICRO,
            plane_counts,
            rows_in,
            expert_pack,
            in_bias,
            out_bias_e,
            acc,
        )
        back.append(plane_swap(y))
    expert_grads, gb1, gb2 = acc

    if rows != BLOCK:
        expert_grads = jnp.concatenate(
            [
                expert_grads[:, : parts * BLOCK]
                .reshape(blocks, parts, total // blocks, rows, width)
                .transpose(0, 2, 1, 3, 4)
                .reshape(total, ff_rows, width),
                expert_grads[:, parts * BLOCK :].reshape(total, ff_rows, width),
            ],
            1,
        )
    expert_grads = lax.psum_scatter(
        expert_grads, "dp", scatter_dimension=0, tiled=True, axis_index_groups=z_groups
    )
    if rows == BLOCK:
        place = me % EXPERTS
        blocks_in = []
        for r in range(EXPERTS):
            block = lax.dynamic_index_in_dim(expert_grads, place ^ r, 0, keepdims=False)
            if r:
                block = lax.ppermute(block, "dp", [(i, i ^ r) for i in range(total)])
            blocks_in.append(block)
    else:
        blocks_in = []
        expert_grads = plane_swap(expert_grads).astype(F32)
        expert_in_grad = (
            expert_grads[:, :ff_rows]
            .reshape(EXPERTS, parts, rows, width)
            .transpose(0, 2, 1, 3)
            .reshape(EXPERTS, rows, ff)
        )
        expert_out_grad = expert_grads[:, ff_rows:]

    prob_sum = prob_sums[0]
    for piece in prob_sums[1:]:
        prob_sum = prob_sum + piece
    p_hi = prob_sum.astype(BF).astype(F32)
    mine = (jnp.arange(EXPERTS) == me % EXPERTS).astype(F32)
    e_in = gb1[0].reshape(total, parts, rows).transpose(1, 0, 2).reshape(parts, 1, width)
    extra = jnp.concatenate(
        [
            jnp.zeros((ROW_PROB, width), F32),
            jnp.broadcast_to(
                jnp.concatenate([p_hi, prob_sum - p_hi])[:, None], (2 * EXPERTS, width)
            ),
            mine[:, None] * gb2[0:1],
            (mine[None, :, None] * e_in).reshape(parts * EXPERTS, width),
            jnp.zeros((SMALL - ROW_EIN - parts * EXPERTS, width), F32),
        ],
        0,
    )

    bal = EXPERTS * counts_all / live_total / live_total
    bal = jnp.concatenate([jnp.zeros((ROW_PROB,), F32), bal, bal])
    bal = jnp.broadcast_to(jnp.pad(bal, (0, SMALL - bal.shape[0]))[None], (8, SMALL))
    extra, bal = lax.optimization_barrier((extra, bal))

    acc = None
    for (m0, mbc), returned, kept in zip(spans, back, saved):
        block_out, image_grad, *acc = backward_call(
            m0,
            mbc,
            m0 + mbc == MICRO,
            rows,
            *held[m0],
            image_count,
            meta,
            returned,
            kept,
            coef,
            weights,
            small,
            extra,
            None if acc is None else (*acc, block_out, image_grad),
        )

    grads = acc[0]
    if rows != BLOCK:
        grads = grads.reshape(total // CORES, CORES, rows, wide).transpose(1, 0, 2, 3)
    grads = lax.all_to_all(grads, "dp", 0, 0, tiled=True, axis_index_groups=chip_groups)
    grads = jnp.sum(grads.astype(F32), 0).astype(BF)
    grads = lax.all_to_all(
        grads.reshape(total // CORES, rows, wide),
        "dp",
        0,
        0,
        tiled=True,
        axis_index_groups=far_groups,
    )
    (
        qkv_grad,
        out_grad,
        router_grad,
        gain1_grad,
        bias1_grad,
        qv_grad,
        obias_grad,
        gain2_grad,
        bias2_grad,
        ein_grad,
        eout_grad,
        balance,
        *expert_pair,
    ) = finish_call(grads, bal, blocks_in, width, ff_rows)
    if blocks_in:
        expert_in_grad, expert_out_grad = expert_pair
    return (
        block_out,
        image_grad,
        balance.reshape(()),
        gain1_grad.reshape(rows),
        bias1_grad.reshape(rows),
        qkv_grad,
        qv_grad,
        out_grad,
        obias_grad.reshape(rows),
        gain2_grad.reshape(rows),
        bias2_grad.reshape(rows),
        router_grad.T,
        expert_in_grad,
        ein_grad,
        expert_out_grad,
        eout_grad,
    )


def solution(mesh):
    placed = (
        P("dp", None, None),
        P("dp"),
        P("dp", None, None),
        P("dp", None, None),
        P("dp", None, None),
        P("dp", None, None),
        P("dp"),
        P("dp"),
        P("dp", None),
        P(None, "dp"),
        P("dp", None),
        P("dp"),
        P("dp"),
        P("dp"),
        P("dp", None),
        P(None, "dp", None),
        P(None, "dp"),
        P(None, "dp", None),
        P(None, "dp"),
    )
    return jax.shard_map(
        functools.partial(shards, mesh.shape["dp"]),
        mesh=mesh,
        in_specs=placed,
        out_specs=(
            P("dp", None, None),
            P("dp", None, None),
            P(),
            P("dp"),
            P("dp"),
            P("dp", None),
            P(None, "dp"),
            P("dp", None),
            P("dp"),
            P("dp"),
            P("dp"),
            P("dp", None),
            P(None, "dp", None),
            P(None, "dp"),
            P(None, "dp", None),
            P(None, "dp"),
        ),
        check_vma=False,
    )
```

```python
import functools
import math

import jax
import jax.numpy as jnp
from jax import lax
from jax.experimental import pallas as pl
from jax.experimental.pallas import tpu as pltpu
from jax.sharding import PartitionSpec as P

HEADS = 8
HEAD_DIM = 64
EXPERTS = 8
MICRO = 4
CAP = 128
CHUNKS = (2, 2)
PAIR = 2 * HEAD_DIM
DISPATCH = 8

EPSILON = 1e-06
BALANCE_WEIGHT = 8.0

BF = jnp.bfloat16
F32 = jnp.float32

ROW_GAIN1, ROW_BIAS1, ROW_QBIAS, ROW_VBIAS, ROW_OBIAS, ROW_GAIN2, ROW_BIAS2 = range(8, 15)
SMALL = 128
ROW_PROB, ROW_EOUT, ROW_EIN = 16, 32, 40
AT_EIN, AT_EOUT, AT_HIGH, AT_LOW, AT_IMAGES = 16, 48, 56, 64, 72
CORES = 2
CHIPS = EXPERTS // CORES
BLOCK = 16
COL_T0, COL_T1, COL_R0, COL_R1, COL_K0, COL_K1, COL_LIVE = range(7)
VMEM_LIMIT = 60 * 1024 * 1024


def mm(a, b):
    return lax.dot_general(a, b, (((1,), (0,)), ((), ())), preferred_element_type=F32)


def mm_nt(a, b):
    return lax.dot_general(a, b, (((1,), (1,)), ((), ())), preferred_element_type=F32)


def mm_tn(a, b):
    return lax.dot_general(a, b, (((0,), (0,)), ((), ())), preferred_element_type=F32)


def load_padded(dst, src, seq_len, pad_len):
    for i in range(2):
        tail = (seq_len // 16) * 16
        dst[i * pad_len + tail : (i + 1) * pad_len, :] = jnp.zeros(
            (pad_len - tail, dst.shape[1]), dst.dtype
        )
        dst[i * pad_len : i * pad_len + seq_len, :] = src[i].astype(dst.dtype)


def load_table(facts, table, meta_ref, pad_len):
    for i in range(2):
        table[0 : meta_ref.shape[1], :] = meta_ref[i]
        facts[i * pad_len : (i + 1) * pad_len, :] = table[...].T


def norm_parts(x):
    mean = jnp.mean(x, -1, keepdims=True)
    centered = x - mean
    spread = jnp.mean(centered * centered, -1, keepdims=True)
    inv = lax.rsqrt(spread + EPSILON)
    return centered * inv, inv


def norm_back(d_out, xhat, inv, gain):
    d_hat = d_out * gain
    first = jnp.mean(d_hat, -1, keepdims=True)
    second = jnp.mean(d_hat * xhat, -1, keepdims=True)
    return inv * (d_hat - first - xhat * second)


def half_masks():
    lane = lax.broadcasted_iota(jnp.int32, (1, PAIR), 1)
    low = jnp.where(lane < HEAD_DIM, 1.0, 0.0)
    return low.astype(BF), (1.0 - low).astype(BF), lane < HEAD_DIM


def stack_heads(block, low, high):
    return jnp.concatenate([block * low, block * high], 0)


def forward_kernel(
    m0,
    seq_len,
    pad_len,
    assemble,
    cnt_ref,
    img_ref,
    cot_ref,
    meta_ref,
    first_ref,
    second_ref,
    xd_ref,
    qkv_ref,
    p_ref,
    att_ref,
    mid_ref,
    rp_ref,
    psum_ref,
    *rest,
):
    if assemble:
        w_ref, small_ref, xs, cs, facts, table = rest
    else:
        w_ref, small_ref = first_ref, second_ref
        xs, cs, facts, table = rest
    step = pl.program_id(0)
    width = xs.shape[1]
    alive = cnt_ref[0] > 2 * (m0 + step)

    @pl.when(step == 0)
    def _():
        psum_ref[...] = jnp.zeros_like(psum_ref)
        table[...] = jnp.zeros_like(table)
        if assemble:
            core = lax.rem(lax.axis_index("dp"), CORES)
            for ref, owner in ((first_ref, core), (second_ref, 1 - core)):
                for chip in range(CHIPS):
                    for z in range(ref.shape[1] // BLOCK):
                        plane = lax.bitwise_xor(lax.axis_index("dp") // EXPERTS, z)
                        at = plane * EXPERTS + chip * CORES + owner
                        at = pl.multiple_of(at * BLOCK, BLOCK)
                        w_ref[pl.ds(at, BLOCK), :] = ref[chip, z * BLOCK : (z + 1) * BLOCK, :]
            small_ref[...] = w_ref[:, 4 * width :].astype(F32).T

    @pl.when(jnp.logical_not(alive))
    def _():
        xd_ref[...] = jnp.zeros_like(xd_ref)

    @pl.when(alive)
    def _():
        load_padded(xs, img_ref, seq_len, pad_len)
        load_padded(cs, cot_ref, seq_len, pad_len)
        load_table(facts, table, meta_ref, pad_len)
        xhat, inv = norm_parts(xs[...])
        normed = (
            xhat * small_ref[ROW_GAIN1 : ROW_GAIN1 + 1, :] + small_ref[ROW_BIAS1 : ROW_BIAS1 + 1, :]
        ).astype(BF)
        for part, row in ((0, ROW_QBIAS), (1, None), (2, ROW_VBIAS)):
            cols = slice(part * width, (part + 1) * width)
            value = mm(normed, w_ref[:, cols])
            if row is not None:
                value = value + small_ref[row : row + 1, :]
            qkv_ref[0, :, cols] = value.astype(BF)
        low, high, low_mask = half_masks()
        key_ok = lax.broadcasted_iota(jnp.int32, (1, pad_len), 1) < seq_len
        for i in range(2):
            rows = slice(i * pad_len, (i + 1) * pad_len)
            for hp in range(HEADS // 2):
                at = hp * PAIR
                q = qkv_ref[0, rows, at : at + PAIR]
                k = qkv_ref[0, rows, width + at : width + at + PAIR]
                v = qkv_ref[0, rows, 2 * width + at : 2 * width + at + PAIR]
                s = mm_nt(stack_heads(q, low, high), k) * (HEAD_DIM**-0.5)
                s = jnp.where(key_ok, s, -1e30)
                e = jnp.exp(s - jnp.max(s, -1, keepdims=True))
                p = (e * (1.0 / jnp.sum(e, -1, keepdims=True))).astype(BF)
                p_ref[0, i, hp] = p
                o = mm(p, v)
                att_ref[0, rows, at : at + PAIR] = jnp.where(
                    low_mask, o[:pad_len], o[pad_len:]
                ).astype(BF)
        middle = (
            xs[...]
            + mm(att_ref[0], w_ref[:, 3 * width : 4 * width])
            + small_ref[ROW_OBIAS : ROW_OBIAS + 1, :]
        )
        mid_ref[0] = middle
        xhat2, inv2 = norm_parts(middle)
        mixed = (
            xhat2 * small_ref[ROW_GAIN2 : ROW_GAIN2 + 1, :]
            + small_ref[ROW_BIAS2 : ROW_BIAS2 + 1, :]
        ).astype(BF)
        logits = mm(mixed, w_ref[:, 4 * width : 4 * width + SMALL])
        lane = lax.broadcasted_iota(jnp.int32, (1, SMALL), 1)
        logits = jnp.where(lane < EXPERTS, logits, -1e30)
        e = jnp.exp(logits - jnp.max(logits, -1, keepdims=True))
        rp = e * (1.0 / jnp.sum(e, -1, keepdims=True))
        rp_ref[0] = rp
        live = facts[:, COL_LIVE : COL_LIVE + 1]
        psum_ref[0:1, :] += jnp.sum(rp * live, 0, keepdims=True)
        d_final = cs[...] * live
        lane_f = lane.astype(F32)
        weighted = []
        for route, kept in ((COL_R0, COL_K0), (COL_R1, COL_K1)):
            hot = lane_f == facts[:, route : route + 1]
            gate = jnp.sum(jnp.where(hot, rp, 0.0), -1, keepdims=True)
            gate = gate * facts[:, kept : kept + 1]
            weighted.append((gate * d_final).astype(BF))
        slot = lax.broadcasted_iota(jnp.int32, (DISPATCH * CAP, 1), 0).astype(F32)
        targets = facts[...].T
        for e_id in range(0, EXPERTS, DISPATCH):
            here = slot + float(e_id * CAP)
            sel0 = jnp.where(here == targets[COL_T0 : COL_T0 + 1, :], 1.0, 0.0)
            sel1 = jnp.where(here == targets[COL_T1 : COL_T1 + 1, :], 1.0, 0.0)
            shape = (DISPATCH, CAP, width)
            at = slice(e_id, e_id + DISPATCH)
            xd_ref[at, 0, 0] = mm((sel0 + sel1).astype(BF), mixed).astype(BF).reshape(shape)
            xd_ref[at, 1, 0] = (
                (mm(sel0.astype(BF), weighted[0]) + mm(sel1.astype(BF), weighted[1]))
                .astype(BF)
                .reshape(shape)
            )


def full_block(shape):
    return pl.BlockSpec(shape, lambda i: (0,) * len(shape))


def pack_kernel(in_ref, out_ref, pack_ref):
    width = out_ref.shape[2]
    half = out_ref.shape[1]
    for c in range(half // BLOCK):
        pack_ref[:, c * BLOCK : (c + 1) * BLOCK, :] = in_ref[:, :, c * width : (c + 1) * width]
    pack_ref[:, half:, :] = out_ref[...]


def pack_call(expert_in, expert_out):
    vm = pl.BlockSpec(memory_space=pltpu.VMEM)
    shape = (expert_out.shape[0], 2 * expert_out.shape[1], expert_out.shape[2])
    return pl.pallas_call(
        pack_kernel,
        in_specs=[vm] * 2,
        out_specs=vm,
        out_shape=jax.ShapeDtypeStruct(shape, BF),
        name="pack",
    )(expert_in, expert_out)


def prepare_kernel(
    cnt_ref,
    index_ref,
    qkv_ref,
    out_ref,
    router_ref,
    gain1_ref,
    bias1_ref,
    qv_ref,
    obias_ref,
    gain2_ref,
    bias2_ref,
    ein_ref,
    eout_ref,
    packed_ref,
    turned,
):
    rows, width = out_ref.shape
    packed_ref[:, 0 : 3 * width] = qkv_ref[...]
    packed_ref[:, 3 * width : 4 * width] = out_ref[...]
    turned[...] = jnp.zeros_like(turned)
    turned[0:EXPERTS, 0:rows] = router_ref[...].astype(F32)
    for row, ref in (
        (ROW_GAIN1, gain1_ref),
        (ROW_BIAS1, bias1_ref),
        (ROW_OBIAS, obias_ref),
        (ROW_GAIN2, gain2_ref),
        (ROW_BIAS2, bias2_ref),
    ):
        turned[row : row + 1, 0:rows] = ref[...].astype(F32)
    turned[ROW_QBIAS : ROW_VBIAS + 1, 0:rows] = qv_ref[...].astype(F32)
    turned[AT_EOUT : AT_EOUT + EXPERTS, 0:rows] = eout_ref[...].astype(F32)
    ein = ein_ref[...].astype(F32)
    for c in range(ein.shape[1] // rows):
        at = AT_EIN + c * EXPERTS
        turned[at : at + EXPERTS, 0:rows] = ein[:, c * rows : (c + 1) * rows]
    slots, top, seq_len = index_ref.shape
    chosen = index_ref[...]
    slot = lax.broadcasted_iota(jnp.int32, (slots, top, seq_len), 0)
    chosen = jnp.where(slot < cnt_ref[0], chosen, -1)
    for e in range(EXPERTS):
        hits = jnp.where(chosen == e, 1.0, 0.0)
        hits = jnp.sum(jnp.sum(hits, 0), -1, keepdims=True)
        hits = jnp.sum(hits, 0, keepdims=True)
        high = jnp.floor(hits * (1.0 / 128.0))
        turned[AT_HIGH + e : AT_HIGH + e + 1, :] = jnp.broadcast_to(high, (1, SMALL))
        turned[AT_LOW + e : AT_LOW + e + 1, :] = jnp.broadcast_to(hits - 128.0 * high, (1, SMALL))
    turned[AT_IMAGES : AT_IMAGES + 1, :] = jnp.full((1, SMALL), cnt_ref[0].astype(F32))
    turned[...] = turned[...].T
    packed_ref[:, 4 * width :] = turned[0:rows, :].astype(BF)


def prepare_call(count, *args):
    vm = pl.BlockSpec(memory_space=pltpu.VMEM)
    rows, width = args[2].shape
    return pl.pallas_call(
        prepare_kernel,
        in_specs=[pl.BlockSpec(memory_space=pltpu.SMEM)] + [vm] * len(args),
        out_specs=vm,
        out_shape=jax.ShapeDtypeStruct((rows, 4 * width + SMALL), BF),
        scratch_shapes=[pltpu.VMEM((SMALL, SMALL), F32)],
        name="prepare",
    )(count, *args)


def forward_call(m0, mbc, assemble, images, cotangent, count, meta, weights, small):
    seq_len, width = images.shape[1], images.shape[2]
    pad_len = meta.shape[2]
    rows = 2 * pad_len
    at = lambda i: i + m0
    mb = images.shape[0] // mbc
    made_here = []
    if assemble:
        made_here = [
            jax.ShapeDtypeStruct((width, weights.shape[2]), BF),
            jax.ShapeDtypeStruct((SMALL, width), F32),
        ]
    return pl.pallas_call(
        functools.partial(forward_kernel, m0, seq_len, pad_len, assemble),
        grid=(mbc,),
        in_specs=[
            pl.BlockSpec(memory_space=pltpu.SMEM),
            pl.BlockSpec((mb, seq_len, width), lambda i: (i, 0, 0)),
            pl.BlockSpec((mb, seq_len, width), lambda i: (i, 0, 0)),
            pl.BlockSpec((mb, 8, pad_len), lambda i: (at(i), 0, 0)),
            full_block(weights.shape),
            full_block(small.shape),
        ],
        out_specs=[
            pl.BlockSpec((EXPERTS, 2, 1, CAP, width), lambda i: (0, 0, i, 0, 0)),
            pl.BlockSpec((1, rows, 3 * width), lambda i: (i, 0, 0)),
            pl.BlockSpec((1, 2, HEADS // 2, rows, pad_len), lambda i: (i, 0, 0, 0, 0)),
            pl.BlockSpec((1, rows, width), lambda i: (i, 0, 0)),
            pl.BlockSpec((1, rows, width), lambda i: (i, 0, 0)),
            pl.BlockSpec((1, rows, SMALL), lambda i: (i, 0, 0)),
            full_block((8, SMALL)),
        ]
        + [full_block(made.shape) for made in made_here],
        out_shape=[
            jax.ShapeDtypeStruct((EXPERTS, 2, mbc, CAP, width), BF),
            jax.ShapeDtypeStruct((mbc, rows, 3 * width), BF),
            jax.ShapeDtypeStruct((mbc, 2, HEADS // 2, rows, pad_len), BF),
            jax.ShapeDtypeStruct((mbc, rows, width), BF),
            jax.ShapeDtypeStruct((mbc, rows, width), F32),
            jax.ShapeDtypeStruct((mbc, rows, SMALL), F32),
            jax.ShapeDtypeStruct((8, SMALL), F32),
        ]
        + made_here,
        scratch_shapes=[
            pltpu.VMEM((rows, width), F32),
            pltpu.VMEM((rows, width), F32),
            pltpu.VMEM((rows, SMALL), F32),
            pltpu.VMEM((SMALL, pad_len), F32),
        ],
        compiler_params=pltpu.CompilerParams(vmem_limit_bytes=VMEM_LIMIT),
        cost_estimate=pl.CostEstimate(
            flops=mbc * 8 * 10**9, bytes_accessed=mbc * 10 * 10**6, transcendentals=0
        ),
        name="dense_forward",
    )(count, images, cotangent, meta, weights, small)


GROUP = 4


def expert_kernel(
    m0,
    mbc,
    has_acc,
    last,
    cnt_ref,
    x_ref,
    w_ref,
    b1_ref,
    b2_ref,
    *rest,
):
    if has_acc:
        a1_ref, a2_ref, ab1_ref, ab2_ref = rest[:4]
        rest = rest[4:]
    if last:
        y_ref, pack_ref, gb1_ref, gb2_ref, s1, s2, order, xin, din, xout, dout = rest
    else:
        y_ref, s1, s2, gb1_ref, gb2_ref, order, xin, din, xout, dout = rest
    width = x_ref.shape[-1]
    ff = b1_ref.shape[1]
    half = w_ref.shape[1] // 2
    per_tile = width // half
    if has_acc:
        s1[...] = a1_ref[...]
        s2[...] = a2_ref[...]
        gb1_ref[...] = ab1_ref[...]
        gb2_ref[...] = ab2_ref[...]
    else:
        s1[...] = jnp.zeros_like(s1)
        s2[...] = jnp.zeros_like(s2)
        gb1_ref[...] = jnp.zeros_like(gb1_ref)
        gb2_ref[...] = jnp.zeros_like(gb2_ref)
    blocks = EXPERTS * mbc

    def is_live(b):
        return (cnt_ref[b // mbc] > 2 * (m0 + b % mbc)).astype(jnp.int32)

    live_total = jnp.int32(0)
    for b in range(blocks):
        live_total = live_total + is_live(b)
    head, tail = jnp.int32(0), live_total
    for b in range(blocks):
        flag = is_live(b)
        order[jnp.where(flag == 1, head, tail)] = b
        head = head + flag
        tail = tail + (1 - flag)

    def one_group(g, carry):
        for j in range(GROUP):
            b = order[g * GROUP + j]
            xin[j * CAP : (j + 1) * CAP, :] = x_ref[b // mbc, 0, b % mbc]
            din[j * CAP : (j + 1) * CAP, :] = x_ref[b // mbc, 1, b % mbc]
        rows_in, d_res = xin[...], din[...]
        gb2_ref[0:1, :] += jnp.sum(d_res.astype(F32), 0, keepdims=True)
        for f in range(ff // width):
            cols = slice(f * width, (f + 1) * width)
            w1 = w_ref[:, f * BLOCK : (f + 1) * BLOCK, :].reshape(width, width)
            w2 = w_ref[f * per_tile : (f + 1) * per_tile, half:, :].reshape(width, width)
            h = mm(rows_in, w1) + b1_ref[0:1, cols]
            bell = jnp.exp(-0.5 * h * h)
            t = 1.0 / (1.0 + (0.3275911 / math.sqrt(2.0)) * jnp.abs(h))
            poly = t * (
                0.5 * 0.254829592
                + t
                * (
                    0.5 * -0.284496736
                    + t * (0.5 * 1.421413741 + t * (0.5 * -1.453152027 + t * (0.5 * 1.061405429)))
                )
            )
            upper = poly * bell
            cdf = jnp.where(h < 0.0, upper, 1.0 - upper)
            act = (h * cdf).astype(BF)
            slope = cdf + h * bell * (1.0 / math.sqrt(2.0 * math.pi))
            d_act = mm_nt(d_res, w2)
            d_hid_f = (d_act * slope).astype(BF)
            gb1_ref[0:1, cols] += jnp.sum(d_hid_f.astype(F32), 0, keepdims=True)
            res = mm(act, w2)
            d_rows = mm_nt(d_hid_f, w1)
            if f == 0:
                xout[...] = res
                dout[...] = d_rows
            else:
                xout[...] += res
                dout[...] += d_rows
            s1[:, cols] += mm_tn(rows_in, d_hid_f)
            s2[cols, :] += mm_tn(act, d_res)
        for j in range(GROUP):
            b = order[g * GROUP + j]
            y_ref[b // mbc, 0, b % mbc] = (
                xout[j * CAP : (j + 1) * CAP, :] + b2_ref[0:1, :]
            ).astype(BF)
            y_ref[b // mbc, 1, b % mbc] = dout[j * CAP : (j + 1) * CAP, :].astype(BF)
        return carry

    lax.fori_loop(0, (live_total + GROUP - 1) // GROUP, one_group, 0)
    if last:
        blocks_of = width // BLOCK
        for f in range(ff // width):
            tile = s1[:, f * width : (f + 1) * width].astype(BF)
            pack_ref[:, f * BLOCK : (f + 1) * BLOCK, :] = tile.reshape(blocks_of, BLOCK, width)
        pack_ref[:, half:, :] = s2[...].astype(BF).reshape(blocks_of, half, width)


def expert_call(m0, mbc, last, counts, x, weights, b1, b2, acc):
    width, ff = weights.shape[2], b1.shape[1]
    if last:
        grads = [jax.ShapeDtypeStruct(weights.shape, BF)]
    else:
        grads = [jax.ShapeDtypeStruct((width, ff), F32), jax.ShapeDtypeStruct((ff, width), F32)]
    vm = pl.BlockSpec(memory_space=pltpu.VMEM)
    scratch = []
    if last:
        scratch += [pltpu.VMEM((width, ff), F32), pltpu.VMEM((ff, width), F32)]
    scratch += [
        pltpu.SMEM((EXPERTS * mbc,), jnp.int32),
        pltpu.VMEM((GROUP * CAP, width), BF),
        pltpu.VMEM((GROUP * CAP, width), BF),
        pltpu.VMEM((GROUP * CAP, width), F32),
        pltpu.VMEM((GROUP * CAP, width), F32),
    ]
    return pl.pallas_call(
        functools.partial(expert_kernel, m0, mbc, acc is not None, last),
        in_specs=[pl.BlockSpec(memory_space=pltpu.SMEM)] + [vm] * (4 + (0 if acc is None else 4)),
        out_specs=[vm] * (len(grads) + 3),
        out_shape=[
            jax.ShapeDtypeStruct(x.shape, BF),
            *grads,
            jax.ShapeDtypeStruct((8, ff), F32),
            jax.ShapeDtypeStruct((8, width), F32),
        ],
        scratch_shapes=scratch,
        compiler_params=pltpu.CompilerParams(vmem_limit_bytes=VMEM_LIMIT),
        cost_estimate=pl.CostEstimate(
            flops=mbc * 20 * 10**9, bytes_accessed=mbc * 10 * 10**6, transcendentals=0
        ),
        name="expert_both",
    )(counts, x, weights, b1, b2, *(() if acc is None else acc))


def backward_kernel(
    m0,
    seq_len,
    pad_len,
    has_acc,
    last,
    cnt_ref,
    img_ref,
    cot_ref,
    meta_ref,
    y_ref,
    qkv_hbm,
    p_hbm,
    att_ref,
    mid_ref,
    rp_ref,
    coef_ref,
    w_hbm,
    small_ref,
    extra_ref,
    *rest,
):
    if has_acc:
        accw_ref, accs_ref = rest[:2]
        rest = rest[4:]
    if last:
        out_ref, grad_ref, pack_ref, *rest = rest
        gw_ref, gs_ref, earlier, sem = rest[-4:]
        rest = rest[:-4]
    else:
        out_ref, grad_ref, gw_ref, gs_ref, *rest = rest
    xs, cs, dq, facts, table, qkv_all, p_all, w_ref, sems = rest
    step = pl.program_id(0)
    width = xs.shape[1]
    alive = cnt_ref[0] > 2 * (m0 + step)
    qkv_ref, p_ref = qkv_all.at[pl.ds(step, 1)], p_all.at[pl.ds(step, 1)]
    steps = qkv_all.shape[0]

    def late(which, at):
        if which == "rest":
            cols = pl.ds(3 * width, width + SMALL)
            return pltpu.make_async_copy(w_hbm.at[:, cols], w_ref.at[:, cols], sems.at[2 * steps])
        if which == "first":
            cols = pl.ds(0, 3 * width)
            return pltpu.make_async_copy(
                w_hbm.at[:, cols], w_ref.at[:, cols], sems.at[2 * steps + 1]
            )
        if which == "qkv":
            return pltpu.make_async_copy(qkv_hbm.at[at], qkv_all.at[at], sems.at[at])
        return pltpu.make_async_copy(p_hbm.at[at], p_all.at[at], sems.at[steps + at])


    @pl.when(step == 0)
    def _():
        late("rest", 0).start()
        for at in range(steps):
            late("qkv", at).start()
            late("p", at).start()
        late("first", 0).start()
        table[...] = jnp.zeros_like(table)
        gw_ref[...] = jnp.zeros_like(gw_ref)
        if has_acc:
            pltpu.make_async_copy(accw_ref, earlier, sem).start()
            gs_ref[...] = accs_ref[...]
        else:
            gs_ref[...] = jnp.zeros_like(gs_ref)

    @pl.when(jnp.logical_not(alive))
    def _():
        out_ref[...] = jnp.zeros_like(out_ref)
        grad_ref[...] = jnp.zeros_like(grad_ref)
        late("qkv", step).wait()
        late("p", step).wait()

        @pl.when(step == 0)
        def _():
            late("rest", 0).wait()
            late("first", 0).wait()

    def add_row(row, value):
        gs_ref[row : row + 1, :] += jnp.sum(value, 0, keepdims=True)

    @pl.when(alive)
    def _():
        load_padded(xs, img_ref, seq_len, pad_len)
        load_padded(cs, cot_ref, seq_len, pad_len)
        load_table(facts, table, meta_ref, pad_len)
        rows = xs.shape[0]
        live = facts[:, COL_LIVE : COL_LIVE + 1]
        d_final = cs[...] * live
        middle = mid_ref[0]
        rp = rp_ref[0]
        lane = lax.broadcasted_iota(jnp.int32, (1, SMALL), 1)
        lane_f = lane.astype(F32)
        slot = lax.broadcasted_iota(jnp.int32, (1, EXPERTS * CAP), 1).astype(F32)
        res = y_ref[:, 0, 0].reshape(EXPERTS * CAP, width)
        d_rows = y_ref[:, 1, 0].reshape(EXPERTS * CAP, width)
        final = middle
        d_prob = coef_ref[0:1, :] * live
        sel_all = None
        for target, route, kept in ((COL_T0, COL_R0, COL_K0), (COL_T1, COL_R1, COL_K1)):
            sel = jnp.where(slot == facts[:, target : target + 1], 1.0, 0.0).astype(BF)
            sel_all = sel if sel_all is None else sel_all + sel
            picked = mm(sel, res)
            keep = facts[:, kept : kept + 1]
            hot = lane_f == facts[:, route : route + 1]
            gate = jnp.sum(jnp.where(hot, rp, 0.0), -1, keepdims=True) * keep
            final = final + gate * picked
            d_gate = jnp.sum(picked * d_final, -1, keepdims=True) * keep
            d_prob = d_prob + jnp.where(hot, d_gate, 0.0)
        final = final * live
        for i in range(2):
            out_ref[i] = final[i * pad_len : i * pad_len + seq_len, :].astype(BF)
        d_mixed = mm(sel_all, d_rows)

        @pl.when(step == 0)
        def _():
            late("rest", 0).wait()

        d_logits = (rp * (d_prob - jnp.sum(rp * d_prob, -1, keepdims=True))).astype(BF)
        d_mixed = d_mixed + mm_nt(d_logits, w_ref[:, 4 * width : 4 * width + SMALL])
        gain2 = small_ref[ROW_GAIN2 : ROW_GAIN2 + 1, :]
        xhat2, inv2 = norm_parts(middle)
        mixed = (xhat2 * gain2 + small_ref[ROW_BIAS2 : ROW_BIAS2 + 1, :]).astype(BF)
        gs_ref[0:EXPERTS, :] += mm_tn(d_logits, mixed)[0:EXPERTS, :]
        add_row(ROW_GAIN2, d_mixed * xhat2)
        add_row(ROW_BIAS2, d_mixed)
        d_middle = d_final + norm_back(d_mixed, xhat2, inv2, gain2)
        add_row(ROW_OBIAS, d_middle)
        cs[...] = d_middle
        d_branch = d_middle.astype(BF)
        gw_ref[:, 3 * width : 4 * width] += mm_tn(att_ref[0], d_branch)
        d_att_all = mm_nt(d_branch, w_ref[:, 3 * width : 4 * width]).astype(BF)
        late("qkv", step).wait()
        late("p", step).wait()
        low, high, low_mask = half_masks()
        scale = HEAD_DIM**-0.5
        for i in range(2):
            span = slice(i * pad_len, (i + 1) * pad_len)
            for hp in range(HEADS // 2):
                at = hp * PAIR
                q = qkv_ref[0, span, at : at + PAIR]
                k = qkv_ref[0, span, width + at : width + at + PAIR]
                v = qkv_ref[0, span, 2 * width + at : 2 * width + at + PAIR]
                d_att = stack_heads(d_att_all[span, at : at + PAIR], low, high)
                p = p_ref[0, i, hp]
                pf = p.astype(F32)
                d_attn = mm_nt(d_att, v)
                d_s = (pf * (d_attn - jnp.sum(pf * d_attn, -1, keepdims=True))).astype(BF)
                d_v = mm_tn(p, d_att)
                d_k = mm_tn(d_s, stack_heads(q, low, high)) * scale
                d_q = mm(d_s, k) * scale
                dq[span, at : at + PAIR] = jnp.where(
                    low_mask, d_q[:pad_len], d_q[pad_len:]
                ).astype(BF)
                dq[span, width + at : width + at + PAIR] = d_k.astype(BF)
                dq[span, 2 * width + at : 2 * width + at + PAIR] = d_v.astype(BF)
        gain1 = small_ref[ROW_GAIN1 : ROW_GAIN1 + 1, :]
        xhat, inv = norm_parts(xs[...])
        normed = (xhat * gain1 + small_ref[ROW_BIAS1 : ROW_BIAS1 + 1, :]).astype(BF)
        add_row(ROW_QBIAS, dq[:, 0:width].astype(F32))
        add_row(ROW_VBIAS, dq[:, 2 * width : 3 * width].astype(F32))
        gw_ref[:, 0 : 3 * width] += mm_tn(normed, dq[...])

        @pl.when(step == 0)
        def _():
            late("first", 0).wait()

        d_normed = mm_nt(dq[...], w_ref[:, 0 : 3 * width])
        add_row(ROW_GAIN1, d_normed * xhat)
        add_row(ROW_BIAS1, d_normed)
        d_tok = cs[...] + norm_back(d_normed, xhat, inv, gain1)
        for i in range(2):
            grad_ref[i] = d_tok[i * pad_len : i * pad_len + seq_len, :].astype(BF)

    if last:

        @pl.when(step == pl.num_programs(0) - 1)
        def _():
            if has_acc:
                pltpu.make_async_copy(accw_ref, earlier, sem).wait()
                gw_ref[...] += earlier[...]
            small_part = (gs_ref[...] + extra_ref[...]).T.astype(BF)
            for b in range(width // BLOCK):
                at = slice(b * BLOCK, (b + 1) * BLOCK)
                core = b % CORES
                if len(pack_ref.shape) == 4:
                    ref = pack_ref.at[core, b // CORES]
                else:
                    ref = pack_ref.at[at]
                ref[:, 0 : 4 * width] = gw_ref[at, :].astype(BF)
                ref[:, 4 * width :] = small_part[at, :]


def backward_call(
    m0,
    mbc,
    last,
    own_rows,
    images,
    cotangent,
    count,
    meta,
    back,
    saved,
    coef,
    weights,
    small,
    extra,
    acc,
):
    seq_len, width = images.shape[1], images.shape[2]
    pad_len = meta.shape[2]
    rows = 2 * pad_len
    mb = images.shape[0] // mbc
    qkv, probs, att, mid, rp = saved
    at = lambda i: i + m0
    image_block = pl.BlockSpec((mb, seq_len, width), lambda i: (i, 0, 0))
    made_block = pl.BlockSpec((mb, seq_len, width), lambda i: (at(i), 0, 0))
    made = jax.ShapeDtypeStruct((mb * MICRO, seq_len, width), BF)
    in_specs = [
        pl.BlockSpec(memory_space=pltpu.SMEM),
        image_block,
        image_block,
        pl.BlockSpec((mb, 8, pad_len), lambda i: (at(i), 0, 0)),
        pl.BlockSpec((EXPERTS, 2, 1, CAP, width), lambda i: (0, 0, i, 0, 0)),
        pl.BlockSpec(memory_space=pl.ANY),
        pl.BlockSpec(memory_space=pl.ANY),
        pl.BlockSpec((1, rows, width), lambda i: (i, 0, 0)),
        pl.BlockSpec((1, rows, width), lambda i: (i, 0, 0)),
        pl.BlockSpec((1, rows, SMALL), lambda i: (i, 0, 0)),
        full_block(coef.shape),
        pl.BlockSpec(memory_space=pl.ANY),
        full_block(small.shape),
        full_block(extra.shape),
    ]
    args = [count, images, cotangent, meta, back, qkv, probs, att, mid, rp]
    args += [coef, weights, small, extra]
    aliases = {}
    if acc is not None:
        base = len(args)
        in_specs += [pl.BlockSpec(memory_space=pl.ANY), full_block(acc[1].shape)]
        in_specs += [pl.BlockSpec(memory_space=pl.ANY)] * 2
        args += list(acc)
        aliases = {base + 2: 0, base + 3: 1}
    sums = [(width, 4 * width), (SMALL, width)]
    pack_shape = (width, weights.shape[1])
    if own_rows == BLOCK:
        pack_shape = (CORES, width // (CORES * BLOCK), BLOCK, weights.shape[1])
    if last:
        grads = [jax.ShapeDtypeStruct(pack_shape, BF)]
        held = [pltpu.VMEM(shape, F32) for shape in sums]
        held += [pltpu.VMEM(sums[0], F32), pltpu.SemaphoreType.DMA]
    else:
        grads = [jax.ShapeDtypeStruct(shape, F32) for shape in sums]
        held = []
    return pl.pallas_call(
        functools.partial(backward_kernel, m0, seq_len, pad_len, acc is not None, last),
        grid=(mbc,),
        in_specs=in_specs,
        out_specs=[
            made_block,
            made_block,
        ]
        + [full_block(g.shape) for g in grads],
        out_shape=[
            made,
            made,
        ]
        + grads,
        scratch_shapes=[
            pltpu.VMEM((rows, width), F32),
            pltpu.VMEM((rows, width), F32),
            pltpu.VMEM((rows, 3 * width), BF),
            pltpu.VMEM((rows, SMALL), F32),
            pltpu.VMEM((SMALL, pad_len), F32),
            pltpu.VMEM(qkv.shape, BF),
            pltpu.VMEM(probs.shape, BF),
            pltpu.VMEM(weights.shape, BF),
            pltpu.SemaphoreType.DMA((2 * mbc + 2,)),
        ]
        + held,
        input_output_aliases=aliases,
        compiler_params=pltpu.CompilerParams(vmem_limit_bytes=VMEM_LIMIT),
        cost_estimate=pl.CostEstimate(
            flops=mbc * 20 * 10**9, bytes_accessed=mbc * 10 * 10**6, transcendentals=0
        ),
        name="dense_backward",
    )(*args)


def finish_kernel(count, got_ref, bal_ref, *refs):
    experts, refs = refs[:count], refs[count:]
    qkv_ref, out_ref, router_ref, gain1_ref, bias1_ref, qv_ref, obias_ref = refs[:7]
    gain2_ref, bias2_ref, ein_ref, eout_ref, balance_ref, *refs = refs[7:]
    turned = refs[-1]
    if experts:
        in_ref, back_ref = refs[:2]
        half, wide_of = back_ref.shape[1:]
        for r, block in enumerate(experts):
            e = lax.bitwise_xor(lax.rem(lax.axis_index("dp"), EXPERTS), r)
            for c in range(half // BLOCK):
                in_ref[e, :, c * wide_of : (c + 1) * wide_of] = block[
                    c * BLOCK : (c + 1) * BLOCK, :
                ].astype(F32)
            back_ref[e] = block[half:, :].astype(F32)
    sources, rows, wide = got_ref.shape
    width = out_ref.shape[1]
    whole = got_ref[0].astype(F32)
    for source in range(1, sources):
        whole = whole + got_ref[source].astype(F32)
    qkv_ref[...] = whole[:, : 3 * width]
    out_ref[...] = whole[:, 3 * width : 4 * width]
    turned[...] = jnp.zeros_like(turned)
    turned[0:rows, :] = whole[:, 4 * width :]
    balance_ref[...] = jnp.sum(turned[0:1, :] * bal_ref[0:1, :], -1, keepdims=True)
    turned[...] = turned[...].T
    router_ref[...] = turned[0:EXPERTS, 0:rows]
    for row, ref in (
        (ROW_GAIN1, gain1_ref),
        (ROW_BIAS1, bias1_ref),
        (ROW_OBIAS, obias_ref),
        (ROW_GAIN2, gain2_ref),
        (ROW_BIAS2, bias2_ref),
    ):
        ref[...] = turned[row : row + 1, 0:rows]
    qv_ref[...] = turned[ROW_QBIAS : ROW_VBIAS + 1, 0:rows]
    eout_ref[...] = turned[ROW_EOUT : ROW_EOUT + EXPERTS, 0:rows]
    for c in range(ein_ref.shape[1] // rows):
        at = ROW_EIN + c * EXPERTS
        ein_ref[:, c * rows : (c + 1) * rows] = turned[at : at + EXPERTS, 0:rows]


def finish_call(got, bal, experts, width, ff_rows):
    rows = got.shape[1]
    shapes = [
        (rows, 3 * width),
        (rows, width),
        (EXPERTS, rows),
        (1, rows),
        (1, rows),
        (2, rows),
        (1, rows),
        (1, rows),
        (1, rows),
        (EXPERTS, ff_rows),
        (EXPERTS, rows),
        (1, 1),
    ]
    if experts:
        half = experts[0].shape[0] // 2
        shapes += [(EXPERTS, BLOCK, half // BLOCK * width), (EXPERTS, half, width)]
    vm = pl.BlockSpec(memory_space=pltpu.VMEM)
    return pl.pallas_call(
        functools.partial(finish_kernel, len(experts)),
        in_specs=[vm] * (2 + len(experts)),
        out_specs=[vm] * len(shapes),
        out_shape=[jax.ShapeDtypeStruct(shape, F32) for shape in shapes],
        scratch_shapes=[pltpu.VMEM((SMALL, SMALL), F32)],
        name="finish",
    )(got, bal, *experts)


def shards(
    total,
    images,
    image_count,
    expert_index,
    expert_slot,
    keep,
    cotangent,
    ln1_gain,
    ln1_bias,
    qkv_weight,
    qv_bias,
    out_weight,
    out_bias,
    ln2_gain,
    ln2_bias,
    router_weight,
    expert_in,
    expert_in_bias,
    expert_out,
    expert_out_bias,
):
    slots, seq_len, width = images.shape
    planes = total // EXPERTS
    rows = width // total
    ff = expert_in.shape[2]
    ff_rows = ff // total
    mb = slots // MICRO
    pad_len = -(-seq_len // 16) * 16
    plane_groups = [[z * EXPERTS + p for p in range(EXPERTS)] for z in range(planes)]
    core_groups = [
        [z * EXPERTS + c * CORES + k for c in range(CHIPS)]
        for z in range(planes)
        for k in range(CORES)
    ]
    far_groups = [[CORES * i + k for i in range(total // CORES)] for k in range(CORES)]
    chip_groups = [[CORES * i + k for k in range(CORES)] for i in range(total // CORES)]
    z_groups = [[z * EXPERTS + p for z in range(planes)] for p in range(EXPERTS)]

    def plane_swap(v):
        return lax.all_to_all(v, "dp", 0, 0, tiled=True, axis_index_groups=plane_groups)

    def z_swap(v):
        return lax.all_to_all(v, "dp", 0, 0, tiled=True, axis_index_groups=z_groups)

    def z_gather(v):
        return lax.all_gather(v, "dp", axis=0, tiled=True, axis_index_groups=z_groups)

    parts = ff // width
    if rows == BLOCK:
        expert_pack = pack_call(expert_in, expert_out)
    else:
        expert_pack = jnp.concatenate(
            [
                expert_in.reshape(EXPERTS, rows, parts, width)
                .transpose(0, 2, 1, 3)
                .reshape(EXPERTS, ff_rows, width),
                expert_out,
            ],
            1,
        )
    expert_pack = plane_swap(expert_pack)

    live_img = (jnp.arange(slots) < image_count[0]).astype(F32)
    live_tok = jnp.broadcast_to(live_img[:, None, None], (slots, seq_len, 1))
    if rows == BLOCK:
        vectors = [v[None] for v in (ln1_gain, ln1_bias, out_bias, ln2_gain, ln2_bias)]
        packed = prepare_call(
            image_count,
            expert_index.transpose(0, 2, 1),
            qkv_weight,
            out_weight,
            router_weight.T,
            vectors[0],
            vectors[1],
            qv_bias,
            *vectors[2:],
            expert_in_bias,
            expert_out_bias,
        )
    else:
        hits = (expert_index[..., None] == jnp.arange(EXPERTS)).astype(F32) * live_tok[..., None]
        local_counts = jnp.sum(hits, axis=(0, 1, 2))
        high = jnp.floor(local_counts * (1.0 / 128.0))
        told = jnp.concatenate([high, local_counts - 128.0 * high, image_count.astype(F32)])
        small_cols = jnp.concatenate(
            [
                router_weight,
                ln1_gain[:, None],
                ln1_bias[:, None],
                qv_bias.T,
                out_bias[:, None],
                ln2_gain[:, None],
                ln2_bias[:, None],
                jnp.zeros((rows, 1), BF),
                expert_in_bias.reshape(EXPERTS, parts, rows).transpose(2, 1, 0).reshape(rows, -1),
                expert_out_bias.T,
                jnp.broadcast_to(told.astype(BF)[None], (rows, 2 * EXPERTS + 1)),
            ],
            1,
        )
        small_cols = jnp.pad(small_cols, ((0, 0), (0, SMALL - small_cols.shape[1])))
        packed = jnp.concatenate([qkv_weight, out_weight, small_cols], 1)
    wide = packed.shape[1]
    if rows == BLOCK:
        pieces = [packed]
        for z in range(1, planes):
            pieces.append(
                lax.ppermute(packed, "dp", [(i, i ^ (z * EXPERTS)) for i in range(total)])
            )
        packed = jnp.concatenate(pieces, 0)
    else:
        packed = z_gather(packed)
    spans = []
    for size in CHUNKS:
        spans.append((sum(span[1] for span in spans), size))
    held = {
        m0: [v[m0 * mb : (m0 + mbc) * mb] for v in (images, cotangent)] for m0, mbc in spans
    }
    packed = jnp.broadcast_to(packed[None], (CHIPS,) + packed.shape)
    packed, expert_pack = lax.optimization_barrier((packed, expert_pack))
    first = lax.all_to_all(
        packed,
        "dp",
        0,
        0,
        tiled=True,
        axis_index_groups=core_groups,
    )
    second = lax.ppermute(first, "dp", [(i, i ^ 1) for i in range(total)])
    me = lax.axis_index("dp")
    if rows != BLOCK:
        even = me % CORES == 0
        both = jnp.stack([jnp.where(even, first, second), jnp.where(even, second, first)], 1)
        first = (
            both.reshape(CHIPS, CORES, planes, rows, wide)
            .transpose(2, 0, 1, 3, 4)
            .reshape(width, wide)
        )
        second = first[:, 4 * width :].astype(F32).T

    index_t, slot_t, keep_t = (v.transpose(0, 2, 1) for v in (expert_index, expert_slot, keep))
    target = jnp.where(keep_t == 1, index_t * CAP + slot_t, -1).astype(F32)
    live_row = jnp.broadcast_to(live_img[:, None, None], (slots, 1, seq_len))
    flags = jnp.concatenate(
        [index_t.astype(F32), keep_t.astype(F32), live_row, jnp.zeros_like(live_row)], 1
    )
    beyond = ((0, 0), (0, 0), (0, pad_len - seq_len))
    meta = jnp.concatenate(
        [jnp.pad(target, beyond, constant_values=-1.0), jnp.pad(flags, beyond)], 1
    )

    expert_pack = z_gather(expert_pack)
    if rows != BLOCK:
        blocks = width // BLOCK
        expert_pack = jnp.concatenate(
            [
                expert_pack[:, :ff_rows]
                .reshape(blocks, total // blocks, parts, rows, width)
                .transpose(0, 2, 1, 3, 4)
                .reshape(blocks, parts * BLOCK, width),
                expert_pack[:, ff_rows:].reshape(blocks, parts * BLOCK, width),
            ],
            1,
        )

    saved, sent, prob_sums = [], [], []
    for m0, mbc in spans:
        assemble = m0 == 0 and rows == BLOCK
        xd, qkv, probs, att, mid, rp, prob, *made = forward_call(
            m0, mbc, assemble, *held[m0], image_count, meta, first, second
        )
        if assemble:
            first, second = made
        saved.append((qkv, probs, att, mid, rp))
        prob_sums.append(prob[0, :EXPERTS])
        sent.append(plane_swap(xd))
    weights = first
    small, _ = lax.optimization_barrier((second, prob_sums[-1]))

    in_bias = small[AT_EIN : AT_EIN + parts * EXPERTS].reshape(parts, EXPERTS, width)
    in_bias = lax.dynamic_index_in_dim(in_bias, me % EXPERTS, 1, keepdims=False)
    in_bias = in_bias.reshape(parts, total, rows).transpose(1, 0, 2).reshape(1, ff)
    out_bias_e = lax.dynamic_slice_in_dim(small, AT_EOUT + me % EXPERTS, 1, 0)
    sums = jnp.sum(small[AT_HIGH : AT_IMAGES + 1], 1) * (1.0 / rows)
    counts_all = sums[:EXPERTS] * 128.0 + sums[EXPERTS : 2 * EXPERTS]
    live_total = sums[2 * EXPERTS] * float(seq_len)
    plane_counts = lax.dynamic_slice_in_dim(
        small[AT_IMAGES], (me // EXPERTS) * (EXPERTS * rows), EXPERTS * rows, 0
    )
    plane_counts = plane_counts.reshape(EXPERTS, rows)[:, 0].astype(jnp.int32)
    coef = jnp.pad(BALANCE_WEIGHT * EXPERTS * counts_all / live_total, (0, SMALL - EXPERTS))
    coef = jnp.broadcast_to(coef[None], (8, SMALL))
    in_bias = jnp.broadcast_to(in_bias, (8, ff))
    out_bias_e = jnp.broadcast_to(out_bias_e, (8, width))

    acc = None
    back = []
    for (m0, mbc), rows_in in zip(spans, sent):
        y, *acc = expert_call(
            m0,
            mbc,
            m0 + mbc == MICRO,
            plane_counts,
            rows_in,
            expert_pack,
            in_bias,
            out_bias_e,
            acc,
        )
        back.append(plane_swap(y))
    expert_grads, gb1, gb2 = acc

    if rows != BLOCK:
        expert_grads = jnp.concatenate(
            [
                expert_grads[:, : parts * BLOCK]
                .reshape(blocks, parts, total // blocks, rows, width)
                .transpose(0, 2, 1, 3, 4)
                .reshape(total, ff_rows, width),
                expert_grads[:, parts * BLOCK :].reshape(total, ff_rows, width),
            ],
            1,
        )
    expert_grads = lax.psum_scatter(
        expert_grads, "dp", scatter_dimension=0, tiled=True, axis_index_groups=z_groups
    )
    if rows == BLOCK:
        place = me % EXPERTS
        blocks_in = []
        for r in range(EXPERTS):
            block = lax.dynamic_index_in_dim(expert_grads, place ^ r, 0, keepdims=False)
            if r:
                block = lax.ppermute(block, "dp", [(i, i ^ r) for i in range(total)])
            blocks_in.append(block)
    else:
        blocks_in = []
        expert_grads = plane_swap(expert_grads).astype(F32)
        expert_in_grad = (
            expert_grads[:, :ff_rows]
            .reshape(EXPERTS, parts, rows, width)
            .transpose(0, 2, 1, 3)
            .reshape(EXPERTS, rows, ff)
        )
        expert_out_grad = expert_grads[:, ff_rows:]

    prob_sum = prob_sums[0]
    for piece in prob_sums[1:]:
        prob_sum = prob_sum + piece
    p_hi = prob_sum.astype(BF).astype(F32)
    mine = (jnp.arange(EXPERTS) == me % EXPERTS).astype(F32)
    e_in = gb1[0].reshape(total, parts, rows).transpose(1, 0, 2).reshape(parts, 1, width)
    extra = jnp.concatenate(
        [
            jnp.zeros((ROW_PROB, width), F32),
            jnp.broadcast_to(
                jnp.concatenate([p_hi, prob_sum - p_hi])[:, None], (2 * EXPERTS, width)
            ),
            mine[:, None] * gb2[0:1],
            (mine[None, :, None] * e_in).reshape(parts * EXPERTS, width),
            jnp.zeros((SMALL - ROW_EIN - parts * EXPERTS, width), F32),
        ],
        0,
    )

    bal = EXPERTS * counts_all / live_total / live_total
    bal = jnp.concatenate([jnp.zeros((ROW_PROB,), F32), bal, bal])
    bal = jnp.broadcast_to(jnp.pad(bal, (0, SMALL - bal.shape[0]))[None], (8, SMALL))
    extra, bal = lax.optimization_barrier((extra, bal))

    acc = None
    for (m0, mbc), returned, kept in zip(spans, back, saved):
        block_out, image_grad, *acc = backward_call(
            m0,
            mbc,
            m0 + mbc == MICRO,
            rows,
            *held[m0],
            image_count,
            meta,
            returned,
            kept,
            coef,
            weights,
            small,
            extra,
            None if acc is None else (*acc, block_out, image_grad),
        )

    grads = acc[0]
    if rows != BLOCK:
        grads = grads.reshape(total // CORES, CORES, rows, wide).transpose(1, 0, 2, 3)
    grads = lax.all_to_all(grads, "dp", 0, 0, tiled=True, axis_index_groups=chip_groups)
    grads = jnp.sum(grads.astype(F32), 0).astype(BF)
    grads = lax.all_to_all(
        grads.reshape(total // CORES, rows, wide),
        "dp",
        0,
        0,
        tiled=True,
        axis_index_groups=far_groups,
    )
    (
        qkv_grad,
        out_grad,
        router_grad,
        gain1_grad,
        bias1_grad,
        qv_grad,
        obias_grad,
        gain2_grad,
        bias2_grad,
        ein_grad,
        eout_grad,
        balance,
        *expert_pair,
    ) = finish_call(grads, bal, blocks_in, width, ff_rows)
    if blocks_in:
        expert_in_grad, expert_out_grad = expert_pair
    return (
        block_out,
        image_grad,
        balance.reshape(()),
        gain1_grad.reshape(rows),
        bias1_grad.reshape(rows),
        qkv_grad,
        qv_grad,
        out_grad,
        obias_grad.reshape(rows),
        gain2_grad.reshape(rows),
        bias2_grad.reshape(rows),
        router_grad.T,
        expert_in_grad,
        ein_grad,
        expert_out_grad,
        eout_grad,
    )


def solution(mesh):
    placed = (
        P("dp", None, None),
        P("dp"),
        P("dp", None, None),
        P("dp", None, None),
        P("dp", None, None),
        P("dp", None, None),
        P("dp"),
        P("dp"),
        P("dp", None),
        P(None, "dp"),
        P("dp", None),
        P("dp"),
        P("dp"),
        P("dp"),
        P("dp", None),
        P(None, "dp", None),
        P(None, "dp"),
        P(None, "dp", None),
        P(None, "dp"),
    )
    return jax.shard_map(
        functools.partial(shards, mesh.shape["dp"]),
        mesh=mesh,
        in_specs=placed,
        out_specs=(
            P("dp", None, None),
            P("dp", None, None),
            P(),
            P("dp"),
            P("dp"),
            P("dp", None),
            P(None, "dp"),
            P("dp", None),
            P("dp"),
            P("dp"),
            P("dp"),
            P("dp", None),
            P(None, "dp", None),
            P(None, "dp"),
            P(None, "dp", None),
            P(None, "dp"),
        ),
        check_vma=False,
    )
```

```python
import functools
import math

import jax
import jax.numpy as jnp
from jax import lax
from jax.experimental import pallas as pl
from jax.experimental.pallas import tpu as pltpu
from jax.sharding import PartitionSpec as P

HEADS = 8
HEAD_DIM = 64
EXPERTS = 8
MICRO = 4
CAP = 128
CHUNKS = (2, 2)
PAIR = 2 * HEAD_DIM
DISPATCH = 8

EPSILON = 1e-06
BALANCE_WEIGHT = 8.0

BF = jnp.bfloat16
F32 = jnp.float32

ROW_GAIN1, ROW_BIAS1, ROW_QBIAS, ROW_VBIAS, ROW_OBIAS, ROW_GAIN2, ROW_BIAS2 = range(8, 15)
SMALL = 128
ROW_PROB, ROW_EOUT, ROW_EIN = 16, 32, 40
AT_EIN, AT_EOUT, AT_HIGH, AT_LOW, AT_IMAGES = 16, 48, 56, 64, 72
CORES = 2
CHIPS = EXPERTS // CORES
BLOCK = 16
COL_T0, COL_T1, COL_R0, COL_R1, COL_K0, COL_K1, COL_LIVE = range(7)
VMEM_LIMIT = 60 * 1024 * 1024


def mm(a, b):
    return lax.dot_general(a, b, (((1,), (0,)), ((), ())), preferred_element_type=F32)


def mm_nt(a, b):
    return lax.dot_general(a, b, (((1,), (1,)), ((), ())), preferred_element_type=F32)


def mm_tn(a, b):
    return lax.dot_general(a, b, (((0,), (0,)), ((), ())), preferred_element_type=F32)


def load_padded(dst, src, seq_len, pad_len):
    for i in range(2):
        tail = (seq_len // 16) * 16
        dst[i * pad_len + tail : (i + 1) * pad_len, :] = jnp.zeros(
            (pad_len - tail, dst.shape[1]), dst.dtype
        )
        dst[i * pad_len : i * pad_len + seq_len, :] = src[i].astype(dst.dtype)


def load_table(facts, table, meta_ref, pad_len):
    for i in range(2):
        table[0 : meta_ref.shape[1], :] = meta_ref[i]
        facts[i * pad_len : (i + 1) * pad_len, :] = table[...].T


def norm_parts(x):
    mean = jnp.mean(x, -1, keepdims=True)
    centered = x - mean
    spread = jnp.mean(centered * centered, -1, keepdims=True)
    inv = lax.rsqrt(spread + EPSILON)
    return centered * inv, inv


def norm_back(d_out, xhat, inv, gain):
    d_hat = d_out * gain
    first = jnp.mean(d_hat, -1, keepdims=True)
    second = jnp.mean(d_hat * xhat, -1, keepdims=True)
    return inv * (d_hat - first - xhat * second)


def half_masks():
    lane = lax.broadcasted_iota(jnp.int32, (1, PAIR), 1)
    low = jnp.where(lane < HEAD_DIM, 1.0, 0.0)
    return low.astype(BF), (1.0 - low).astype(BF), lane < HEAD_DIM


def stack_heads(block, low, high):
    return jnp.concatenate([block * low, block * high], 0)


def forward_kernel(
    m0,
    seq_len,
    pad_len,
    assemble,
    cnt_ref,
    img_ref,
    cot_ref,
    meta_ref,
    first_ref,
    second_ref,
    xd_ref,
    qkv_ref,
    p_ref,
    att_ref,
    mid_ref,
    rp_ref,
    psum_ref,
    *rest,
):
    if assemble:
        w_ref, small_ref, xs, cs, facts, table = rest
    else:
        w_ref, small_ref = first_ref, second_ref
        xs, cs, facts, table = rest
    step = pl.program_id(0)
    width = xs.shape[1]
    alive = cnt_ref[0] > 2 * (m0 + step)

    @pl.when(step == 0)
    def _():
        psum_ref[...] = jnp.zeros_like(psum_ref)
        table[...] = jnp.zeros_like(table)
        if assemble:
            core = lax.rem(lax.axis_index("dp"), CORES)
            for ref, owner in ((first_ref, core), (second_ref, 1 - core)):
                for chip in range(CHIPS):
                    for z in range(ref.shape[1] // BLOCK):
                        plane = lax.bitwise_xor(lax.axis_index("dp") // EXPERTS, z)
                        at = plane * EXPERTS + chip * CORES + owner
                        at = pl.multiple_of(at * BLOCK, BLOCK)
                        w_ref[pl.ds(at, BLOCK), :] = ref[chip, z * BLOCK : (z + 1) * BLOCK, :]
            small_ref[...] = w_ref[:, 4 * width :].astype(F32).T

    @pl.when(jnp.logical_not(alive))
    def _():
        xd_ref[...] = jnp.zeros_like(xd_ref)

    @pl.when(alive)
    def _():
        load_padded(xs, img_ref, seq_len, pad_len)
        load_padded(cs, cot_ref, seq_len, pad_len)
        load_table(facts, table, meta_ref, pad_len)
        xhat, inv = norm_parts(xs[...])
        normed = (
            xhat * small_ref[ROW_GAIN1 : ROW_GAIN1 + 1, :] + small_ref[ROW_BIAS1 : ROW_BIAS1 + 1, :]
        ).astype(BF)
        for part, row in ((0, ROW_QBIAS), (1, None), (2, ROW_VBIAS)):
            cols = slice(part * width, (part + 1) * width)
            value = mm(normed, w_ref[:, cols])
            if row is not None:
                value = value + small_ref[row : row + 1, :]
            qkv_ref[0, :, cols] = value.astype(BF)
        low, high, low_mask = half_masks()
        key_ok = lax.broadcasted_iota(jnp.int32, (1, pad_len), 1) < seq_len
        for i in range(2):
            rows = slice(i * pad_len, (i + 1) * pad_len)
            for hp in range(HEADS // 2):
                at = hp * PAIR
                q = qkv_ref[0, rows, at : at + PAIR]
                k = qkv_ref[0, rows, width + at : width + at + PAIR]
                v = qkv_ref[0, rows, 2 * width + at : 2 * width + at + PAIR]
                s = mm_nt(stack_heads(q, low, high), k) * (HEAD_DIM**-0.5)
                s = jnp.where(key_ok, s, -1e30)
                e = jnp.exp(s - jnp.max(s, -1, keepdims=True))
                p = (e * (1.0 / jnp.sum(e, -1, keepdims=True))).astype(BF)
                p_ref[0, i, hp] = p
                o = mm(p, v)
                att_ref[0, rows, at : at + PAIR] = jnp.where(
                    low_mask, o[:pad_len], o[pad_len:]
                ).astype(BF)
        middle = (
            xs[...]
            + mm(att_ref[0], w_ref[:, 3 * width : 4 * width])
            + small_ref[ROW_OBIAS : ROW_OBIAS + 1, :]
        )
        mid_ref[0] = middle
        xhat2, inv2 = norm_parts(middle)
        mixed = (
            xhat2 * small_ref[ROW_GAIN2 : ROW_GAIN2 + 1, :]
            + small_ref[ROW_BIAS2 : ROW_BIAS2 + 1, :]
        ).astype(BF)
        logits = mm(mixed, w_ref[:, 4 * width : 4 * width + SMALL])
        lane = lax.broadcasted_iota(jnp.int32, (1, SMALL), 1)
        logits = jnp.where(lane < EXPERTS, logits, -1e30)
        e = jnp.exp(logits - jnp.max(logits, -1, keepdims=True))
        rp = e * (1.0 / jnp.sum(e, -1, keepdims=True))
        rp_ref[0] = rp
        live = facts[:, COL_LIVE : COL_LIVE + 1]
        psum_ref[0:1, :] += jnp.sum(rp * live, 0, keepdims=True)
        d_final = cs[...] * live
        lane_f = lane.astype(F32)
        weighted = []
        for route, kept in ((COL_R0, COL_K0), (COL_R1, COL_K1)):
            hot = lane_f == facts[:, route : route + 1]
            gate = jnp.sum(jnp.where(hot, rp, 0.0), -1, keepdims=True)
            gate = gate * facts[:, kept : kept + 1]
            weighted.append((gate * d_final).astype(BF))
        slot = lax.broadcasted_iota(jnp.int32, (DISPATCH * CAP, 1), 0).astype(F32)
        targets = facts[...].T
        for e_id in range(0, EXPERTS, DISPATCH):
            here = slot + float(e_id * CAP)
            sel0 = jnp.where(here == targets[COL_T0 : COL_T0 + 1, :], 1.0, 0.0)
            sel1 = jnp.where(here == targets[COL_T1 : COL_T1 + 1, :], 1.0, 0.0)
            shape = (DISPATCH, CAP, width)
            at = slice(e_id, e_id + DISPATCH)
            xd_ref[at, 0, 0] = mm((sel0 + sel1).astype(BF), mixed).astype(BF).reshape(shape)
            xd_ref[at, 1, 0] = (
                (mm(sel0.astype(BF), weighted[0]) + mm(sel1.astype(BF), weighted[1]))
                .astype(BF)
                .reshape(shape)
            )


def full_block(shape):
    return pl.BlockSpec(shape, lambda i: (0,) * len(shape))


def pack_kernel(in_ref, out_ref, pack_ref):
    width = out_ref.shape[2]
    half = out_ref.shape[1]
    for c in range(half // BLOCK):
        pack_ref[:, c * BLOCK : (c + 1) * BLOCK, :] = in_ref[:, :, c * width : (c + 1) * width]
    pack_ref[:, half:, :] = out_ref[...]


def pack_call(expert_in, expert_out):
    vm = pl.BlockSpec(memory_space=pltpu.VMEM)
    shape = (expert_out.shape[0], 2 * expert_out.shape[1], expert_out.shape[2])
    return pl.pallas_call(
        pack_kernel,
        in_specs=[vm] * 2,
        out_specs=vm,
        out_shape=jax.ShapeDtypeStruct(shape, BF),
        name="pack",
    )(expert_in, expert_out)


def prepare_kernel(
    cnt_ref,
    index_ref,
    qkv_ref,
    out_ref,
    router_ref,
    gain1_ref,
    bias1_ref,
    qv_ref,
    obias_ref,
    gain2_ref,
    bias2_ref,
    ein_ref,
    eout_ref,
    packed_ref,
    turned,
):
    rows, width = out_ref.shape
    packed_ref[:, 0 : 3 * width] = qkv_ref[...]
    packed_ref[:, 3 * width : 4 * width] = out_ref[...]
    turned[...] = jnp.zeros_like(turned)
    turned[0:EXPERTS, 0:rows] = router_ref[...].astype(F32)
    for row, ref in (
        (ROW_GAIN1, gain1_ref),
        (ROW_BIAS1, bias1_ref),
        (ROW_OBIAS, obias_ref),
        (ROW_GAIN2, gain2_ref),
        (ROW_BIAS2, bias2_ref),
    ):
        turned[row : row + 1, 0:rows] = ref[...].astype(F32)
    turned[ROW_QBIAS : ROW_VBIAS + 1, 0:rows] = qv_ref[...].astype(F32)
    turned[AT_EOUT : AT_EOUT + EXPERTS, 0:rows] = eout_ref[...].astype(F32)
    ein = ein_ref[...].astype(F32)
    for c in range(ein.shape[1] // rows):
        at = AT_EIN + c * EXPERTS
        turned[at : at + EXPERTS, 0:rows] = ein[:, c * rows : (c + 1) * rows]
    slots, top, seq_len = index_ref.shape
    chosen = index_ref[...]
    slot = lax.broadcasted_iota(jnp.int32, (slots, top, seq_len), 0)
    chosen = jnp.where(slot < cnt_ref[0], chosen, -1)
    for e in range(EXPERTS):
        hits = jnp.where(chosen == e, 1.0, 0.0)
        hits = jnp.sum(jnp.sum(hits, 0), -1, keepdims=True)
        hits = jnp.sum(hits, 0, keepdims=True)
        high = jnp.floor(hits * (1.0 / 128.0))
        turned[AT_HIGH + e : AT_HIGH + e + 1, :] = jnp.broadcast_to(high, (1, SMALL))
        turned[AT_LOW + e : AT_LOW + e + 1, :] = jnp.broadcast_to(hits - 128.0 * high, (1, SMALL))
    turned[AT_IMAGES : AT_IMAGES + 1, :] = jnp.full((1, SMALL), cnt_ref[0].astype(F32))
    turned[...] = turned[...].T
    packed_ref[:, 4 * width :] = turned[0:rows, :].astype(BF)


def prepare_call(count, *args):
    vm = pl.BlockSpec(memory_space=pltpu.VMEM)
    rows, width = args[2].shape
    return pl.pallas_call(
        prepare_kernel,
        in_specs=[pl.BlockSpec(memory_space=pltpu.SMEM)] + [vm] * len(args),
        out_specs=vm,
        out_shape=jax.ShapeDtypeStruct((rows, 4 * width + SMALL), BF),
        scratch_shapes=[pltpu.VMEM((SMALL, SMALL), F32)],
        name="prepare",
    )(count, *args)


def forward_call(m0, mbc, assemble, images, cotangent, count, meta, weights, small):
    seq_len, width = images.shape[1], images.shape[2]
    pad_len = meta.shape[2]
    rows = 2 * pad_len
    at = lambda i: i + m0
    mb = images.shape[0] // mbc
    made_here = []
    if assemble:
        made_here = [
            jax.ShapeDtypeStruct((width, weights.shape[2]), BF),
            jax.ShapeDtypeStruct((SMALL, width), F32),
        ]
    return pl.pallas_call(
        functools.partial(forward_kernel, m0, seq_len, pad_len, assemble),
        grid=(mbc,),
        in_specs=[
            pl.BlockSpec(memory_space=pltpu.SMEM),
            pl.BlockSpec((mb, seq_len, width), lambda i: (i, 0, 0)),
            pl.BlockSpec((mb, seq_len, width), lambda i: (i, 0, 0)),
            pl.BlockSpec((mb, 8, pad_len), lambda i: (at(i), 0, 0)),
            full_block(weights.shape),
            full_block(small.shape),
        ],
        out_specs=[
            pl.BlockSpec((EXPERTS, 2, 1, CAP, width), lambda i: (0, 0, i, 0, 0)),
            pl.BlockSpec((1, rows, 3 * width), lambda i: (i, 0, 0)),
            pl.BlockSpec((1, 2, HEADS // 2, rows, pad_len), lambda i: (i, 0, 0, 0, 0)),
            pl.BlockSpec((1, rows, width), lambda i: (i, 0, 0)),
            pl.BlockSpec((1, rows, width), lambda i: (i, 0, 0)),
            pl.BlockSpec((1, rows, SMALL), lambda i: (i, 0, 0)),
            full_block((8, SMALL)),
        ]
        + [full_block(made.shape) for made in made_here],
        out_shape=[
            jax.ShapeDtypeStruct((EXPERTS, 2, mbc, CAP, width), BF),
            jax.ShapeDtypeStruct((mbc, rows, 3 * width), BF),
            jax.ShapeDtypeStruct((mbc, 2, HEADS // 2, rows, pad_len), BF),
            jax.ShapeDtypeStruct((mbc, rows, width), BF),
            jax.ShapeDtypeStruct((mbc, rows, width), F32),
            jax.ShapeDtypeStruct((mbc, rows, SMALL), F32),
            jax.ShapeDtypeStruct((8, SMALL), F32),
        ]
        + made_here,
        scratch_shapes=[
            pltpu.VMEM((rows, width), F32),
            pltpu.VMEM((rows, width), F32),
            pltpu.VMEM((rows, SMALL), F32),
            pltpu.VMEM((SMALL, pad_len), F32),
        ],
        compiler_params=pltpu.CompilerParams(vmem_limit_bytes=VMEM_LIMIT),
        cost_estimate=pl.CostEstimate(
            flops=mbc * 8 * 10**9, bytes_accessed=mbc * 10 * 10**6, transcendentals=0
        ),
        name="dense_forward",
    )(count, images, cotangent, meta, weights, small)


GROUP = 4


def expert_kernel(
    m0,
    mbc,
    has_acc,
    last,
    cnt_ref,
    x_ref,
    w_ref,
    b1_ref,
    b2_ref,
    *rest,
):
    if has_acc:
        a1_ref, a2_ref, ab1_ref, ab2_ref = rest[:4]
        rest = rest[4:]
    if last:
        y_ref, pack_ref, gb1_ref, gb2_ref, s1, s2, order, xin, din, xout, dout = rest
    else:
        y_ref, s1, s2, gb1_ref, gb2_ref, order, xin, din, xout, dout = rest
    width = x_ref.shape[-1]
    ff = b1_ref.shape[1]
    half = w_ref.shape[1] // 2
    per_tile = width // half
    if has_acc:
        s1[...] = a1_ref[...]
        s2[...] = a2_ref[...]
        gb1_ref[...] = ab1_ref[...]
        gb2_ref[...] = ab2_ref[...]
    else:
        s1[...] = jnp.zeros_like(s1)
        s2[...] = jnp.zeros_like(s2)
        gb1_ref[...] = jnp.zeros_like(gb1_ref)
        gb2_ref[...] = jnp.zeros_like(gb2_ref)
    blocks = EXPERTS * mbc

    def is_live(b):
        return (cnt_ref[b // mbc] > 2 * (m0 + b % mbc)).astype(jnp.int32)

    live_total = jnp.int32(0)
    for b in range(blocks):
        live_total = live_total + is_live(b)
    head, tail = jnp.int32(0), live_total
    for b in range(blocks):
        flag = is_live(b)
        order[jnp.where(flag == 1, head, tail)] = b
        head = head + flag
        tail = tail + (1 - flag)

    def one_group(g, carry):
        for j in range(GROUP):
            b = order[g * GROUP + j]
            xin[j * CAP : (j + 1) * CAP, :] = x_ref[b // mbc, 0, b % mbc]
            din[j * CAP : (j + 1) * CAP, :] = x_ref[b // mbc, 1, b % mbc]
        rows_in, d_res = xin[...], din[...]
        gb2_ref[0:1, :] += jnp.sum(d_res.astype(F32), 0, keepdims=True)
        for f in range(ff // width):
            cols = slice(f * width, (f + 1) * width)
            w1 = w_ref[:, f * BLOCK : (f + 1) * BLOCK, :].reshape(width, width)
            w2 = w_ref[f * per_tile : (f + 1) * per_tile, half:, :].reshape(width, width)
            h = mm(rows_in, w1) + b1_ref[0:1, cols]
            bell = jnp.exp(-0.5 * h * h)
            t = 1.0 / (1.0 + (0.3275911 / math.sqrt(2.0)) * jnp.abs(h))
            poly = t * (
                0.5 * 0.254829592
                + t
                * (
                    0.5 * -0.284496736
                    + t * (0.5 * 1.421413741 + t * (0.5 * -1.453152027 + t * (0.5 * 1.061405429)))
                )
            )
            upper = poly * bell
            cdf = jnp.where(h < 0.0, upper, 1.0 - upper)
            act = (h * cdf).astype(BF)
            slope = cdf + h * bell * (1.0 / math.sqrt(2.0 * math.pi))
            d_act = mm_nt(d_res, w2)
            d_hid_f = (d_act * slope).astype(BF)
            gb1_ref[0:1, cols] += jnp.sum(d_hid_f.astype(F32), 0, keepdims=True)
            res = mm(act, w2)
            d_rows = mm_nt(d_hid_f, w1)
            if f == 0:
                xout[...] = res
                dout[...] = d_rows
            else:
                xout[...] += res
                dout[...] += d_rows
            s1[:, cols] += mm_tn(rows_in, d_hid_f)
            s2[cols, :] += mm_tn(act, d_res)
        for j in range(GROUP):
            b = order[g * GROUP + j]
            y_ref[b // mbc, 0, b % mbc] = (
                xout[j * CAP : (j + 1) * CAP, :] + b2_ref[0:1, :]
            ).astype(BF)
            y_ref[b // mbc, 1, b % mbc] = dout[j * CAP : (j + 1) * CAP, :].astype(BF)
        return carry

    lax.fori_loop(0, (live_total + GROUP - 1) // GROUP, one_group, 0)
    if last:
        blocks_of = width // BLOCK
        for f in range(ff // width):
            tile = s1[:, f * width : (f + 1) * width].astype(BF)
            pack_ref[:, f * BLOCK : (f + 1) * BLOCK, :] = tile.reshape(blocks_of, BLOCK, width)
        pack_ref[:, half:, :] = s2[...].astype(BF).reshape(blocks_of, half, width)


def expert_call(m0, mbc, last, counts, x, weights, b1, b2, acc):
    width, ff = weights.shape[2], b1.shape[1]
    if last:
        grads = [jax.ShapeDtypeStruct(weights.shape, BF)]
    else:
        grads = [jax.ShapeDtypeStruct((width, ff), F32), jax.ShapeDtypeStruct((ff, width), F32)]
    vm = pl.BlockSpec(memory_space=pltpu.VMEM)
    scratch = []
    if last:
        scratch += [pltpu.VMEM((width, ff), F32), pltpu.VMEM((ff, width), F32)]
    scratch += [
        pltpu.SMEM((EXPERTS * mbc,), jnp.int32),
        pltpu.VMEM((GROUP * CAP, width), BF),
        pltpu.VMEM((GROUP * CAP, width), BF),
        pltpu.VMEM((GROUP * CAP, width), F32),
        pltpu.VMEM((GROUP * CAP, width), F32),
    ]
    return pl.pallas_call(
        functools.partial(expert_kernel, m0, mbc, acc is not None, last),
        in_specs=[pl.BlockSpec(memory_space=pltpu.SMEM)] + [vm] * (4 + (0 if acc is None else 4)),
        out_specs=[vm] * (len(grads) + 3),
        out_shape=[
            jax.ShapeDtypeStruct(x.shape, BF),
            *grads,
            jax.ShapeDtypeStruct((8, ff), F32),
            jax.ShapeDtypeStruct((8, width), F32),
        ],
        scratch_shapes=scratch,
        compiler_params=pltpu.CompilerParams(vmem_limit_bytes=VMEM_LIMIT),
        cost_estimate=pl.CostEstimate(
            flops=mbc * 20 * 10**9, bytes_accessed=mbc * 10 * 10**6, transcendentals=0
        ),
        name="expert_both",
    )(counts, x, weights, b1, b2, *(() if acc is None else acc))


def backward_kernel(
    m0,
    seq_len,
    pad_len,
    has_acc,
    last,
    cnt_ref,
    img_ref,
    cot_ref,
    meta_ref,
    y_ref,
    qkv_hbm,
    p_hbm,
    att_ref,
    mid_ref,
    rp_ref,
    coef_ref,
    w_hbm,
    small_ref,
    extra_ref,
    *rest,
):
    if has_acc:
        accw_ref, accs_ref = rest[:2]
        rest = rest[4:]
    if last:
        out_ref, grad_ref, pack_ref, *rest = rest
        gw_ref, gs_ref, earlier, sem = rest[-4:]
        rest = rest[:-4]
    else:
        out_ref, grad_ref, gw_ref, gs_ref, *rest = rest
    xs, cs, dq, facts, table, qkv_all, p_all, w_ref, sems = rest
    step = pl.program_id(0)
    width = xs.shape[1]
    alive = cnt_ref[0] > 2 * (m0 + step)
    qkv_ref, p_ref = qkv_all.at[pl.ds(step, 1)], p_all.at[pl.ds(step, 1)]
    steps = qkv_all.shape[0]

    def late(which, at):
        if which == "rest":
            cols = pl.ds(3 * width, width + SMALL)
            return pltpu.make_async_copy(w_hbm.at[:, cols], w_ref.at[:, cols], sems.at[2 * steps])
        if which == "first":
            cols = pl.ds(0, 3 * width)
            return pltpu.make_async_copy(
                w_hbm.at[:, cols], w_ref.at[:, cols], sems.at[2 * steps + 1]
            )
        if which == "qkv":
            return pltpu.make_async_copy(qkv_hbm.at[at], qkv_all.at[at], sems.at[at])
        return pltpu.make_async_copy(p_hbm.at[at], p_all.at[at], sems.at[steps + at])


    @pl.when(step == 0)
    def _():
        late("rest", 0).start()
        for at in range(steps):
            late("qkv", at).start()
            late("p", at).start()
        late("first", 0).start()
        table[...] = jnp.zeros_like(table)
        gw_ref[...] = jnp.zeros_like(gw_ref)
        if has_acc:
            pltpu.make_async_copy(accw_ref, earlier, sem).start()
            gs_ref[...] = accs_ref[...]
        else:
            gs_ref[...] = jnp.zeros_like(gs_ref)

    @pl.when(jnp.logical_not(alive))
    def _():
        out_ref[...] = jnp.zeros_like(out_ref)
        grad_ref[...] = jnp.zeros_like(grad_ref)
        late("qkv", step).wait()
        late("p", step).wait()

        @pl.when(step == 0)
        def _():
            late("rest", 0).wait()
            late("first", 0).wait()

    def add_row(row, value):
        gs_ref[row : row + 1, :] += jnp.sum(value, 0, keepdims=True)

    @pl.when(alive)
    def _():
        load_padded(xs, img_ref, seq_len, pad_len)
        load_padded(cs, cot_ref, seq_len, pad_len)
        load_table(facts, table, meta_ref, pad_len)
        rows = xs.shape[0]
        live = facts[:, COL_LIVE : COL_LIVE + 1]
        d_final = cs[...] * live
        middle = mid_ref[0]
        rp = rp_ref[0]
        lane = lax.broadcasted_iota(jnp.int32, (1, SMALL), 1)
        lane_f = lane.astype(F32)
        slot = lax.broadcasted_iota(jnp.int32, (1, EXPERTS * CAP), 1).astype(F32)
        res = y_ref[:, 0, 0].reshape(EXPERTS * CAP, width)
        d_rows = y_ref[:, 1, 0].reshape(EXPERTS * CAP, width)
        final = middle
        d_prob = coef_ref[0:1, :] * live
        sel_all = None
        for target, route, kept in ((COL_T0, COL_R0, COL_K0), (COL_T1, COL_R1, COL_K1)):
            sel = jnp.where(slot == facts[:, target : target + 1], 1.0, 0.0).astype(BF)
            sel_all = sel if sel_all is None else sel_all + sel
            picked = mm(sel, res)
            keep = facts[:, kept : kept + 1]
            hot = lane_f == facts[:, route : route + 1]
            gate = jnp.sum(jnp.where(hot, rp, 0.0), -1, keepdims=True) * keep
            final = final + gate * picked
            d_gate = jnp.sum(picked * d_final, -1, keepdims=True) * keep
            d_prob = d_prob + jnp.where(hot, d_gate, 0.0)
        final = final * live
        for i in range(2):
            out_ref[i] = final[i * pad_len : i * pad_len + seq_len, :].astype(BF)
        d_mixed = mm(sel_all, d_rows)

        @pl.when(step == 0)
        def _():
            late("rest", 0).wait()

        d_logits = (rp * (d_prob - jnp.sum(rp * d_prob, -1, keepdims=True))).astype(BF)
        d_mixed = d_mixed + mm_nt(d_logits, w_ref[:, 4 * width : 4 * width + SMALL])
        gain2 = small_ref[ROW_GAIN2 : ROW_GAIN2 + 1, :]
        xhat2, inv2 = norm_parts(middle)
        mixed = (xhat2 * gain2 + small_ref[ROW_BIAS2 : ROW_BIAS2 + 1, :]).astype(BF)
        gs_ref[0:EXPERTS, :] += mm_tn(d_logits, mixed)[0:EXPERTS, :]
        add_row(ROW_GAIN2, d_mixed * xhat2)
        add_row(ROW_BIAS2, d_mixed)
        d_middle = d_final + norm_back(d_mixed, xhat2, inv2, gain2)
        add_row(ROW_OBIAS, d_middle)
        cs[...] = d_middle
        d_branch = d_middle.astype(BF)
        gw_ref[:, 3 * width : 4 * width] += mm_tn(att_ref[0], d_branch)
        d_att_all = mm_nt(d_branch, w_ref[:, 3 * width : 4 * width]).astype(BF)
        late("qkv", step).wait()
        late("p", step).wait()
        low, high, low_mask = half_masks()
        scale = HEAD_DIM**-0.5
        for i in range(2):
            span = slice(i * pad_len, (i + 1) * pad_len)
            for hp in range(HEADS // 2):
                at = hp * PAIR
                q = qkv_ref[0, span, at : at + PAIR]
                k = qkv_ref[0, span, width + at : width + at + PAIR]
                v = qkv_ref[0, span, 2 * width + at : 2 * width + at + PAIR]
                d_att = stack_heads(d_att_all[span, at : at + PAIR], low, high)
                p = p_ref[0, i, hp]
                pf = p.astype(F32)
                d_attn = mm_nt(d_att, v)
                d_s = (pf * (d_attn - jnp.sum(pf * d_attn, -1, keepdims=True))).astype(BF)
                d_v = mm_tn(p, d_att)
                d_k = mm_tn(d_s, stack_heads(q, low, high)) * scale
                d_q = mm(d_s, k) * scale
                dq[span, at : at + PAIR] = jnp.where(
                    low_mask, d_q[:pad_len], d_q[pad_len:]
                ).astype(BF)
                dq[span, width + at : width + at + PAIR] = d_k.astype(BF)
                dq[span, 2 * width + at : 2 * width + at + PAIR] = d_v.astype(BF)
        gain1 = small_ref[ROW_GAIN1 : ROW_GAIN1 + 1, :]
        xhat, inv = norm_parts(xs[...])
        normed = (xhat * gain1 + small_ref[ROW_BIAS1 : ROW_BIAS1 + 1, :]).astype(BF)
        add_row(ROW_QBIAS, dq[:, 0:width].astype(F32))
        add_row(ROW_VBIAS, dq[:, 2 * width : 3 * width].astype(F32))
        gw_ref[:, 0 : 3 * width] += mm_tn(normed, dq[...])

        @pl.when(step == 0)
        def _():
            late("first", 0).wait()

        d_normed = mm_nt(dq[...], w_ref[:, 0 : 3 * width])
        add_row(ROW_GAIN1, d_normed * xhat)
        add_row(ROW_BIAS1, d_normed)
        d_tok = cs[...] + norm_back(d_normed, xhat, inv, gain1)
        for i in range(2):
            grad_ref[i] = d_tok[i * pad_len : i * pad_len + seq_len, :].astype(BF)

    if last:

        @pl.when(step == pl.num_programs(0) - 1)
        def _():
            if has_acc:
                pltpu.make_async_copy(accw_ref, earlier, sem).wait()
                gw_ref[...] += earlier[...]
            small_part = (gs_ref[...] + extra_ref[...]).T.astype(BF)
            for b in range(width // BLOCK):
                at = slice(b * BLOCK, (b + 1) * BLOCK)
                core = b % CORES
                if len(pack_ref.shape) == 4:
                    ref = pack_ref.at[core, b // CORES]
                else:
                    ref = pack_ref.at[at]
                ref[:, 0 : 4 * width] = gw_ref[at, :].astype(BF)
                ref[:, 4 * width :] = small_part[at, :]


def backward_call(
    m0,
    mbc,
    last,
    own_rows,
    images,
    cotangent,
    count,
    meta,
    back,
    saved,
    coef,
    weights,
    small,
    extra,
    acc,
):
    seq_len, width = images.shape[1], images.shape[2]
    pad_len = meta.shape[2]
    rows = 2 * pad_len
    mb = images.shape[0] // mbc
    qkv, probs, att, mid, rp = saved
    at = lambda i: i + m0
    image_block = pl.BlockSpec((mb, seq_len, width), lambda i: (i, 0, 0))
    made_block = pl.BlockSpec((mb, seq_len, width), lambda i: (at(i), 0, 0))
    made = jax.ShapeDtypeStruct((mb * MICRO, seq_len, width), BF)
    in_specs = [
        pl.BlockSpec(memory_space=pltpu.SMEM),
        image_block,
        image_block,
        pl.BlockSpec((mb, 8, pad_len), lambda i: (at(i), 0, 0)),
        pl.BlockSpec((EXPERTS, 2, 1, CAP, width), lambda i: (0, 0, i, 0, 0)),
        pl.BlockSpec(memory_space=pl.ANY),
        pl.BlockSpec(memory_space=pl.ANY),
        pl.BlockSpec((1, rows, width), lambda i: (i, 0, 0)),
        pl.BlockSpec((1, rows, width), lambda i: (i, 0, 0)),
        pl.BlockSpec((1, rows, SMALL), lambda i: (i, 0, 0)),
        full_block(coef.shape),
        pl.BlockSpec(memory_space=pl.ANY),
        full_block(small.shape),
        full_block(extra.shape),
    ]
    args = [count, images, cotangent, meta, back, qkv, probs, att, mid, rp]
    args += [coef, weights, small, extra]
    aliases = {}
    if acc is not None:
        base = len(args)
        in_specs += [pl.BlockSpec(memory_space=pl.ANY), full_block(acc[1].shape)]
        in_specs += [pl.BlockSpec(memory_space=pl.ANY)] * 2
        args += list(acc)
        aliases = {base + 2: 0, base + 3: 1}
    sums = [(width, 4 * width), (SMALL, width)]
    pack_shape = (width, weights.shape[1])
    if own_rows == BLOCK:
        pack_shape = (CORES, width // (CORES * BLOCK), BLOCK, weights.shape[1])
    if last:
        grads = [jax.ShapeDtypeStruct(pack_shape, BF)]
        held = [pltpu.VMEM(shape, F32) for shape in sums]
        held += [pltpu.VMEM(sums[0], F32), pltpu.SemaphoreType.DMA]
    else:
        grads = [jax.ShapeDtypeStruct(shape, F32) for shape in sums]
        held = []
    return pl.pallas_call(
        functools.partial(backward_kernel, m0, seq_len, pad_len, acc is not None, last),
        grid=(mbc,),
        in_specs=in_specs,
        out_specs=[
            made_block,
            made_block,
        ]
        + [full_block(g.shape) for g in grads],
        out_shape=[
            made,
            made,
        ]
        + grads,
        scratch_shapes=[
            pltpu.VMEM((rows, width), F32),
            pltpu.VMEM((rows, width), F32),
            pltpu.VMEM((rows, 3 * width), BF),
            pltpu.VMEM((rows, SMALL), F32),
            pltpu.VMEM((SMALL, pad_len), F32),
            pltpu.VMEM(qkv.shape, BF),
            pltpu.VMEM(probs.shape, BF),
            pltpu.VMEM(weights.shape, BF),
            pltpu.SemaphoreType.DMA((2 * mbc + 2,)),
        ]
        + held,
        input_output_aliases=aliases,
        compiler_params=pltpu.CompilerParams(vmem_limit_bytes=VMEM_LIMIT),
        cost_estimate=pl.CostEstimate(
            flops=mbc * 20 * 10**9, bytes_accessed=mbc * 10 * 10**6, transcendentals=0
        ),
        name="dense_backward",
    )(*args)


def finish_kernel(count, got_ref, bal_ref, *refs):
    experts, refs = refs[:count], refs[count:]
    qkv_ref, out_ref, router_ref, gain1_ref, bias1_ref, qv_ref, obias_ref = refs[:7]
    gain2_ref, bias2_ref, ein_ref, eout_ref, balance_ref, *refs = refs[7:]
    turned = refs[-1]
    if experts:
        in_ref, back_ref = refs[:2]
        half, wide_of = back_ref.shape[1:]
        for r, block in enumerate(experts):
            e = lax.bitwise_xor(lax.rem(lax.axis_index("dp"), EXPERTS), count - 1 - r)
            for c in range(half // BLOCK):
                in_ref[e, :, c * wide_of : (c + 1) * wide_of] = block[
                    c * BLOCK : (c + 1) * BLOCK, :
                ].astype(F32)
            back_ref[e] = block[half:, :].astype(F32)
    sources, rows, wide = got_ref.shape
    width = out_ref.shape[1]
    whole = got_ref[0].astype(F32)
    for source in range(1, sources):
        whole = whole + got_ref[source].astype(F32)
    qkv_ref[...] = whole[:, : 3 * width]
    out_ref[...] = whole[:, 3 * width : 4 * width]
    turned[...] = jnp.zeros_like(turned)
    turned[0:rows, :] = whole[:, 4 * width :]
    balance_ref[...] = jnp.sum(turned[0:1, :] * bal_ref[0:1, :], -1, keepdims=True)
    turned[...] = turned[...].T
    router_ref[...] = turned[0:EXPERTS, 0:rows]
    for row, ref in (
        (ROW_GAIN1, gain1_ref),
        (ROW_BIAS1, bias1_ref),
        (ROW_OBIAS, obias_ref),
        (ROW_GAIN2, gain2_ref),
        (ROW_BIAS2, bias2_ref),
    ):
        ref[...] = turned[row : row + 1, 0:rows]
    qv_ref[...] = turned[ROW_QBIAS : ROW_VBIAS + 1, 0:rows]
    eout_ref[...] = turned[ROW_EOUT : ROW_EOUT + EXPERTS, 0:rows]
    for c in range(ein_ref.shape[1] // rows):
        at = ROW_EIN + c * EXPERTS
        ein_ref[:, c * rows : (c + 1) * rows] = turned[at : at + EXPERTS, 0:rows]


def finish_call(got, bal, experts, width, ff_rows):
    rows = got.shape[1]
    shapes = [
        (rows, 3 * width),
        (rows, width),
        (EXPERTS, rows),
        (1, rows),
        (1, rows),
        (2, rows),
        (1, rows),
        (1, rows),
        (1, rows),
        (EXPERTS, ff_rows),
        (EXPERTS, rows),
        (1, 1),
    ]
    if experts:
        half = experts[0].shape[0] // 2
        shapes += [(EXPERTS, BLOCK, half // BLOCK * width), (EXPERTS, half, width)]
    vm = pl.BlockSpec(memory_space=pltpu.VMEM)
    return pl.pallas_call(
        functools.partial(finish_kernel, len(experts)),
        in_specs=[vm] * (2 + len(experts)),
        out_specs=[vm] * len(shapes),
        out_shape=[jax.ShapeDtypeStruct(shape, F32) for shape in shapes],
        scratch_shapes=[pltpu.VMEM((SMALL, SMALL), F32)],
        name="finish",
    )(got, bal, *experts)


def shards(
    total,
    images,
    image_count,
    expert_index,
    expert_slot,
    keep,
    cotangent,
    ln1_gain,
    ln1_bias,
    qkv_weight,
    qv_bias,
    out_weight,
    out_bias,
    ln2_gain,
    ln2_bias,
    router_weight,
    expert_in,
    expert_in_bias,
    expert_out,
    expert_out_bias,
):
    slots, seq_len, width = images.shape
    planes = total // EXPERTS
    rows = width // total
    ff = expert_in.shape[2]
    ff_rows = ff // total
    mb = slots // MICRO
    pad_len = -(-seq_len // 16) * 16
    plane_groups = [[z * EXPERTS + p for p in range(EXPERTS)] for z in range(planes)]
    core_groups = [
        [z * EXPERTS + c * CORES + k for c in range(CHIPS)]
        for z in range(planes)
        for k in range(CORES)
    ]
    far_groups = [[CORES * i + k for i in range(total // CORES)] for k in range(CORES)]
    chip_groups = [[CORES * i + k for k in range(CORES)] for i in range(total // CORES)]
    z_groups = [[z * EXPERTS + p for z in range(planes)] for p in range(EXPERTS)]

    def plane_swap(v):
        return lax.all_to_all(v, "dp", 0, 0, tiled=True, axis_index_groups=plane_groups)

    def z_swap(v):
        return lax.all_to_all(v, "dp", 0, 0, tiled=True, axis_index_groups=z_groups)

    def z_gather(v):
        return lax.all_gather(v, "dp", axis=0, tiled=True, axis_index_groups=z_groups)

    parts = ff // width
    if rows == BLOCK:
        expert_pack = pack_call(expert_in, expert_out)
    else:
        expert_pack = jnp.concatenate(
            [
                expert_in.reshape(EXPERTS, rows, parts, width)
                .transpose(0, 2, 1, 3)
                .reshape(EXPERTS, ff_rows, width),
                expert_out,
            ],
            1,
        )
    expert_pack = plane_swap(expert_pack)

    live_img = (jnp.arange(slots) < image_count[0]).astype(F32)
    live_tok = jnp.broadcast_to(live_img[:, None, None], (slots, seq_len, 1))
    if rows == BLOCK:
        vectors = [v[None] for v in (ln1_gain, ln1_bias, out_bias, ln2_gain, ln2_bias)]
        packed = prepare_call(
            image_count,
            expert_index.transpose(0, 2, 1),
            qkv_weight,
            out_weight,
            router_weight.T,
            vectors[0],
            vectors[1],
            qv_bias,
            *vectors[2:],
            expert_in_bias,
            expert_out_bias,
        )
    else:
        hits = (expert_index[..., None] == jnp.arange(EXPERTS)).astype(F32) * live_tok[..., None]
        local_counts = jnp.sum(hits, axis=(0, 1, 2))
        high = jnp.floor(local_counts * (1.0 / 128.0))
        told = jnp.concatenate([high, local_counts - 128.0 * high, image_count.astype(F32)])
        small_cols = jnp.concatenate(
            [
                router_weight,
                ln1_gain[:, None],
                ln1_bias[:, None],
                qv_bias.T,
                out_bias[:, None],
                ln2_gain[:, None],
                ln2_bias[:, None],
                jnp.zeros((rows, 1), BF),
                expert_in_bias.reshape(EXPERTS, parts, rows).transpose(2, 1, 0).reshape(rows, -1),
                expert_out_bias.T,
                jnp.broadcast_to(told.astype(BF)[None], (rows, 2 * EXPERTS + 1)),
            ],
            1,
        )
        small_cols = jnp.pad(small_cols, ((0, 0), (0, SMALL - small_cols.shape[1])))
        packed = jnp.concatenate([qkv_weight, out_weight, small_cols], 1)
    wide = packed.shape[1]
    if rows == BLOCK:
        pieces = [packed]
        for z in range(1, planes):
            pieces.append(
                lax.ppermute(packed, "dp", [(i, i ^ (z * EXPERTS)) for i in range(total)])
            )
        packed = jnp.concatenate(pieces, 0)
    else:
        packed = z_gather(packed)
    spans = []
    for size in CHUNKS:
        spans.append((sum(span[1] for span in spans), size))
    held = {
        m0: [v[m0 * mb : (m0 + mbc) * mb] for v in (images, cotangent)] for m0, mbc in spans
    }
    packed = jnp.broadcast_to(packed[None], (CHIPS,) + packed.shape)
    packed, expert_pack = lax.optimization_barrier((packed, expert_pack))
    first = lax.all_to_all(
        packed,
        "dp",
        0,
        0,
        tiled=True,
        axis_index_groups=core_groups,
    )
    second = lax.ppermute(first, "dp", [(i, i ^ 1) for i in range(total)])
    me = lax.axis_index("dp")
    if rows != BLOCK:
        even = me % CORES == 0
        both = jnp.stack([jnp.where(even, first, second), jnp.where(even, second, first)], 1)
        first = (
            both.reshape(CHIPS, CORES, planes, rows, wide)
            .transpose(2, 0, 1, 3, 4)
            .reshape(width, wide)
        )
        second = first[:, 4 * width :].astype(F32).T

    index_t, slot_t, keep_t = (v.transpose(0, 2, 1) for v in (expert_index, expert_slot, keep))
    target = jnp.where(keep_t == 1, index_t * CAP + slot_t, -1).astype(F32)
    live_row = jnp.broadcast_to(live_img[:, None, None], (slots, 1, seq_len))
    flags = jnp.concatenate(
        [index_t.astype(F32), keep_t.astype(F32), live_row, jnp.zeros_like(live_row)], 1
    )
    beyond = ((0, 0), (0, 0), (0, pad_len - seq_len))
    meta = jnp.concatenate(
        [jnp.pad(target, beyond, constant_values=-1.0), jnp.pad(flags, beyond)], 1
    )

    expert_pack = z_gather(expert_pack)
    if rows != BLOCK:
        blocks = width // BLOCK
        expert_pack = jnp.concatenate(
            [
                expert_pack[:, :ff_rows]
                .reshape(blocks, total // blocks, parts, rows, width)
                .transpose(0, 2, 1, 3, 4)
                .reshape(blocks, parts * BLOCK, width),
                expert_pack[:, ff_rows:].reshape(blocks, parts * BLOCK, width),
            ],
            1,
        )

    saved, sent, prob_sums = [], [], []
    for m0, mbc in spans:
        assemble = m0 == 0 and rows == BLOCK
        xd, qkv, probs, att, mid, rp, prob, *made = forward_call(
            m0, mbc, assemble, *held[m0], image_count, meta, first, second
        )
        if assemble:
            first, second = made
        saved.append((qkv, probs, att, mid, rp))
        prob_sums.append(prob[0, :EXPERTS])
        sent.append(plane_swap(xd))
    weights = first
    small, _ = lax.optimization_barrier((second, prob_sums[-1]))

    in_bias = small[AT_EIN : AT_EIN + parts * EXPERTS].reshape(parts, EXPERTS, width)
    in_bias = lax.dynamic_index_in_dim(in_bias, me % EXPERTS, 1, keepdims=False)
    in_bias = in_bias.reshape(parts, total, rows).transpose(1, 0, 2).reshape(1, ff)
    out_bias_e = lax.dynamic_slice_in_dim(small, AT_EOUT + me % EXPERTS, 1, 0)
    sums = jnp.sum(small[AT_HIGH : AT_IMAGES + 1], 1) * (1.0 / rows)
    counts_all = sums[:EXPERTS] * 128.0 + sums[EXPERTS : 2 * EXPERTS]
    live_total = sums[2 * EXPERTS] * float(seq_len)
    plane_counts = lax.dynamic_slice_in_dim(
        small[AT_IMAGES], (me // EXPERTS) * (EXPERTS * rows), EXPERTS * rows, 0
    )
    plane_counts = plane_counts.reshape(EXPERTS, rows)[:, 0].astype(jnp.int32)
    coef = jnp.pad(BALANCE_WEIGHT * EXPERTS * counts_all / live_total, (0, SMALL - EXPERTS))
    coef = jnp.broadcast_to(coef[None], (8, SMALL))
    in_bias = jnp.broadcast_to(in_bias, (8, ff))
    out_bias_e = jnp.broadcast_to(out_bias_e, (8, width))

    acc = None
    back = []
    for (m0, mbc), rows_in in zip(spans, sent):
        y, *acc = expert_call(
            m0,
            mbc,
            m0 + mbc == MICRO,
            plane_counts,
            rows_in,
            expert_pack,
            in_bias,
            out_bias_e,
            acc,
        )
        back.append(plane_swap(y))
    expert_grads, gb1, gb2 = acc

    if rows != BLOCK:
        expert_grads = jnp.concatenate(
            [
                expert_grads[:, : parts * BLOCK]
                .reshape(blocks, parts, total // blocks, rows, width)
                .transpose(0, 2, 1, 3, 4)
                .reshape(total, ff_rows, width),
                expert_grads[:, parts * BLOCK :].reshape(total, ff_rows, width),
            ],
            1,
        )
    expert_grads = lax.psum_scatter(
        expert_grads, "dp", scatter_dimension=0, tiled=True, axis_index_groups=z_groups
    )
    if rows == BLOCK:
        place = me % EXPERTS
        blocks_in = {}
        for r in reversed(range(EXPERTS)):
            block = lax.dynamic_index_in_dim(expert_grads, place ^ r, 0, keepdims=False)
            if r:
                block = lax.ppermute(block, "dp", [(i, i ^ r) for i in range(total)])
            blocks_in[r] = block
        blocks_in = [blocks_in[r] for r in reversed(range(EXPERTS))]
    else:
        blocks_in = []
        expert_grads = plane_swap(expert_grads).astype(F32)
        expert_in_grad = (
            expert_grads[:, :ff_rows]
            .reshape(EXPERTS, parts, rows, width)
            .transpose(0, 2, 1, 3)
            .reshape(EXPERTS, rows, ff)
        )
        expert_out_grad = expert_grads[:, ff_rows:]

    prob_sum = prob_sums[0]
    for piece in prob_sums[1:]:
        prob_sum = prob_sum + piece
    p_hi = prob_sum.astype(BF).astype(F32)
    mine = (jnp.arange(EXPERTS) == me % EXPERTS).astype(F32)
    e_in = gb1[0].reshape(total, parts, rows).transpose(1, 0, 2).reshape(parts, 1, width)
    extra = jnp.concatenate(
        [
            jnp.zeros((ROW_PROB, width), F32),
            jnp.broadcast_to(
                jnp.concatenate([p_hi, prob_sum - p_hi])[:, None], (2 * EXPERTS, width)
            ),
            mine[:, None] * gb2[0:1],
            (mine[None, :, None] * e_in).reshape(parts * EXPERTS, width),
            jnp.zeros((SMALL - ROW_EIN - parts * EXPERTS, width), F32),
        ],
        0,
    )

    bal = EXPERTS * counts_all / live_total / live_total
    bal = jnp.concatenate([jnp.zeros((ROW_PROB,), F32), bal, bal])
    bal = jnp.broadcast_to(jnp.pad(bal, (0, SMALL - bal.shape[0]))[None], (8, SMALL))
    extra, bal = lax.optimization_barrier((extra, bal))

    acc = None
    for (m0, mbc), returned, kept in zip(spans, back, saved):
        block_out, image_grad, *acc = backward_call(
            m0,
            mbc,
            m0 + mbc == MICRO,
            rows,
            *held[m0],
            image_count,
            meta,
            returned,
            kept,
            coef,
            weights,
            small,
            extra,
            None if acc is None else (*acc, block_out, image_grad),
        )

    grads = acc[0]
    if rows != BLOCK:
        grads = grads.reshape(total // CORES, CORES, rows, wide).transpose(1, 0, 2, 3)
    grads = lax.all_to_all(grads, "dp", 0, 0, tiled=True, axis_index_groups=chip_groups)
    grads = jnp.sum(grads.astype(F32), 0).astype(BF)
    grads = lax.all_to_all(
        grads.reshape(total // CORES, rows, wide),
        "dp",
        0,
        0,
        tiled=True,
        axis_index_groups=far_groups,
    )
    (
        qkv_grad,
        out_grad,
        router_grad,
        gain1_grad,
        bias1_grad,
        qv_grad,
        obias_grad,
        gain2_grad,
        bias2_grad,
        ein_grad,
        eout_grad,
        balance,
        *expert_pair,
    ) = finish_call(grads, bal, blocks_in, width, ff_rows)
    if blocks_in:
        expert_in_grad, expert_out_grad = expert_pair
    return (
        block_out,
        image_grad,
        balance.reshape(()),
        gain1_grad.reshape(rows),
        bias1_grad.reshape(rows),
        qkv_grad,
        qv_grad,
        out_grad,
        obias_grad.reshape(rows),
        gain2_grad.reshape(rows),
        bias2_grad.reshape(rows),
        router_grad.T,
        expert_in_grad,
        ein_grad,
        expert_out_grad,
        eout_grad,
    )


def solution(mesh):
    placed = (
        P("dp", None, None),
        P("dp"),
        P("dp", None, None),
        P("dp", None, None),
        P("dp", None, None),
        P("dp", None, None),
        P("dp"),
        P("dp"),
        P("dp", None),
        P(None, "dp"),
        P("dp", None),
        P("dp"),
        P("dp"),
        P("dp"),
        P("dp", None),
        P(None, "dp", None),
        P(None, "dp"),
        P(None, "dp", None),
        P(None, "dp"),
    )
    return jax.shard_map(
        functools.partial(shards, mesh.shape["dp"]),
        mesh=mesh,
        in_specs=placed,
        out_specs=(
            P("dp", None, None),
            P("dp", None, None),
            P(),
            P("dp"),
            P("dp"),
            P("dp", None),
            P(None, "dp"),
            P("dp", None),
            P("dp"),
            P("dp"),
            P("dp"),
            P("dp", None),
            P(None, "dp", None),
            P(None, "dp"),
            P(None, "dp", None),
            P(None, "dp"),
        ),
        check_vma=False,
    )
```
